128 devices in a mesh: rows: 32 (over x, y, core), cols: 4 (over z).
Axes of the slice: x: 4, y: 4, z: 4, core: 2. Of those that a mesh axis runs over, the one named last changes fastest.
Arguments:
- trace_values: float32 [32, 2097152], P('cols', 'rows'), may hold values from -6 to 6
- challenges: float32 [32], P('cols'), may hold values from 0.5 to 4
- multiplicity: int32 [32, 4194304], P('cols', 'rows'), may hold values from 0 to 3
- table_index: int32 [32, 4194304], P('cols', 'rows'), may hold values from 0 to 8187
Outputs:
- extended: float32 [32, 4194304], P('cols', 'rows')
- fraction: float32 [4194304], P(('rows', 'cols'))
- running: float32 [4194304], P(('rows', 'cols'))
The draws below stay inside these ranges and needn't reach their ends.
All inputs are finite; a program needn't handle non-finite values.
Results may differ from the reference program's by a relative error of at most 0.000068.
Values sent between devices are 32-bit elements; how exact they have to be, the bound alone decides.
A program may use at most 192 MiB of HBM per device.

```python
import math
import jax
import jax.numpy as jnp

COLS = 32
TABLE_ROWS = 8188
ROWS = 2097152
EXT_ROWS = 4194304


def draw_trace_values(key, part):
    key = jax.random.fold_in(key, 11)
    noise_key, freq_key, phase_key, amp_key = jax.random.split(key, 4)
    positions = jnp.arange(ROWS, dtype=jnp.int32)
    alternate = (1 - 2 * (positions % 2)).astype(jnp.float32)
    noise = jax.random.truncated_normal(noise_key, -3.0, 3.0, (COLS, ROWS), jnp.float32)
    amplitudes = jax.random.uniform(amp_key, (3, COLS, 1), jnp.float32, 0.4, 1.0)
    frequencies = jax.random.randint(freq_key, (3, COLS, 1), 1, 5)
    phases = jax.random.uniform(phase_key, (3, COLS, 1), jnp.float32, 0.0, 2.0 * math.pi)
    envelope = jnp.zeros((COLS, ROWS), jnp.float32)
    for term in range(3):
        cycles = (frequencies[term] * positions[None, :] % ROWS).astype(jnp.float32) * (2.0 * math.pi / ROWS)
        envelope = envelope + amplitudes[term] * jnp.cos(cycles + phases[term])
    return (noise + alternate[None, :] * envelope).astype(jnp.float32)


def with_ends(result, own_key, low, largest):
    index_at = [jax.random.randint(jax.random.fold_in(own_key, axis), (), 0, length) for axis, length in enumerate(result.shape)]
    longest = result.shape.index(max(result.shape))
    beside = index_at[:longest] + [(index_at[longest] + 1) % result.shape[longest]] + index_at[longest + 1:]
    return result.at[tuple(index_at)].set(low).at[tuple(beside)].set(largest)


def level_of(stream_key, dims, pieces, low, largest):
    def one(axis_at, shards_of):
        draws = jax.random.uniform(jax.random.fold_in(jax.random.fold_in(stream_key, 6), axis_at), (shards_of,), jnp.float32, low / len(pieces), largest / len(pieces))
        return jnp.repeat(jnp.exp(draws), dims[axis_at] // shards_of).reshape((-1,) + (1,) * (len(dims) - axis_at - 1))

    factor_of = one(*pieces[0])
    for cut in pieces[1:]:
        factor_of = factor_of * one(*cut)
    return factor_of


def setup_inputs(seed: int = 0) -> dict:
    arg_keys = jax.random.split(jax.random.key(seed), 5)
    return {
        "trace_values": draw_trace_values(jax.random.fold_in(arg_keys[4], 71), 0),
        "challenges": jnp.clip(jnp.exp(math.log(4.0) - 2.0794415 * jax.random.uniform(arg_keys[1], (COLS,), jnp.float32) ** level_of(arg_keys[1], (COLS,), ((0, 4),), -0.2, 0.2)), 0.5, 4.0),
        "multiplicity": with_ends(jax.random.randint(arg_keys[2], (COLS, EXT_ROWS), 0, 4), jax.random.fold_in(arg_keys[2], 1), 0, 3).astype(jnp.int32),
        "table_index": with_ends(jax.random.randint(arg_keys[3], (COLS, EXT_ROWS), 0, TABLE_ROWS), jax.random.fold_in(arg_keys[3], 1), 0, TABLE_ROWS - 1).astype(jnp.int32),
    }


def reference(trace_values, challenges, multiplicity, table_index):
    spectrum = jnp.fft.fft(trace_values, axis=1)
    frequency = jnp.arange(ROWS)
    signed = jnp.where(frequency < ROWS // 2, frequency, frequency - ROWS).astype(jnp.float32)
    angle_values = signed * (math.pi / ROWS)
    keep_mask = (frequency != ROWS // 2).astype(jnp.float32)
    shifted = spectrum * ((jnp.cos(angle_values) + 1j * jnp.sin(angle_values)) * keep_mask)
    coset = jnp.real(jnp.fft.ifft(shifted, axis=1)).astype(jnp.float32)
    extended = jnp.stack([trace_values, coset], axis=2).reshape(COLS, EXT_ROWS)
    table_value = (table_index.astype(jnp.float32) - TABLE_ROWS / 2) * (8.0 / TABLE_ROWS)
    weights = challenges[:, None]
    terms = 1.0 / (weights + extended * extended) - multiplicity.astype(jnp.float32) / (weights + table_value * table_value)
    fraction = jnp.sum(terms, axis=0)
    running = jnp.cumsum(fraction) / EXT_ROWS
    return extended, fraction, running
```

```python
import functools
import math

import jax
import jax.numpy as jnp
import ml_dtypes
import numpy as np
from jax import lax
from jax.experimental import pallas as pl
from jax.experimental.pallas import tpu as pltpu
from jax.sharding import PartitionSpec as P

TABLE_ROWS = 8188
NODES = 16
LEAF = 128
RADIX = 16
LANES = 128
MESH = pl.DeviceIdType.MESH
HIGHEST = lax.Precision.HIGHEST
F32 = jnp.float32
BF16 = jnp.bfloat16


def chebyshev():
    return np.cos((2 * np.arange(NODES) + 1) * np.pi / (2 * NODES))


def lagrange(places):
    order = np.arange(1, NODES)
    waves = np.cos(order * np.arccos(np.clip(places, -1, 1))[..., None])
    at_nodes = np.cos(order * np.arccos(chebyshev())[:, None])
    return (1 + 2 * waves @ at_nodes.T) / NODES


def sign(index):
    return 1.0 - 2.0 * (index % 2)


def cotangent(offset, total):
    return 1.0 / np.tan(np.pi * offset / total) / total


def point_to_moment():
    rows = np.arange(LEAF)
    return sign(rows)[:, None] * lagrange((rows - LEAF / 2) / (LEAF / 2))


def local_to_point():
    rows = np.arange(LEAF)
    return (sign(rows)[:, None] * lagrange((rows + 0.5 - LEAF / 2) / (LEAF / 2))).T


def child_to_parent():
    child = np.arange(RADIX)[:, None]
    return lagrange((2 * child + 1 + chebyshev()[None]) / RADIX - 1).reshape(RADIX * NODES, NODES)


def far_weights(sources, targets, width, total, blocks):
    nodes = chebyshev()
    apart = (targets[None, :] - sources[:, None])[:, None, :, None]
    offset = width * apart + width / 2 * (nodes[None, None, None, :] - nodes[None, :, None, None])
    far = np.abs(apart) >= 2
    if blocks:
        far = far & (np.abs(apart) <= blocks - 2)
    far = np.broadcast_to(far, offset.shape)
    weights = np.where(far, cotangent(np.where(far, offset, 1.0), total), 0.0)
    return weights.reshape(sources.size * NODES, targets.size * NODES)


def near_weights(total):
    source = np.arange(3 * LEAF)[:, None] - LEAF
    target = np.arange(LEAF)[None, :]
    return sign(target - source) * cotangent(target - source + 0.5, total)


def split(matrix):
    high = matrix.astype(np.float32).astype(ml_dtypes.bfloat16)
    low = (matrix - high.astype(np.float64)).astype(np.float32).astype(ml_dtypes.bfloat16)
    return high, low


def matrices(total, groups):
    middle = LEAF * RADIX
    top = middle * RADIX
    blocks = total // top
    per_device = blocks // groups
    p2m = point_to_moment()
    packed = np.zeros((RADIX, LEAF, RADIX, NODES))
    for leaf in range(RADIX):
        packed[leaf, :, leaf, :] = p2m
    c2p = child_to_parent()
    three = np.arange(3 * RADIX) - RADIX
    one = np.arange(RADIX)
    top_far = np.zeros((blocks * NODES, LANES))
    top_far[:, : per_device * NODES] = far_weights(
        np.arange(blocks), np.arange(per_device), top, total, blocks
    )
    top_down = np.zeros((LANES, per_device * RADIX * NODES))
    for block in range(per_device):
        at = slice(block * NODES, (block + 1) * NODES)
        top_down[at, block * RADIX * NODES : (block + 1) * RADIX * NODES] = c2p.T
    out = np.zeros((4 * LEAF, 2 * LEAF))
    out[: 3 * LEAF, 1::2] = near_weights(total)
    out[LEAF + np.arange(LEAF), 2 * np.arange(LEAF)] = 1.0
    out[3 * LEAF :, 1::2] = np.tile(local_to_point(), (LEAF // NODES, 1))
    keep = np.zeros((LEAF, 2 * LEAF))
    keep[np.arange(LEAF), 2 * np.arange(LEAF)] = 1.0
    f32 = lambda m: m.astype(np.float32)
    return dict(
        p2m=f32(packed.reshape(RADIX * LEAF, RADIX * NODES)),
        up=f32(np.tile(c2p, (1, RADIX))),
        far0=f32(far_weights(three, one, LEAF, total, 0)),
        far1=f32(far_weights(three, one, middle, total, 0)),
        top=f32(top_far),
        top_down=f32(top_down),
        down=f32(np.tile(c2p.T, (LANES // NODES, 1))),
        out=split(out),
        keep=split(keep)[0],
    )


def dot(left, right):
    return jnp.dot(left, right, preferred_element_type=F32, precision=HIGHEST)


def dot16(left, right):
    return jnp.dot(left, right, preferred_element_type=F32)


def lane_group(rows):
    return lax.broadcasted_iota(jnp.int32, (rows, LANES), 1) // NODES


def spread(local):
    group = lane_group(8)
    half = LANES // NODES
    tiles = []
    for child in range(RADIX):
        tile = local[:, (child // half) * LANES : (child // half + 1) * LANES]
        tiles.append(jnp.where(group == child % half, tile, 0.0))
    return jnp.concatenate(tiles, axis=0)


def gather_children(copies):
    group = lax.broadcasted_iota(jnp.int32, (8, RADIX * NODES), 1) // NODES
    total = jnp.zeros((8, RADIX * NODES), F32)
    for child in range(RADIX):
        total = jnp.where(group == child, copies[8 * child : 8 * child + 8], total)
    return total


def column_sums(tiles):
    row = lax.broadcasted_iota(jnp.int32, (8, LANES), 0)
    for shift in (1, 2, 4):
        first = (row // shift) % 2 == 0
        tiles = [
            jnp.where(first, a, b) + pltpu.roll(jnp.where(first, b, a), shift, 0)
            for a, b in zip(tiles[0::2], tiles[1::2])
        ]
    return tiles[0]


def invert(value):
    guess = pl.reciprocal(value, approx=True)
    return guess * (2.0 - value * guess)


def challenge_tile(challenge_ref):
    row = lax.broadcasted_iota(jnp.int32, (8, LANES), 0)
    tile = jnp.zeros((8, LANES), F32)
    for column in range(8):
        tile = jnp.where(row == column, challenge_ref[column], tile)
    return tile


def greet(axes):
    barrier = pltpu.get_barrier_semaphore()
    for axis, size in axes:
        me = lax.axis_index(axis)

        @pl.loop(1, size)
        def _(step):
            peer = lax.rem(me + step, size)
            pl.semaphore_signal(barrier, inc=1, device_id={axis: peer}, device_id_type=MESH)

    return barrier


def far_kernel(
    groups, challenge_ref, x_hbm, multiplicity_hbm, index_hbm, p2m_ref, up_ref, far0_ref, far1_ref, top_ref,
    top_down_ref, down_ref, local_ref, halo_ref, table_ref,
    x_ref, multiplicity_ref, index_ref, moments_ref, send_ref, gathered_ref, edge_send, edge_recv,
    load_sem, send_sem, recv_sem, edge_send_sem, edge_recv_sem,
):
    me = lax.axis_index("rows")
    rows = x_ref.shape[1]
    parents = rows // (LEAF * RADIX)
    tops = parents // RADIX
    loads = [
        pltpu.make_async_copy(source, target, load_sem.at[k])
        for k, (source, target) in enumerate(
            ((x_hbm, x_ref), (multiplicity_hbm, multiplicity_ref), (index_hbm, index_ref))
        )
    ]
    for load in loads:
        load.start()
    barrier = greet((("rows", groups),))
    loads[0].wait()

    span = LEAF * RADIX
    total = jnp.zeros((8 * parents, RADIX * NODES), F32)
    for part in range(span // 256):
        left = jnp.concatenate(
            [x_ref[:, span * p + 256 * part : span * p + 256 * part + 256] for p in range(parents)], axis=0
        )
        total = total + dot(left, p2m_ref[256 * part : 256 * part + 256, :])
    moments_ref[...] = total
    copies = dot(total, up_ref[...])
    middle = [gather_children(copies[128 * g : 128 * g + 128]) for g in range(tops)]
    high = dot(jnp.concatenate(middle, axis=0), up_ref[:, :LANES])
    group = lane_group(8)
    packed = high[0:8]
    for g in range(1, tops):
        packed = jnp.where(group % tops == g, high[8 * g : 8 * g + 8], packed)
    send_ref[...] = packed
    wide = RADIX * NODES
    edge_send[0, :, 0:LEAF] = x_ref[:, rows - LEAF : rows]
    edge_send[0, :, LEAF : LEAF + wide] = total[8 * (parents - 1) : 8 * parents]
    edge_send[0, :, LEAF + wide :] = middle[tops - 1]
    edge_send[1, :, 0:LEAF] = x_ref[:, 0:LEAF]
    edge_send[1, :, LEAF : LEAF + wide] = total[0:8]
    edge_send[1, :, LEAF + wide :] = middle[0]

    pl.semaphore_wait(barrier, groups - 1)

    def edge(k):
        peer = lax.rem(me + (1 if k == 0 else groups - 1), groups)
        return pltpu.make_async_remote_copy(
            src_ref=edge_send.at[k], dst_ref=edge_recv.at[k], send_sem=edge_send_sem.at[k],
            recv_sem=edge_recv_sem.at[k], device_id={"rows": peer}, device_id_type=MESH,
        )

    def message(step):
        peer = lax.rem(me + groups - step, groups)
        return pltpu.make_async_remote_copy(
            src_ref=send_ref, dst_ref=gathered_ref.at[step], send_sem=send_sem.at[step],
            recv_sem=recv_sem.at[step], device_id={"rows": peer}, device_id_type=MESH,
        )

    @pl.loop(1, groups)
    def _(step):
        message(step).start()

    edge(0).start()
    edge(1).start()

    loads[1].wait()
    loads[2].wait()
    weight = challenge_tile(challenge_ref)

    @pl.loop(0, index_ref.shape[1] // 1024)
    def _(k):
        tiles = []
        for tile in range(8):
            at = pl.ds(pl.multiple_of(k * 1024 + tile * LANES, LANES), LANES)
            value = (index_ref[:, at].astype(F32) - TABLE_ROWS / 2) * (8.0 / TABLE_ROWS)
            tiles.append(multiplicity_ref[:, at].astype(F32) * invert(weight + value * value))
        table_ref[pl.ds(pl.multiple_of(8 * k, 8), 8), :] = column_sums(tiles)

    gathered_ref[0] = send_ref[...]

    @pl.loop(1, groups)
    def _(step):
        message(step).wait()

    edge(0).wait()
    edge(1).wait()
    per_tile = LANES // (tops * NODES)
    pieces = []
    for k in range(groups // per_tile):
        tile = gathered_ref[per_tile * k]
        for place in range(1, per_tile):
            tile = jnp.where(group // tops == place, gathered_ref[per_tile * k + place], tile)
        pieces.append(tile)
    top_local = dot(jnp.concatenate(pieces, axis=1), top_ref[...])
    from_top = dot(top_local, top_down_ref[...])
    line = [edge_recv[0, :, LEAF + wide :]] + middle + [edge_recv[1, :, LEAF + wide :]]
    left = jnp.concatenate([jnp.concatenate(line[g : g + 3], axis=1) for g in range(tops)], axis=0)
    middle_local = dot(left, far1_ref[...])
    middle_local = [
        middle_local[8 * g : 8 * g + 8] + from_top[:, wide * g : wide * g + wide] for g in range(tops)
    ]
    moments = moments_ref[...]
    before = jnp.concatenate([edge_recv[0, :, LEAF : LEAF + wide], moments[:-8]], axis=0)
    after = jnp.concatenate([moments[8:], edge_recv[1, :, LEAF : LEAF + wide]], axis=0)
    local = dot(before, far0_ref[0:wide]) + dot(moments, far0_ref[wide : 2 * wide])
    local = local + dot(after, far0_ref[2 * wide :])
    local_ref[...] = local + dot(
        jnp.concatenate([spread(m) for m in middle_local], axis=0), down_ref[...]
    )
    halo_ref[0] = edge_recv[0, :, 0:LEAF]
    halo_ref[1] = edge_recv[1, :, 0:LEAF]


def two(value):
    high = value.astype(BF16)
    return high, (value - high.astype(F32)).astype(BF16)


def rows_kernel(
    challenge_ref, x_ref, halo_ref, local_ref, table_ref, high_ref, low_ref, keep_ref, extended_ref, partial_ref
):
    step = pl.program_id(0)
    steps = pl.num_programs(0)
    rows = x_ref.shape[1] // steps
    leaves = rows // LEAF
    start = pl.multiple_of(step * rows, rows)
    before = pl.multiple_of(jnp.maximum(start - LEAF, 0), LEAF)
    after = pl.multiple_of(jnp.minimum(start + rows, x_ref.shape[1] - LEAF), LEAF)
    tiles = [jnp.where(step == 0, halo_ref[0], x_ref[:, pl.ds(before, LEAF)])]
    for leaf in range(leaves):
        tiles.append(x_ref[:, pl.ds(pl.multiple_of(start + leaf * LEAF, LEAF), LEAF)])
    tiles.append(jnp.where(step == steps - 1, halo_ref[1], x_ref[:, pl.ds(after, LEAF)]))
    values = jnp.concatenate(tiles, axis=0)
    local = local_ref[...]
    sources = [values[8 * k : 8 * k + 8 * leaves] for k in range(3)]
    sources.append(
        jnp.concatenate([spread(local[8 * p : 8 * p + 8]) for p in range(leaves // RADIX)], axis=0)
    )
    pairs = [two(source) for source in sources]
    high = jnp.concatenate([pair[0] for pair in pairs], axis=1)
    low = jnp.concatenate([pair[1] for pair in pairs], axis=1)
    own = sources[1]
    rest = (own - pairs[1][0].astype(F32) - pairs[1][1].astype(F32)).astype(BF16)
    result = dot16(rest, keep_ref[...]) + dot16(low, high_ref[...])
    result = result + dot16(high, low_ref[...]) + dot16(high, high_ref[...])
    weight = challenge_tile(challenge_ref)
    terms = []
    for leaf in range(leaves):
        both = result[8 * leaf : 8 * leaf + 8]
        extended_ref[:, 2 * LEAF * leaf : 2 * LEAF * leaf + 2 * LEAF] = both
        for half in range(2):
            value = both[:, LANES * half : LANES * half + LANES]
            terms.append(invert(weight + value * value))
    for k in range(len(terms) // 8):
        partial_ref[8 * k : 8 * k + 8, :] = column_sums(terms[8 * k : 8 * k + 8]) - table_ref[8 * k : 8 * k + 8, :]


def sums_kernel(
    groups, parts, scale, partial_ref, lane_ref, row_ref, fraction_ref, running_ref,
    pieces_ref, note_ref, notes_ref, entry_ref, entries_ref,
    piece_send, piece_recv, note_send, note_recv, entry_send, entry_recv,
):
    me = lax.axis_index("rows")
    part = lax.axis_index("cols")
    size = partial_ref.shape[0] // parts
    barrier = greet((("rows", groups), ("cols", parts)))
    totals = []
    for p in range(parts):
        totals.append(jnp.sum(partial_ref[size * p : size * p + size, :]))
    note_ref[...] = jnp.full(note_ref.shape, sum(totals[1:], totals[0]), F32)
    pl.semaphore_wait(barrier, groups + parts - 2)

    def piece(step):
        peer = lax.rem(part + parts - step, parts)
        return pltpu.make_async_remote_copy(
            src_ref=partial_ref.at[pl.ds(pl.multiple_of(peer * size, size), size)], dst_ref=pieces_ref.at[step],
            send_sem=piece_send.at[step], recv_sem=piece_recv.at[step], device_id={"cols": peer},
            device_id_type=MESH,
        )

    def note(step):
        peer = lax.rem(me + groups - step, groups)
        return pltpu.make_async_remote_copy(
            src_ref=note_ref, dst_ref=notes_ref.at[step], send_sem=note_send.at[step],
            recv_sem=note_recv.at[step], device_id={"rows": peer}, device_id_type=MESH,
        )

    def entry(step):
        peer = lax.rem(part + parts - step, parts)
        return pltpu.make_async_remote_copy(
            src_ref=entry_ref.at[peer], dst_ref=entries_ref.at[step], send_sem=entry_send.at[step],
            recv_sem=entry_recv.at[step], device_id={"cols": peer}, device_id_type=MESH,
        )

    @pl.loop(1, groups)
    def _(step):
        note(step).start()

    @pl.loop(1, parts)
    def _(step):
        piece(step).start()

    @pl.loop(1, groups)
    def _(step):
        note(step).wait()

    entering = jnp.zeros(note_ref.shape, F32)
    for step in range(1, groups):
        entering = entering + jnp.where(me + step >= groups, notes_ref[step], 0.0)
    for p in range(parts):
        entry_ref[p] = entering
        entering = entering + totals[p]

    @pl.loop(1, parts)
    def _(step):
        entry(step).start()

    @pl.loop(1, parts)
    def _(step):
        piece(step).wait()

    own = partial_ref[pl.ds(pl.multiple_of(part * size, size), size), :]
    for step in range(1, parts):
        own = own + pieces_ref[step]
    fraction_ref[...] = own
    within = dot(own, lane_ref[...])
    rows_before = dot(row_ref[...], jnp.broadcast_to(within[:, LANES - 1 :], within.shape))

    @pl.loop(1, parts)
    def _(step):
        entry(step).wait()

    carry = entry_ref[part]
    for step in range(1, parts):
        carry = carry + entries_ref[step]
    running_ref[...] = (within + rows_before + carry[0:1]) * scale


def local(groups, parts, trace_values, challenges, multiplicity, table_index):
    columns, rows = trace_values.shape
    total = groups * rows
    m = matrices(total, groups)
    wide = RADIX * NODES
    parents = rows // (LEAF * RADIX)
    vmem = pl.BlockSpec(memory_space=pltpu.VMEM)
    smem = pl.BlockSpec(memory_space=pltpu.SMEM)
    hbm = pl.BlockSpec(memory_space=pl.ANY)
    dma = pltpu.SemaphoreType.DMA
    sum_rows = 2 * rows // LANES
    far, halo, table = pl.pallas_call(
        functools.partial(far_kernel, groups),
        out_shape=(
            jax.ShapeDtypeStruct((columns * parents, wide), F32),
            jax.ShapeDtypeStruct((2, columns, LEAF), F32),
            jax.ShapeDtypeStruct((sum_rows, LANES), F32),
        ),
        in_specs=[smem, hbm, hbm, hbm] + [vmem] * 7,
        out_specs=(vmem, vmem, vmem),
        scratch_shapes=[
            pltpu.VMEM((columns, rows), F32),
            pltpu.VMEM((columns, 2 * rows), jnp.int32),
            pltpu.VMEM((columns, 2 * rows), jnp.int32),
            pltpu.VMEM((columns * parents, wide), F32),
            pltpu.VMEM((columns, LANES), F32),
            pltpu.VMEM((groups, columns, LANES), F32),
            pltpu.VMEM((2, columns, LEAF + 2 * wide), F32),
            pltpu.VMEM((2, columns, LEAF + 2 * wide), F32),
            dma((3,)), dma((groups,)), dma((groups,)), dma((2,)), dma((2,)),
        ],
        compiler_params=pltpu.CompilerParams(
            collective_id=0, has_side_effects=True, vmem_limit_bytes=48 * 2**20
        ),
        name="far",
    )(
        challenges, trace_values, multiplicity, table_index, m["p2m"], m["up"], m["far0"], m["far1"], m["top"],
        m["top_down"], m["down"],
    )
    steps = parents // 2
    whole = lambda shape: pl.BlockSpec(shape, lambda i: (0,) * len(shape))
    extended, partial = pl.pallas_call(
        rows_kernel,
        grid=(steps,),
        out_shape=(
            jax.ShapeDtypeStruct((columns, 2 * rows), F32),
            jax.ShapeDtypeStruct((sum_rows, LANES), F32),
        ),
        in_specs=[
            smem,
            whole((columns, rows)),
            whole((2, columns, LEAF)),
            pl.BlockSpec((columns * parents // steps, wide), lambda i: (i, 0)),
            pl.BlockSpec((sum_rows // steps, LANES), lambda i: (i, 0)),
            whole((4 * LEAF, 2 * LEAF)),
            whole((4 * LEAF, 2 * LEAF)),
            whole((LEAF, 2 * LEAF)),
        ],
        out_specs=(
            pl.BlockSpec((columns, 2 * rows // steps), lambda i: (0, i)),
            pl.BlockSpec((sum_rows // steps, LANES), lambda i: (i, 0)),
        ),
        compiler_params=pltpu.CompilerParams(vmem_limit_bytes=48 * 2**20),
        name="rows",
    )(challenges, trace_values, halo, far, table, m["out"][0], m["out"][1], m["keep"])
    size = sum_rows // parts
    own = jax.ShapeDtypeStruct((size, LANES), F32)
    lane_sum = np.triu(np.ones((LANES, LANES), np.float32))
    row_sum = np.tril(np.ones((size, size), np.float32), -1)
    fraction, running = pl.pallas_call(
        functools.partial(sums_kernel, groups, parts, 1.0 / (2 * total)),
        out_shape=(own, own),
        in_specs=[vmem, vmem, vmem],
        out_specs=(vmem, vmem),
        scratch_shapes=[
            pltpu.VMEM((parts, size, LANES), F32),
            pltpu.VMEM((8, LANES), F32),
            pltpu.VMEM((groups, 8, LANES), F32),
            pltpu.VMEM((parts, 8, LANES), F32),
            pltpu.VMEM((parts, 8, LANES), F32),
            dma((parts,)), dma((parts,)), dma((groups,)), dma((groups,)), dma((parts,)), dma((parts,)),
        ],
        compiler_params=pltpu.CompilerParams(
            collective_id=1, has_side_effects=True, vmem_limit_bytes=32 * 2**20
        ),
        name="sums",
    )(partial, lane_sum, row_sum)
    return extended, fraction.reshape(-1), running.reshape(-1)


def solution(mesh):
    return jax.shard_map(
        functools.partial(local, mesh.shape["rows"], mesh.shape["cols"]),
        mesh=mesh,
        in_specs=(P("cols", "rows"), P("cols"), P("cols", "rows"), P("cols", "rows")),
        out_specs=(P("cols", "rows"), P(("rows", "cols")), P(("rows", "cols"))),
        check_vma=False,
    )
```

```python
import functools
import math

import jax
import jax.numpy as jnp
import ml_dtypes
import numpy as np
from jax import lax
from jax.experimental import pallas as pl
from jax.experimental.pallas import tpu as pltpu
from jax.sharding import PartitionSpec as P

TABLE_ROWS = 8188
NODES = 16
LEAF = 128
RADIX = 16
LANES = 128
WIDE = RADIX * NODES
BATCH = 4
MESH = pl.DeviceIdType.MESH
F32 = jnp.float32
BF16 = jnp.bfloat16


def chebyshev():
    return np.cos((2 * np.arange(NODES) + 1) * np.pi / (2 * NODES))


def lagrange(places):
    order = np.arange(1, NODES)
    waves = np.cos(order * np.arccos(np.clip(places, -1, 1))[..., None])
    at_nodes = np.cos(order * np.arccos(chebyshev())[:, None])
    return (1 + 2 * waves @ at_nodes.T) / NODES


def sign(index):
    return 1.0 - 2.0 * (index % 2)


def cotangent(offset, total):
    return 1.0 / np.tan(np.pi * offset / total) / total


def point_to_moment():
    rows = np.arange(LEAF)
    return sign(rows)[:, None] * lagrange((rows - LEAF / 2) / (LEAF / 2))


def local_to_point():
    rows = np.arange(LEAF)
    return (sign(rows)[:, None] * lagrange((rows + 0.5 - LEAF / 2) / (LEAF / 2))).T


def child_to_parent():
    child = np.arange(RADIX)[:, None]
    return lagrange((2 * child + 1 + chebyshev()[None]) / RADIX - 1).reshape(RADIX * NODES, NODES)


def far_weights(sources, targets, width, total, blocks):
    nodes = chebyshev()
    apart = (targets[None, :] - sources[:, None])[:, None, :, None]
    offset = width * apart + width / 2 * (nodes[None, None, None, :] - nodes[None, :, None, None])
    far = np.abs(apart) >= 2
    if blocks:
        far = far & (np.abs(apart) <= blocks - 2)
    far = np.broadcast_to(far, offset.shape)
    weights = np.where(far, cotangent(np.where(far, offset, 1.0), total), 0.0)
    return weights.reshape(sources.size * NODES, targets.size * NODES)


def split(matrix):
    high = matrix.astype(np.float32).astype(ml_dtypes.bfloat16)
    low = (matrix - high.astype(np.float64)).astype(np.float32).astype(ml_dtypes.bfloat16)
    return high, low


def matrices(total, groups):
    middle = LEAF * RADIX
    top = middle * RADIX
    blocks = total // top
    per_device = blocks // groups
    c2p = child_to_parent()
    three = np.arange(3 * RADIX) - RADIX
    one = np.arange(RADIX)
    top_far = np.zeros((blocks * NODES, WIDE))
    top_far[:, : per_device * NODES] = far_weights(
        np.arange(blocks), np.arange(per_device), top, total, blocks
    )
    top_down = np.zeros((per_device, LANES, WIDE))
    for block in range(per_device):
        top_down[block, block * NODES : (block + 1) * NODES] = c2p.T
    source = np.arange(4 * LEAF)[:, None] - LEAF
    target = np.arange(2 * LEAF)[None, :]
    near = sign(target - source) * cotangent(target - source + 0.5, total)
    near = np.where(np.abs(target // LEAF - source // LEAF) <= 1, near, 0.0)
    child_out = np.zeros((LANES // NODES, NODES, 2, LEAF))
    for child in range(LANES // NODES):
        child_out[child, :, child % 2] = local_to_point()
    weave = np.zeros((2, LEAF, 2 * LEAF))
    for side in range(2):
        weave[side, np.arange(LEAF), 2 * np.arange(LEAF) + side] = 1.0
    parts = dict(
        p2m=np.tile(point_to_moment(), (1, RADIX)),
        up=np.tile(c2p, (1, RADIX)),
        far0=far_weights(three, one, LEAF, total, 0),
        far1=far_weights(three, one, middle, total, 0),
        top=top_far,
        top_down=top_down.reshape(-1, WIDE),
        down=np.tile(c2p.T, (LANES // NODES, 1)),
        out=np.concatenate([near, child_out.reshape(LANES, WIDE)]),
        weave=weave.reshape(2 * LEAF, WIDE),
    )
    places, start = {}, 0
    for name, part in parts.items():
        places[name] = (start, start + part.shape[0])
        start += part.shape[0]
    return split(np.concatenate(list(parts.values()))), places


def dot16(left, right):
    return jnp.dot(left, right, preferred_element_type=F32)


def two(value):
    high = value.astype(BF16)
    return high, (value - high.astype(F32)).astype(BF16)


def dot_pieces(left, right):
    return dot16(left[1], right[0]) + dot16(left[0], right[1]) + dot16(left[0], right[0])


def dot_exact(left, right):
    high, low = two(left)
    rest = (left - high.astype(F32) - low.astype(F32)).astype(BF16)
    return dot16(rest, right) + dot16(low, right) + dot16(high, right)


def spread(local, span):
    group = lax.broadcasted_iota(jnp.int32, (8, LANES), 1) // span
    half = LANES // span
    tiles = []
    for child in range(WIDE // span):
        tile = local[:, (child // half) * LANES : (child // half + 1) * LANES]
        tiles.append(jnp.where(group == child % half, tile, 0.0))
    return tiles


def gather_children(copies):
    group = lax.broadcasted_iota(jnp.int32, (8, WIDE), 1) // NODES
    total = jnp.zeros((8, WIDE), F32)
    for child in range(RADIX):
        total = jnp.where(group == child, copies[8 * child : 8 * child + 8], total)
    return total


def column_sums(tiles):
    row = lax.broadcasted_iota(jnp.int32, (8, LANES), 0)
    for shift in (1, 2, 4):
        first = (row // shift) % 2 == 0
        tiles = [
            jnp.where(first, a, b) + pltpu.roll(jnp.where(first, b, a), shift, 0)
            for a, b in zip(tiles[0::2], tiles[1::2])
        ]
    return tiles[0]


def invert(value):
    guess = pl.reciprocal(value, approx=True)
    return guess * (2.0 - value * guess)


def challenge_tile(challenge_ref):
    row = lax.broadcasted_iota(jnp.int32, (8, LANES), 0)
    tile = jnp.zeros((8, LANES), F32)
    for column in range(8):
        tile = jnp.where(row == column, challenge_ref[column], tile)
    return tile


def fold(rows):
    total = jnp.zeros((8, LANES), F32)
    for r in range(rows.shape[0] // 8):
        for l in range(rows.shape[1] // LANES):
            total = total + rows[8 * r : 8 * r + 8, LANES * l : LANES * l + LANES]
    return total


def aligned(start, size):
    return pl.ds(pl.multiple_of(start, size), size)


def greet(axes):
    barrier = pltpu.get_barrier_semaphore()
    for axis, size in axes:
        me = lax.axis_index(axis)

        @pl.loop(1, size)
        def _(step):
            peer = lax.rem(me + step, size)
            pl.semaphore_signal(barrier, inc=1, device_id={axis: peer}, device_id_type=MESH)

    return barrier


def main_kernel(
    groups, parts, places, batch, challenge_ref, x_hbm, multiplicity_hbm, index_hbm, high_hbm, low_hbm,
    coset_hbm, own_ref, carry_ref,
    x_ref, multiplicity_ref, index_ref, high_ref, low_ref, coset_ref, moments_ref, local_ref, sums_ref, table_ref,
    partial_ref, send_ref, gathered_ref, edge_send, edge_recv, pieces_ref, note_ref, notes_ref, entry_ref, entries_ref,
    x_sem, load_sem, table_sem, store_sem, send_sem, recv_sem, edge_send_sem, edge_recv_sem,
    piece_send, piece_recv, note_send, note_recv, entry_send, entry_recv,
):
    me = lax.axis_index("rows")
    part = lax.axis_index("cols")
    rows = x_hbm.shape[1]
    leaves = rows // LEAF
    parents = leaves // RADIX
    tops = parents // RADIX
    span = LEAF * RADIX
    quarter_rows = rows // parts
    inner = pl.ds(LEAF, rows)

    def weights(name, first=0, last=None):
        start, stop = places[name]
        at = slice(start + first, stop if last is None else start + last)
        return high_ref[at, :], low_ref[at, :]

    early = places["up"][1]
    late = high_ref.shape[0] - early
    load_x = pltpu.make_async_copy(x_hbm, x_ref.at[:, inner], x_sem)
    loads = []
    for k, at in enumerate((pl.ds(0, early), pl.ds(early, late))):
        loads.append(
            [
                pltpu.make_async_copy(high_hbm.at[at], high_ref.at[at], load_sem.at[2 * k]),
                pltpu.make_async_copy(low_hbm.at[at], low_ref.at[at], load_sem.at[2 * k + 1]),
            ]
        )

    def table_loads(k):
        at = aligned(k * 2 * quarter_rows, 2 * quarter_rows)
        return (
            pltpu.make_async_copy(multiplicity_hbm.at[:, at], multiplicity_ref.at[:, at], table_sem.at[0, k]),
            pltpu.make_async_copy(index_hbm.at[:, at], index_ref.at[:, at], table_sem.at[1, k]),
        )

    for load in loads[0]:
        load.start()
    load_x.start()
    for k in range(parts):
        for load in table_loads(k):
            load.start()
    for load in loads[1]:
        load.start()
    barrier = greet((("rows", groups), ("cols", parts)))
    for load in loads[0]:
        load.wait()
    load_x.wait()

    own_group = lax.broadcasted_iota(jnp.int32, (LEAF, WIDE), 1) // NODES
    p2m = weights("p2m")
    total = jnp.zeros((8 * parents, WIDE), F32)
    for pair in range(RADIX // 2):
        start = LEAF + 2 * LEAF * pair
        left = jnp.concatenate(
            [x_ref[:, span * p + start : span * p + start + 2 * LEAF] for p in range(parents)], axis=0
        )
        right = [
            jnp.concatenate(
                [jnp.where(own_group == 2 * pair + k, piece, jnp.zeros_like(piece)) for k in range(2)], axis=0
            )
            for piece in p2m
        ]
        total = total + dot_pieces(two(left), right)
    moments_ref[...] = total
    up = weights("up")
    copies = dot_pieces(two(total), up)
    middle = [gather_children(copies[128 * g : 128 * g + 128]) for g in range(tops)]
    high = dot_pieces(two(jnp.concatenate(middle, axis=0)), [piece[:, :LANES] for piece in up])
    group = lax.broadcasted_iota(jnp.int32, (8, LANES), 1) // NODES
    packed = high[0:8]
    for g in range(1, tops):
        packed = jnp.where(group % tops == g, high[8 * g : 8 * g + 8], packed)
    send_ref[...] = packed
    edge_send[0, :, 0:LEAF] = x_ref[:, rows : rows + LEAF]
    edge_send[0, :, LEAF : LEAF + WIDE] = total[8 * (parents - 1) : 8 * parents]
    edge_send[0, :, LEAF + WIDE :] = middle[tops - 1]
    edge_send[1, :, 0:LEAF] = x_ref[:, LEAF : 2 * LEAF]
    edge_send[1, :, LEAF : LEAF + WIDE] = total[0:8]
    edge_send[1, :, LEAF + WIDE :] = middle[0]

    pl.semaphore_wait(barrier, groups + parts - 2)

    def edge(k):
        peer = lax.rem(me + (1 if k == 0 else groups - 1), groups)
        return pltpu.make_async_remote_copy(
            src_ref=edge_send.at[k], dst_ref=edge_recv.at[k], send_sem=edge_send_sem.at[k],
            recv_sem=edge_recv_sem.at[k], device_id={"rows": peer}, device_id_type=MESH,
        )

    def message(step):
        peer = lax.rem(me + groups - step, groups)
        return pltpu.make_async_remote_copy(
            src_ref=send_ref, dst_ref=gathered_ref.at[step], send_sem=send_sem.at[step],
            recv_sem=recv_sem.at[step], device_id={"rows": peer}, device_id_type=MESH,
        )

    @pl.loop(1, groups)
    def _(step):
        message(step).start()

    edge(0).start()
    edge(1).start()

    weight = challenge_tile(challenge_ref)
    per_part = leaves // parts // 8

    @pl.loop(0, parts)
    def _(k):
        for load in table_loads(k):
            load.wait()

        @pl.loop(0, per_part)
        def _(j):
            block = k * per_part + j
            out = aligned(8 * block, 8)
            tiles = [[], []]
            for tile in range(16):
                at = aligned((16 * block + tile) * LANES, LANES)
                value = (index_ref[:, at].astype(F32) - TABLE_ROWS / 2) * (8.0 / TABLE_ROWS)
                tiles[tile % 2].append(multiplicity_ref[:, at].astype(F32) * invert(weight + value * value))
            table_ref[out, 0:LANES] = column_sums(tiles[0])
            table_ref[out, LANES:] = column_sums(tiles[1])
            terms = []
            for tile in range(8):
                value = x_ref[:, aligned((8 * block + tile + 1) * LANES, LANES)]
                terms.append(invert(weight + value * value))
            sums_ref[out, 0:LANES] = column_sums(terms)

    for load in loads[1]:
        load.wait()
    gathered_ref[0] = send_ref[...]

    @pl.loop(1, groups)
    def _(step):
        message(step).wait()

    edge(0).wait()
    edge(1).wait()
    x_ref[:, 0:LEAF] = edge_recv[0, :, 0:LEAF]
    x_ref[:, rows + LEAF :] = edge_recv[1, :, 0:LEAF]
    per_tile = LANES // (tops * NODES)
    pieces = []
    for k in range(groups // per_tile):
        tile = gathered_ref[per_tile * k]
        for place in range(1, per_tile):
            tile = jnp.where(group // tops == place, gathered_ref[per_tile * k + place], tile)
        pieces.append(tile)
    top_local = dot_pieces(
        two(jnp.concatenate(pieces, axis=1)), [piece[:, :LANES] for piece in weights("top")]
    )
    top_pair = two(top_local)
    line = [edge_recv[0, :, LEAF + WIDE :]] + middle + [edge_recv[1, :, LEAF + WIDE :]]
    left = jnp.concatenate([jnp.concatenate(line[g : g + 3], axis=1) for g in range(tops)], axis=0)
    middle_local = dot_pieces(two(left), weights("far1"))
    expanded = []
    for g in range(tops):
        from_top = dot_pieces(top_pair, weights("top_down", LANES * g, LANES * g + LANES))
        expanded += spread(middle_local[8 * g : 8 * g + 8] + from_top, NODES)
    local = dot_pieces(two(jnp.concatenate(expanded, axis=0)), weights("down"))
    moments = moments_ref[...]
    before = jnp.concatenate([edge_recv[0, :, LEAF : LEAF + WIDE], moments[:-8]], axis=0)
    after = jnp.concatenate([moments[8:], edge_recv[1, :, LEAF : LEAF + WIDE]], axis=0)
    for k, source in enumerate((before, moments, after)):
        local = local + dot_pieces(two(source), weights("far0", k * WIDE, k * WIDE + WIDE))
    local_ref[...] = local

    def piece(step):
        peer = lax.rem(part + 1 + step, parts)
        at = aligned(peer * (leaves // parts), leaves // parts)
        return pltpu.make_async_remote_copy(
            src_ref=partial_ref.at[at], dst_ref=pieces_ref.at[step], send_sem=piece_send.at[step],
            recv_sem=piece_recv.at[step], device_id={"cols": peer}, device_id_type=MESH,
        )

    def store(step):
        at = aligned(lax.rem(part + 1 + step, parts) * quarter_rows, quarter_rows)
        return pltpu.make_async_copy(coset_ref.at[:, at], coset_hbm.at[:, at], store_sem.at[step])

    @pl.loop(0, parts)
    def _(step):
        quarter = lax.rem(part + 1 + step, parts)

        @pl.loop(0, parents // parts // batch)
        def _(chunk):
            first = quarter * (parents // parts) + chunk * batch
            start = first * span
            count = batch * RADIX
            tiles = [x_ref[:, aligned(start + LEAF * j, LEAF)] for j in range(count + 2)]
            sources = [jnp.concatenate(tiles[k : k + count : 2], axis=0) for k in range(4)]
            expanded = []
            for p in range(batch):
                expanded += spread(local_ref[aligned(8 * (first + p), 8), :], 2 * NODES)
            sources.append(jnp.concatenate(expanded, axis=0))
            pairs = [two(source) for source in sources]
            left = [jnp.concatenate([pair[k] for pair in pairs], axis=1) for k in range(2)]
            result = dot_pieces(left, weights("out"))
            terms = []
            for j in range(count // 2):
                both = result[8 * j : 8 * j + 8]
                coset_ref[:, aligned(start + 2 * LEAF * j, 2 * LEAF)] = both
                for half in range(2):
                    value = both[:, LANES * half : LANES * half + LANES]
                    terms.append(invert(weight + value * value))
            for j in range(count // 8):
                sums_ref[aligned(first * RADIX + 8 * j, 8), LANES:] = column_sums(terms[8 * j : 8 * j + 8])

        at = aligned(quarter * (leaves // parts), leaves // parts)
        partial_ref[at, :] = dot_exact(sums_ref[at, :], weights("weave")[0]) - table_ref[at, :]
        note_ref[quarter] = fold(partial_ref[at, :])
        store(step).start()

        @pl.when(step < parts - 1)
        def _():
            piece(step).start()

    totals = [note_ref[p] for p in range(parts)]
    entry_ref[0] = (totals[0] + totals[1]) + (totals[2] + totals[3])

    def note(step):
        peer = lax.rem(me + groups - step, groups)
        return pltpu.make_async_remote_copy(
            src_ref=entry_ref.at[0], dst_ref=notes_ref.at[step], send_sem=note_send.at[step],
            recv_sem=note_recv.at[step], device_id={"rows": peer}, device_id_type=MESH,
        )

    def entry(step):
        peer = lax.rem(part + parts - step, parts)
        return pltpu.make_async_remote_copy(
            src_ref=entry_ref.at[1 + peer], dst_ref=entries_ref.at[step], send_sem=entry_send.at[step],
            recv_sem=entry_recv.at[step], device_id={"cols": peer}, device_id_type=MESH,
        )

    @pl.loop(1, groups)
    def _(step):
        note(step).start()

    @pl.loop(0, parts - 1)
    def _(step):
        piece(step).wait()

    own = partial_ref[aligned(part * (leaves // parts), leaves // parts), :]
    for step in range(parts - 1):
        own = own + pieces_ref[step]
    own_ref[...] = own

    @pl.loop(0, parts)
    def _(step):
        store(step).wait()

    @pl.loop(1, groups)
    def _(step):
        note(step).wait()

    entering = jnp.zeros((8, LANES), F32)
    for step in range(1, groups):
        entering = entering + jnp.where(me + step >= groups, notes_ref[step], 0.0)
    for p in range(parts):
        entry_ref[1 + p] = entering
        entering = entering + totals[p]

    @pl.loop(1, parts)
    def _(step):
        entry(step).start()

    @pl.loop(1, parts)
    def _(step):
        entry(step).wait()

    carry = entry_ref[1 + part]
    for step in range(1, parts):
        carry = carry + entries_ref[step]
    carry_ref[...] = carry


def output_kernel(
    scale, x_ref, coset_ref, own_ref, carry_ref, lane_ref, row_ref, extended_ref, fraction_ref, running_ref
):
    lane = lax.broadcasted_iota(jnp.int32, (8, LANES), 1)
    even = lane % 2 == 0
    for tile in range(x_ref.shape[1] // LANES):
        at = slice(tile * LANES, (tile + 1) * LANES)
        values = (x_ref[:, at], coset_ref[:, at])
        for half in range(2):
            place = lane // 2 + half * (LANES // 2)
            sides = [jnp.take_along_axis(value, place, axis=1) for value in values]
            out = (2 * tile + half) * LANES
            extended_ref[:, out : out + LANES] = jnp.where(even, sides[0], sides[1])

    @pl.when(pl.program_id(0) == 0)
    def _():
        own = own_ref[...]
        size = own.shape[0]
        within = dot_exact(own, lane_ref[...])
        ends = jnp.broadcast_to(within[:, WIDE - 1 :], (size, LANES))
        high, low = two(ends)
        rest = (ends - high.astype(F32) - low.astype(F32)).astype(BF16)
        before = dot16(row_ref[...], rest) + dot16(row_ref[...], low) + dot16(row_ref[...], high)
        before = before + jnp.sum(carry_ref[...])
        for half in range(2):
            at = slice(half * LANES, (half + 1) * LANES)
            out = pl.ds(half, size, stride=2)
            fraction_ref[out, :] = own[:, at]
            running_ref[out, :] = (within[:, at] + before) * scale


def local(groups, parts, trace_values, challenges, multiplicity, table_index):
    columns, rows = trace_values.shape
    total = groups * rows
    (high, low), places = matrices(total, groups)
    leaves = rows // LEAF
    parents = leaves // RADIX
    vmem = pl.BlockSpec(memory_space=pltpu.VMEM)
    smem = pl.BlockSpec(memory_space=pltpu.SMEM)
    hbm = pl.BlockSpec(memory_space=pl.ANY)
    dma = pltpu.SemaphoreType.DMA
    size = leaves // parts
    tile = lambda *lead: pltpu.VMEM(lead + (columns, LANES), F32)
    coset, own, carry = pl.pallas_call(
        functools.partial(main_kernel, groups, parts, places, BATCH),
        out_shape=(
            jax.ShapeDtypeStruct((columns, rows), F32),
            jax.ShapeDtypeStruct((size, WIDE), F32),
            jax.ShapeDtypeStruct((columns, LANES), F32),
        ),
        in_specs=[smem] + [hbm] * 5,
        out_specs=(hbm, vmem, vmem),
        scratch_shapes=[
            pltpu.VMEM((columns, rows + 2 * LEAF), F32),
            pltpu.VMEM((columns, 2 * rows), jnp.int32),
            pltpu.VMEM((columns, 2 * rows), jnp.int32),
            pltpu.VMEM(high.shape, BF16),
            pltpu.VMEM(high.shape, BF16),
            pltpu.VMEM((columns, rows), F32),
            pltpu.VMEM((columns * parents, WIDE), F32),
            pltpu.VMEM((columns * parents, WIDE), F32),
            pltpu.VMEM((leaves, WIDE), F32),
            pltpu.VMEM((leaves, WIDE), F32),
            pltpu.VMEM((leaves, WIDE), F32),
            tile(),
            tile(groups),
            pltpu.VMEM((2, columns, LEAF + 2 * WIDE), F32),
            pltpu.VMEM((2, columns, LEAF + 2 * WIDE), F32),
            pltpu.VMEM((parts - 1, size, WIDE), F32),
            tile(parts),
            tile(groups),
            tile(1 + parts),
            tile(parts),
            dma, dma((4,)), dma((2, parts)), dma((parts,)),
            dma((groups,)), dma((groups,)), dma((2,)), dma((2,)),
            dma((parts,)), dma((parts,)), dma((groups,)), dma((groups,)), dma((parts,)), dma((parts,)),
        ],
        compiler_params=pltpu.CompilerParams(
            collective_id=0, has_side_effects=True, vmem_limit_bytes=56 * 2**20
        ),
        name="main",
    )(challenges, trace_values, multiplicity, table_index, high, low)
    steps = 8
    whole = lambda *shape: pl.BlockSpec(shape, lambda i: (0,) * len(shape))
    lane_sum = np.triu(np.ones((WIDE, WIDE))).astype(ml_dtypes.bfloat16)
    row_sum = np.tril(np.ones((size, size)), -1).astype(ml_dtypes.bfloat16)
    flat = jax.ShapeDtypeStruct((2 * size, LANES), F32)
    extended, fraction, running = pl.pallas_call(
        functools.partial(output_kernel, 1.0 / (2 * total)),
        grid=(steps,),
        out_shape=(jax.ShapeDtypeStruct((columns, 2 * rows), F32), flat, flat),
        in_specs=[
            pl.BlockSpec((columns, rows // steps), lambda i: (0, i)),
            pl.BlockSpec((columns, rows // steps), lambda i: (0, i)),
            whole(size, WIDE),
            whole(columns, LANES),
            whole(WIDE, WIDE),
            whole(size, size),
        ],
        out_specs=(
            pl.BlockSpec((columns, 2 * rows // steps), lambda i: (0, i)),
            whole(2 * size, LANES),
            whole(2 * size, LANES),
        ),
        compiler_params=pltpu.CompilerParams(vmem_limit_bytes=32 * 2**20),
        name="weave",
    )(trace_values, coset, own, carry, lane_sum, row_sum)
    return extended, fraction.reshape(-1), running.reshape(-1)


def solution(mesh):
    return jax.shard_map(
        functools.partial(local, mesh.shape["rows"], mesh.shape["cols"]),
        mesh=mesh,
        in_specs=(P("cols", "rows"), P("cols"), P("cols", "rows"), P("cols", "rows")),
        out_specs=(P("cols", "rows"), P(("rows", "cols")), P(("rows", "cols"))),
        check_vma=False,
    )
```

```python
import functools
import math

import jax
import jax.numpy as jnp
import ml_dtypes
import numpy as np
from jax import lax
from jax.experimental import pallas as pl
from jax.experimental.pallas import tpu as pltpu
from jax.sharding import PartitionSpec as P

TABLE_ROWS = 8188
NODES = 16
LEAF = 128
RADIX = 16
LANES = 128
WIDE = RADIX * NODES
BATCH = 4
CHUNKS = 4
STEPS = ((2, 0), (2, 1), (1, 1), (3, 0), (1, 0), (3, 1), (0, 0), (0, 1))
QUARTERS = sum(quarter * 4**step for step, (quarter, _) in enumerate(STEPS))
HALVES = sum(half * 2**step for step, (_, half) in enumerate(STEPS))
MESH = pl.DeviceIdType.MESH
F32 = jnp.float32
BF16 = jnp.bfloat16


def chebyshev():
    return np.cos((2 * np.arange(NODES) + 1) * np.pi / (2 * NODES))


def lagrange(places):
    order = np.arange(1, NODES)
    waves = np.cos(order * np.arccos(np.clip(places, -1, 1))[..., None])
    at_nodes = np.cos(order * np.arccos(chebyshev())[:, None])
    return (1 + 2 * waves @ at_nodes.T) / NODES


def sign(index):
    return 1.0 - 2.0 * (index % 2)


def cotangent(offset, total):
    return 1.0 / np.tan(np.pi * offset / total) / total


def point_to_moment():
    rows = np.arange(LEAF)
    return sign(rows)[:, None] * lagrange((rows - LEAF / 2) / (LEAF / 2))


def local_to_point():
    rows = np.arange(LEAF)
    return (sign(rows)[:, None] * lagrange((rows + 0.5 - LEAF / 2) / (LEAF / 2))).T


def child_to_parent():
    child = np.arange(RADIX)[:, None]
    return lagrange((2 * child + 1 + chebyshev()[None]) / RADIX - 1).reshape(RADIX * NODES, NODES)


def far_weights(sources, targets, width, total, blocks):
    nodes = chebyshev()
    apart = (targets[None, :] - sources[:, None])[:, None, :, None]
    offset = width * apart + width / 2 * (nodes[None, None, None, :] - nodes[None, :, None, None])
    far = np.abs(apart) >= 2
    if blocks:
        far = far & (np.abs(apart) <= blocks - 2)
    far = np.broadcast_to(far, offset.shape)
    weights = np.where(far, cotangent(np.where(far, offset, 1.0), total), 0.0)
    return weights.reshape(sources.size * NODES, targets.size * NODES)


def split(matrix):
    high = matrix.astype(np.float32).astype(ml_dtypes.bfloat16)
    low = (matrix - high.astype(np.float64)).astype(np.float32).astype(ml_dtypes.bfloat16)
    return high, low


def matrices(total, groups):
    middle = LEAF * RADIX
    top = middle * RADIX
    blocks = total // top
    per_device = blocks // groups
    c2p = child_to_parent()
    three = np.arange(3 * RADIX) - RADIX
    one = np.arange(RADIX)
    top_far = np.zeros((blocks * NODES, WIDE))
    top_far[:, : per_device * NODES] = far_weights(
        np.arange(blocks), np.arange(per_device), top, total, blocks
    )
    top_down = np.zeros((per_device, LANES, WIDE))
    for block in range(per_device):
        top_down[block, block * NODES : (block + 1) * NODES] = c2p.T
    source = np.arange(4 * LEAF)[:, None] - LEAF
    target = np.arange(2 * LEAF)[None, :]
    near = sign(target - source) * cotangent(target - source + 0.5, total)
    near = np.where(np.abs(target // LEAF - source // LEAF) <= 1, near, 0.0)
    child_out = np.zeros((LANES // NODES, NODES, 2, LEAF))
    for child in range(LANES // NODES):
        child_out[child, :, child % 2] = local_to_point()
    weave = np.zeros((2, LEAF, 2 * LEAF))
    for side in range(2):
        weave[side, np.arange(LEAF), 2 * np.arange(LEAF) + side] = 1.0
    parts = dict(
        p2m=np.tile(point_to_moment(), (1, RADIX)),
        up=np.tile(c2p, (1, RADIX)),
        far0=far_weights(three, one, LEAF, total, 0),
        far1=far_weights(three, one, middle, total, 0),
        top=top_far,
        top_down=top_down.reshape(-1, WIDE),
        down=np.tile(c2p.T, (LANES // NODES, 1)),
        out=np.concatenate([near, child_out.reshape(LANES, WIDE)]),
        weave=weave.reshape(2 * LEAF, WIDE),
    )
    places, start = {}, 0
    for name, part in parts.items():
        places[name] = (start, start + part.shape[0])
        start += part.shape[0]
    return split(np.concatenate(list(parts.values()))), places


def dot16(left, right):
    return jnp.dot(left, right, preferred_element_type=F32)


def two(value):
    high = value.astype(BF16)
    return high, (value - high.astype(F32)).astype(BF16)


def dot_pieces(left, right):
    rows = left[0].shape[0]
    both = dot16(jnp.concatenate(left, axis=0), right[0])
    return both[rows:] + dot16(left[0], right[1]) + both[:rows]


def dot_exact(left, right):
    rows = left.shape[0]
    high, low = two(left)
    rest = (left - high.astype(F32) - low.astype(F32)).astype(BF16)
    pieces = dot16(jnp.concatenate([rest, low, high], axis=0), right)
    return pieces[:rows] + pieces[rows : 2 * rows] + pieces[2 * rows :]


def spread(local, span):
    group = lax.broadcasted_iota(jnp.int32, (8, LANES), 1) // span
    half = LANES // span
    tiles = []
    for child in range(WIDE // span):
        tile = local[:, (child // half) * LANES : (child // half + 1) * LANES]
        tiles.append(jnp.where(group == child % half, tile, 0.0))
    return tiles


def gather_children(copies):
    group = lax.broadcasted_iota(jnp.int32, (8, WIDE), 1) // NODES
    total = jnp.zeros((8, WIDE), F32)
    for child in range(RADIX):
        total = jnp.where(group == child, copies[8 * child : 8 * child + 8], total)
    return total


def column_sums(tiles):
    row = lax.broadcasted_iota(jnp.int32, (8, LANES), 0)
    for shift in (1, 2, 4):
        first = (row // shift) % 2 == 0
        tiles = [
            jnp.where(first, a, b) + pltpu.roll(jnp.where(first, b, a), shift, 0)
            for a, b in zip(tiles[0::2], tiles[1::2])
        ]
    return tiles[0]


def invert(value):
    guess = pl.reciprocal(value, approx=True)
    return guess * (2.0 - value * guess)


def challenge_tile(challenge_ref):
    row = lax.broadcasted_iota(jnp.int32, (8, LANES), 0)
    tile = jnp.zeros((8, LANES), F32)
    for column in range(8):
        tile = jnp.where(row == column, challenge_ref[column], tile)
    return tile


def fold(rows):
    total = jnp.zeros((8, LANES), F32)
    for r in range(rows.shape[0] // 8):
        for l in range(rows.shape[1] // LANES):
            total = total + rows[8 * r : 8 * r + 8, LANES * l : LANES * l + LANES]
    return total


def aligned(start, size):
    return pl.ds(pl.multiple_of(start, size), size)


def greet(axes):
    barrier = pltpu.get_barrier_semaphore()
    for axis, size in axes:
        me = lax.axis_index(axis)

        @pl.loop(1, size)
        def _(step):
            peer = lax.rem(me + step, size)
            pl.semaphore_signal(barrier, inc=1, device_id={axis: peer}, device_id_type=MESH)

    return barrier


def main_kernel(
    groups, parts, places, batch, challenge_ref, x_hbm, multiplicity_hbm, index_hbm, high_hbm, low_hbm,
    coset_hbm, own_ref, carry_ref,
    x_ref, multiplicity_ref, index_ref, high_ref, low_ref, coset_ref, moments_ref, local_ref, sums_ref, table_ref,
    partial_ref, send_ref, gathered_ref, edge_send, edge_recv, pieces_ref, note_ref, notes_ref, entry_ref, entries_ref,
    x_sem, load_sem, table_sem, store_sem, send_sem, recv_sem, edge_send_sem, edge_recv_sem,
    piece_send, piece_recv, note_send, note_recv, entry_send, entry_recv,
):
    me = lax.axis_index("rows")
    part = lax.axis_index("cols")
    rows = x_hbm.shape[1]
    leaves = rows // LEAF
    parents = leaves // RADIX
    tops = parents // RADIX
    span = LEAF * RADIX
    quarter_rows = rows // parts
    inner = pl.ds(LEAF, rows)

    def weights(name, first=0, last=None):
        start, stop = places[name]
        at = slice(start + first, stop if last is None else start + last)
        return high_ref[at, :], low_ref[at, :]

    early = places["up"][1]
    late = high_ref.shape[0] - early
    load_x = pltpu.make_async_copy(x_hbm, x_ref.at[:, inner], x_sem)
    loads = []
    for k, at in enumerate((pl.ds(0, early), pl.ds(early, late))):
        loads.append(
            [
                pltpu.make_async_copy(high_hbm.at[at], high_ref.at[at], load_sem.at[2 * k]),
                pltpu.make_async_copy(low_hbm.at[at], low_ref.at[at], load_sem.at[2 * k + 1]),
            ]
        )

    def table_loads(k):
        at = aligned(k * 2 * quarter_rows, 2 * quarter_rows)
        return (
            pltpu.make_async_copy(multiplicity_hbm.at[:, at], multiplicity_ref.at[:, at], table_sem.at[0, k]),
            pltpu.make_async_copy(index_hbm.at[:, at], index_ref.at[:, at], table_sem.at[1, k]),
        )

    for load in loads[0]:
        load.start()
    load_x.start()
    barrier = greet((("rows", groups), ("cols", parts)))
    for load in loads[0]:
        load.wait()
    load_x.wait()
    for k in range(parts):
        for load in table_loads(k):
            load.start()
    for load in loads[1]:
        load.start()

    own_group = lax.broadcasted_iota(jnp.int32, (LEAF, WIDE), 1) // NODES
    p2m = weights("p2m")
    total = jnp.zeros((8 * parents, WIDE), F32)
    for pair in range(RADIX // 2):
        start = LEAF + 2 * LEAF * pair
        left = jnp.concatenate(
            [x_ref[:, span * p + start : span * p + start + 2 * LEAF] for p in range(parents)], axis=0
        )
        right = [
            jnp.concatenate(
                [jnp.where(own_group == 2 * pair + k, piece, jnp.zeros_like(piece)) for k in range(2)], axis=0
            )
            for piece in p2m
        ]
        total = total + dot_pieces(two(left), right)
    moments_ref[...] = total
    up = weights("up")
    copies = dot_pieces(two(total), up)
    middle = [gather_children(copies[128 * g : 128 * g + 128]) for g in range(tops)]
    high = dot_pieces(two(jnp.concatenate(middle, axis=0)), [piece[:, :LANES] for piece in up])
    group = lax.broadcasted_iota(jnp.int32, (8, LANES), 1) // NODES
    packed = high[0:8]
    for g in range(1, tops):
        packed = jnp.where(group % tops == g, high[8 * g : 8 * g + 8], packed)
    send_ref[...] = packed
    edge_send[0, :, 0:LEAF] = x_ref[:, rows : rows + LEAF]
    edge_send[0, :, LEAF : LEAF + WIDE] = total[8 * (parents - 1) : 8 * parents]
    edge_send[0, :, LEAF + WIDE :] = middle[tops - 1]
    edge_send[1, :, 0:LEAF] = x_ref[:, LEAF : 2 * LEAF]
    edge_send[1, :, LEAF : LEAF + WIDE] = total[0:8]
    edge_send[1, :, LEAF + WIDE :] = middle[0]

    pl.semaphore_wait(barrier, groups + parts - 2)

    def edge(k):
        peer = lax.rem(me + (1 if k == 0 else groups - 1), groups)
        return pltpu.make_async_remote_copy(
            src_ref=edge_send.at[k], dst_ref=edge_recv.at[k], send_sem=edge_send_sem.at[k],
            recv_sem=edge_recv_sem.at[k], device_id={"rows": peer}, device_id_type=MESH,
        )

    def message(step):
        peer = lax.rem(me + groups - step, groups)
        return pltpu.make_async_remote_copy(
            src_ref=send_ref, dst_ref=gathered_ref.at[step], send_sem=send_sem.at[step],
            recv_sem=recv_sem.at[step], device_id={"rows": peer}, device_id_type=MESH,
        )

    edge(0).start()
    edge(1).start()

    @pl.loop(1, groups)
    def _(step):
        message(step).start()

    weight = challenge_tile(challenge_ref)
    per_part = leaves // parts // 8

    @pl.loop(0, parts)
    def _(k):
        for load in table_loads(k):
            load.wait()

        @pl.loop(0, per_part)
        def _(j):
            block = k * per_part + j
            out = aligned(8 * block, 8)
            tiles = [[], []]
            for tile in range(16):
                at = aligned((16 * block + tile) * LANES, LANES)
                value = (index_ref[:, at].astype(F32) - TABLE_ROWS / 2) * (8.0 / TABLE_ROWS)
                tiles[tile % 2].append(multiplicity_ref[:, at].astype(F32) * invert(weight + value * value))
            table_ref[out, 0:LANES] = column_sums(tiles[0])
            table_ref[out, LANES:] = column_sums(tiles[1])
            terms = []
            for tile in range(8):
                value = x_ref[:, aligned((8 * block + tile + 1) * LANES, LANES)]
                terms.append(invert(weight + value * value))
            sums_ref[out, 0:LANES] = column_sums(terms)

    for load in loads[1]:
        load.wait()
    moments = moments_ref[...]
    blank = jnp.zeros((8, WIDE), F32)
    far0 = [weights("far0", k * WIDE, k * WIDE + WIDE) for k in range(3)]
    far1 = [weights("far1", k * WIDE, k * WIDE + WIDE) for k in range(3)]
    local = dot_pieces(two(moments), far0[1])
    local = local + dot_pieces(two(jnp.concatenate([blank, moments[:-8]], axis=0)), far0[0])
    local_ref[...] = local + dot_pieces(two(jnp.concatenate([moments[8:], blank], axis=0)), far0[2])
    line = [blank] + middle + [blank]
    left = jnp.concatenate([jnp.concatenate(line[g : g + 3], axis=1) for g in range(tops)], axis=0)
    inner_local = dot_pieces(two(left), weights("far1"))
    gathered_ref[0] = send_ref[...]

    edge(0).wait()
    edge(1).wait()
    x_ref[:, 0:LEAF] = edge_recv[0, :, 0:LEAF]
    x_ref[:, rows + LEAF :] = edge_recv[1, :, 0:LEAF]
    for k, at in ((0, slice(0, 8)), (1, slice(8 * parents - 8, 8 * parents))):
        local_ref[at, :] = local_ref[at, :] + dot_pieces(two(edge_recv[k, :, LEAF : LEAF + WIDE]), far0[2 * k])
    edges = [dot_pieces(two(edge_recv[k, :, LEAF + WIDE :]), far1[2 * k]) for k in range(2)]

    @pl.loop(1, groups)
    def _(step):
        message(step).wait()

    per_tile = LANES // (tops * NODES)
    pieces = []
    for k in range(groups // per_tile):
        tile = gathered_ref[per_tile * k]
        for place in range(1, per_tile):
            tile = jnp.where(group // tops == place, gathered_ref[per_tile * k + place], tile)
        pieces.append(tile)
    top_local = dot_pieces(
        two(jnp.concatenate(pieces, axis=1)), [piece[:, :LANES] for piece in weights("top")]
    )
    top_pair = two(top_local)
    expanded = []
    for g in range(tops):
        here = dot_pieces(top_pair, weights("top_down", LANES * g, LANES * g + LANES))
        here = here + inner_local[8 * g : 8 * g + 8]
        if g == 0:
            here = here + edges[0]
        if g == tops - 1:
            here = here + edges[1]
        expanded += spread(here, NODES)
    local_ref[...] = local_ref[...] + dot_pieces(two(jnp.concatenate(expanded, axis=0)), weights("down"))

    half_leaves = leaves // parts // 2
    half_rows = quarter_rows // 2
    before_me = lax.rem(part + parts - 1, parts)
    after_me = lax.rem(part + 1, parts)

    def half_at(quarter, half):
        return aligned((2 * quarter + half) * half_leaves, half_leaves)

    def ship(slot, source, peer):
        return pltpu.make_async_remote_copy(
            src_ref=partial_ref.at[source], dst_ref=pieces_ref.at[slot], send_sem=piece_send.at[slot],
            recv_sem=piece_recv.at[slot], device_id={"cols": peer}, device_id_type=MESH,
        )

    opposite = lax.rem(part + 2, parts)
    ships = (
        ship(0, half_at(opposite, 0), after_me),
        ship(1, half_at(opposite, 1), before_me),
        ship(2, half_at(after_me, 1), after_me),
        ship(3, half_at(before_me, 0), before_me),
        ship(4, half_at(after_me, 0), after_me),
        ship(5, half_at(before_me, 1), before_me),
    )

    def store(step, at):
        return pltpu.make_async_copy(coset_ref.at[:, at], coset_hbm.at[:, at], store_sem.at[step])

    @pl.loop(0, 2 * parts)
    def _(step):
        quarter = lax.rem(part + lax.rem(lax.shift_right_logical(QUARTERS, 2 * step), 4), parts)
        half = 2 * quarter + lax.rem(lax.shift_right_logical(HALVES, step), 2)

        @pl.loop(0, half_leaves // RADIX // batch)
        def _(chunk):
            first = half * (half_leaves // RADIX) + chunk * batch
            start = first * span
            count = batch * RADIX
            tiles = [x_ref[:, aligned(start + LEAF * j, LEAF)] for j in range(count + 2)]
            sources = [jnp.concatenate(tiles[k : k + count : 2], axis=0) for k in range(4)]
            expanded = []
            for p in range(batch):
                expanded += spread(local_ref[aligned(8 * (first + p), 8), :], 2 * NODES)
            sources.append(jnp.concatenate(expanded, axis=0))
            pairs = [two(source) for source in sources]
            left = [jnp.concatenate([pair[k] for pair in pairs], axis=1) for k in range(2)]
            result = dot_pieces(left, weights("out"))
            terms = []
            for j in range(count // 2):
                both = result[8 * j : 8 * j + 8]
                coset_ref[:, aligned(start + 2 * LEAF * j, 2 * LEAF)] = both
                for side in range(2):
                    value = both[:, LANES * side : LANES * side + LANES]
                    terms.append(invert(weight + value * value))
            for j in range(count // 8):
                sums_ref[aligned(first * RADIX + 8 * j, 8), LANES:] = column_sums(terms[8 * j : 8 * j + 8])

        at = aligned(half * half_leaves, half_leaves)
        partial = dot_exact(sums_ref[at, :], weights("weave")[0]) - table_ref[at, :]
        note_ref[half] = fold(partial)
        partial_ref[at, :] = partial
        store(step, aligned(half * half_rows, half_rows)).start()
        for k in range(6):

            @pl.when(step == k)
            def _(k=k):
                if k >= 4:
                    ships[k - 4].wait_recv()
                    partial_ref[at, :] = partial_ref[at, :] + pieces_ref[k - 4]
                ships[k].start()

    totals = [note_ref[2 * p] + note_ref[2 * p + 1] for p in range(parts)]
    entry_ref[0] = (totals[0] + totals[1]) + (totals[2] + totals[3])

    def note(step):
        peer = lax.rem(me + groups - step, groups)
        return pltpu.make_async_remote_copy(
            src_ref=entry_ref.at[0], dst_ref=notes_ref.at[step], send_sem=note_send.at[step],
            recv_sem=note_recv.at[step], device_id={"rows": peer}, device_id_type=MESH,
        )

    def entry(step):
        peer = lax.rem(part + parts - step, parts)
        return pltpu.make_async_remote_copy(
            src_ref=entry_ref.at[1 + peer], dst_ref=entries_ref.at[step], send_sem=entry_send.at[step],
            recv_sem=entry_recv.at[step], device_id={"cols": peer}, device_id_type=MESH,
        )

    @pl.loop(1, groups)
    def _(step):
        note(step).start()

    for k in range(2):
        ships[k].wait_send()
    for k in range(2, 6):
        ships[k].wait()
    for half, slots in ((0, (3, 4)), (1, (2, 5))):
        own = partial_ref[half_at(part, half), :]
        own_ref[half * half_leaves : (half + 1) * half_leaves, :] = own + pieces_ref[slots[0]] + pieces_ref[slots[1]]

    @pl.loop(0, 2 * parts)
    def _(step):
        store(step, aligned(step * half_rows, half_rows)).wait()

    @pl.loop(1, groups)
    def _(step):
        note(step).wait()

    entering = jnp.zeros((8, LANES), F32)
    for step in range(1, groups):
        entering = entering + jnp.where(me + step >= groups, notes_ref[step], 0.0)
    for p in range(parts):
        entry_ref[1 + p] = entering
        entering = entering + totals[p]

    @pl.loop(1, parts)
    def _(step):
        entry(step).start()

    @pl.loop(1, parts)
    def _(step):
        entry(step).wait()

    carry = entry_ref[1 + part]
    for step in range(1, parts):
        carry = carry + entries_ref[step]
    carry_ref[...] = carry


def output_kernel(
    scale, x_hbm, coset_hbm, own_hbm, carry_hbm, weave_hbm, lane_hbm, row_hbm, extended_hbm, fraction_hbm, running_hbm,
    x_ref, coset_ref, own_ref, carry_ref, weave_ref, lane_ref, row_ref, extended_ref, fraction_ref, running_ref,
    load_sem, x_sem, coset_sem, out_sem, store_sem,
):
    rows = x_ref.shape[1]
    chunks = x_sem.shape[0]
    size = rows // chunks
    small = (
        (weave_hbm, weave_ref), (own_hbm, own_ref), (carry_hbm, carry_ref), (lane_hbm, lane_ref), (row_hbm, row_ref),
    )
    loads = [pltpu.make_async_copy(*pair, load_sem.at[k]) for k, pair in enumerate(small)]

    def rows_in(k):
        at = aligned(k * size, size)
        return (
            pltpu.make_async_copy(x_hbm.at[:, at], x_ref.at[:, at], x_sem.at[k]),
            pltpu.make_async_copy(coset_hbm.at[:, at], coset_ref.at[:, at], coset_sem.at[k]),
        )

    def rows_out(k):
        at = aligned(2 * k * size, 2 * size)
        return pltpu.make_async_copy(extended_ref.at[:, at], extended_hbm.at[:, at], out_sem.at[k])

    loads[0].start()
    for k in range(chunks):
        for load in rows_in(k):
            load.start()
    for load in loads[1:]:
        load.start()
    loads[0].wait()

    @pl.loop(0, chunks)
    def _(k):
        for load in rows_in(k):
            load.wait()
        count = size // LANES
        slices = [aligned(k * size + tile * LANES, LANES) for tile in range(count)]
        own = jnp.concatenate([x_ref[:, at] for at in slices], axis=0)
        between = jnp.concatenate([coset_ref[:, at] for at in slices], axis=0)
        high, low = two(own)
        rest = (own - high.astype(F32) - low.astype(F32)).astype(BF16)
        both = dot16(jnp.concatenate([rest, low, high, *two(between)], axis=1), weave_ref[...])
        for tile in range(count):
            extended_ref[:, aligned(2 * k * size + tile * WIDE, WIDE)] = both[8 * tile : 8 * tile + 8]
        rows_out(k).start()

    for load in loads[1:]:
        load.wait()
    own = own_ref[...]
    size_own = own.shape[0]
    within = dot_exact(own, lane_ref[...])
    ends = jnp.broadcast_to(within[:, WIDE - 1 :], (size_own, LANES))
    high, low = two(ends)
    rest = (ends - high.astype(F32) - low.astype(F32)).astype(BF16)
    before = dot16(row_ref[...], rest) + dot16(row_ref[...], low) + dot16(row_ref[...], high)
    before = before + jnp.sum(carry_ref[...])
    for half in range(2):
        at = slice(half * LANES, (half + 1) * LANES)
        out = pl.ds(half, size_own, stride=2)
        fraction_ref[out, :] = own[:, at]
        running_ref[out, :] = (within[:, at] + before) * scale
    stores = [
        pltpu.make_async_copy(fraction_ref, fraction_hbm, store_sem.at[0]),
        pltpu.make_async_copy(running_ref, running_hbm, store_sem.at[1]),
    ]
    for store in stores:
        store.start()

    @pl.loop(0, chunks)
    def _(k):
        rows_out(k).wait()

    for store in stores:
        store.wait()


def local(groups, parts, trace_values, challenges, multiplicity, table_index):
    columns, rows = trace_values.shape
    total = groups * rows
    (high, low), places = matrices(total, groups)
    leaves = rows // LEAF
    parents = leaves // RADIX
    vmem = pl.BlockSpec(memory_space=pltpu.VMEM)
    smem = pl.BlockSpec(memory_space=pltpu.SMEM)
    hbm = pl.BlockSpec(memory_space=pl.ANY)
    dma = pltpu.SemaphoreType.DMA
    size = leaves // parts
    tile = lambda *lead: pltpu.VMEM(lead + (columns, LANES), F32)
    coset, own, carry = pl.pallas_call(
        functools.partial(main_kernel, groups, parts, places, BATCH),
        out_shape=(
            jax.ShapeDtypeStruct((columns, rows), F32),
            jax.ShapeDtypeStruct((size, WIDE), F32),
            jax.ShapeDtypeStruct((columns, LANES), F32),
        ),
        in_specs=[smem] + [hbm] * 5,
        out_specs=(hbm, vmem, vmem),
        scratch_shapes=[
            pltpu.VMEM((columns, rows + 2 * LEAF), F32),
            pltpu.VMEM((columns, 2 * rows), jnp.int32),
            pltpu.VMEM((columns, 2 * rows), jnp.int32),
            pltpu.VMEM(high.shape, BF16),
            pltpu.VMEM(high.shape, BF16),
            pltpu.VMEM((columns, rows), F32),
            pltpu.VMEM((columns * parents, WIDE), F32),
            pltpu.VMEM((columns * parents, WIDE), F32),
            pltpu.VMEM((leaves, WIDE), F32),
            pltpu.VMEM((leaves, WIDE), F32),
            pltpu.VMEM((leaves, WIDE), F32),
            tile(),
            tile(groups),
            pltpu.VMEM((2, columns, LEAF + 2 * WIDE), F32),
            pltpu.VMEM((2, columns, LEAF + 2 * WIDE), F32),
            pltpu.VMEM((6, size // 2, WIDE), F32),
            tile(2 * parts),
            tile(groups),
            tile(1 + parts),
            tile(parts),
            dma, dma((4,)), dma((2, parts)), dma((2 * parts,)),
            dma((groups,)), dma((groups,)), dma((2,)), dma((2,)),
            dma((6,)), dma((6,)), dma((groups,)), dma((groups,)), dma((parts,)), dma((parts,)),
        ],
        compiler_params=pltpu.CompilerParams(
            collective_id=0, has_side_effects=True, vmem_limit_bytes=56 * 2**20
        ),
        name="main",
    )(challenges, trace_values, multiplicity, table_index, high, low)
    weave_rows = high[slice(*places["weave"])].reshape(2, LEAF, WIDE)[np.array((0, 0, 0, 1, 1))].reshape(-1, WIDE)
    lane_sum = np.triu(np.ones((WIDE, WIDE))).astype(ml_dtypes.bfloat16)
    row_sum = np.tril(np.ones((size, size)), -1).astype(ml_dtypes.bfloat16)
    flat = jax.ShapeDtypeStruct((2 * size, LANES), F32)
    extended, fraction, running = pl.pallas_call(
        functools.partial(output_kernel, 1.0 / (2 * total)),
        out_shape=(jax.ShapeDtypeStruct((columns, 2 * rows), F32), flat, flat),
        in_specs=[hbm] * 7,
        out_specs=(hbm, hbm, hbm),
        scratch_shapes=[
            pltpu.VMEM((columns, rows), F32),
            pltpu.VMEM((columns, rows), F32),
            pltpu.VMEM((size, WIDE), F32),
            tile(),
            pltpu.VMEM((5 * LEAF, WIDE), BF16),
            pltpu.VMEM((WIDE, WIDE), BF16),
            pltpu.VMEM((size, size), BF16),
            pltpu.VMEM((columns, 2 * rows), F32),
            pltpu.VMEM((2 * size, LANES), F32),
            pltpu.VMEM((2 * size, LANES), F32),
            dma((5,)), dma((CHUNKS,)), dma((CHUNKS,)), dma((CHUNKS,)), dma((2,)),
        ],
        compiler_params=pltpu.CompilerParams(vmem_limit_bytes=60 * 2**20),
        name="weave",
    )(trace_values, coset, own, carry, weave_rows, lane_sum, row_sum)
    return extended, fraction.reshape(-1), running.reshape(-1)


def solution(mesh):
    return jax.shard_map(
        functools.partial(local, mesh.shape["rows"], mesh.shape["cols"]),
        mesh=mesh,
        in_specs=(P("cols", "rows"), P("cols"), P("cols", "rows"), P("cols", "rows")),
        out_specs=(P("cols", "rows"), P(("rows", "cols")), P(("rows", "cols"))),
        check_vma=False,
    )
```

```python
import functools
import math

import jax
import jax.numpy as jnp
import ml_dtypes
import numpy as np
from jax import lax
from jax.experimental import pallas as pl
from jax.experimental.pallas import tpu as pltpu
from jax.sharding import PartitionSpec as P

TABLE_ROWS = 8188
NODES = 16
LEAF = 128
RADIX = 16
LANES = 128
WIDE = RADIX * NODES
BATCH = 4
CHUNKS = 4
FAR_FIRST = 2 + 1 * 4 + 3 * 16 + 0 * 64
STEPS = ((2, 0), (2, 1), (1, 1), (3, 0), (1, 0), (3, 1), (0, 0), (0, 1))
QUARTERS = sum(quarter * 4**step for step, (quarter, _) in enumerate(STEPS))
HALVES = sum(half * 2**step for step, (_, half) in enumerate(STEPS))
MESH = pl.DeviceIdType.MESH
F32 = jnp.float32
BF16 = jnp.bfloat16


def chebyshev():
    return np.cos((2 * np.arange(NODES) + 1) * np.pi / (2 * NODES))


def lagrange(places):
    order = np.arange(1, NODES)
    waves = np.cos(order * np.arccos(np.clip(places, -1, 1))[..., None])
    at_nodes = np.cos(order * np.arccos(chebyshev())[:, None])
    return (1 + 2 * waves @ at_nodes.T) / NODES


def sign(index):
    return 1.0 - 2.0 * (index % 2)


def cotangent(offset, total):
    return 1.0 / np.tan(np.pi * offset / total) / total


def point_to_moment():
    rows = np.arange(LEAF)
    return sign(rows)[:, None] * lagrange((rows - LEAF / 2) / (LEAF / 2))


def local_to_point():
    rows = np.arange(LEAF)
    return (sign(rows)[:, None] * lagrange((rows + 0.5 - LEAF / 2) / (LEAF / 2))).T


def child_to_parent():
    child = np.arange(RADIX)[:, None]
    return lagrange((2 * child + 1 + chebyshev()[None]) / RADIX - 1).reshape(RADIX * NODES, NODES)


def far_weights(sources, targets, width, total, blocks):
    nodes = chebyshev()
    apart = (targets[None, :] - sources[:, None])[:, None, :, None]
    offset = width * apart + width / 2 * (nodes[None, None, None, :] - nodes[None, :, None, None])
    far = np.abs(apart) >= 2
    if blocks:
        far = far & (np.abs(apart) <= blocks - 2)
    far = np.broadcast_to(far, offset.shape)
    weights = np.where(far, cotangent(np.where(far, offset, 1.0), total), 0.0)
    return weights.reshape(sources.size * NODES, targets.size * NODES)


def split(matrix):
    high = matrix.astype(np.float32).astype(ml_dtypes.bfloat16)
    low = (matrix - high.astype(np.float64)).astype(np.float32).astype(ml_dtypes.bfloat16)
    return high, low


def matrices(total, groups):
    middle = LEAF * RADIX
    top = middle * RADIX
    blocks = total // top
    per_device = blocks // groups
    c2p = child_to_parent()
    three = np.arange(3 * RADIX) - RADIX
    one = np.arange(RADIX)
    top_far = np.zeros((blocks * NODES, WIDE))
    top_far[:, : per_device * NODES] = far_weights(
        np.arange(blocks), np.arange(per_device), top, total, blocks
    )
    top_down = np.zeros((per_device, LANES, WIDE))
    for block in range(per_device):
        top_down[block, block * NODES : (block + 1) * NODES] = c2p.T
    source = np.arange(4 * LEAF)[:, None] - LEAF
    target = np.arange(2 * LEAF)[None, :]
    near = sign(target - source) * cotangent(target - source + 0.5, total)
    near = np.where(np.abs(target // LEAF - source // LEAF) <= 1, near, 0.0)
    child_out = np.zeros((LANES // NODES, NODES, 2, LEAF))
    for child in range(LANES // NODES):
        child_out[child, :, child % 2] = local_to_point()
    weave = np.zeros((2, LEAF, 2 * LEAF))
    for side in range(2):
        weave[side, np.arange(LEAF), 2 * np.arange(LEAF) + side] = 1.0
    parts = dict(
        p2m=np.tile(point_to_moment(), (1, RADIX)),
        up=np.tile(c2p, (1, RADIX)),
        far0=far_weights(three, one, LEAF, total, 0),
        far1=far_weights(three, one, middle, total, 0),
        top=top_far,
        top_down=top_down.reshape(-1, WIDE),
        down=np.tile(c2p.T, (LANES // NODES, 1)),
        out=np.concatenate([near, child_out.reshape(LANES, WIDE)]),
        weave=weave.reshape(2 * LEAF, WIDE),
        part=weave.reshape(2 * LEAF, WIDE).T,
    )
    places, start = {}, 0
    for name, part in parts.items():
        places[name] = (start, start + part.shape[0])
        start += part.shape[0]
    return split(np.concatenate(list(parts.values()))), places


def dot16(left, right):
    return jnp.dot(left, right, preferred_element_type=F32)


def two(value):
    high = value.astype(BF16)
    return high, (value - high.astype(F32)).astype(BF16)


def dot_pieces(left, right):
    rows = left[0].shape[0]
    both = dot16(jnp.concatenate(left, axis=0), right[0])
    return both[rows:] + dot16(left[0], right[1]) + both[:rows]


def dot_exact(left, right):
    rows = left.shape[0]
    high, low = two(left)
    rest = (left - high.astype(F32) - low.astype(F32)).astype(BF16)
    pieces = dot16(jnp.concatenate([rest, low, high], axis=0), right)
    return pieces[:rows] + pieces[rows : 2 * rows] + pieces[2 * rows :]


def spread(local, span):
    group = lax.broadcasted_iota(jnp.int32, (8, LANES), 1) // span
    half = LANES // span
    tiles = []
    for child in range(WIDE // span):
        tile = local[:, (child // half) * LANES : (child // half + 1) * LANES]
        tiles.append(jnp.where(group == child % half, tile, 0.0))
    return tiles


def gather_children(copies):
    group = lax.broadcasted_iota(jnp.int32, (8, WIDE), 1) // NODES
    total = jnp.zeros((8, WIDE), F32)
    for child in range(RADIX):
        total = jnp.where(group == child, copies[8 * child : 8 * child + 8], total)
    return total


def column_sums(tiles):
    row = lax.broadcasted_iota(jnp.int32, (8, LANES), 0)
    for shift in (1, 2, 4):
        first = (row // shift) % 2 == 0
        tiles = [
            jnp.where(first, a, b) + pltpu.roll(jnp.where(first, b, a), shift, 0)
            for a, b in zip(tiles[0::2], tiles[1::2])
        ]
    return tiles[0]


def invert(value):
    return pl.reciprocal(value, approx=True)


def challenge_tile(challenge_ref):
    row = lax.broadcasted_iota(jnp.int32, (8, LANES), 0)
    tile = jnp.zeros((8, LANES), F32)
    for column in range(8):
        tile = jnp.where(row == column, challenge_ref[column], tile)
    return tile


def aligned(start, size):
    return pl.ds(pl.multiple_of(start, size), size)


def row_peer(me, step):
    across = lax.rem(me // 8 + lax.rem(lax.shift_right_logical(FAR_FIRST, 2 * (step // 8)), 4), 4)
    along = lax.rem(me // 2 + lax.rem(lax.shift_right_logical(FAR_FIRST, 2 * lax.rem(step // 2, 4)), 4), 4)
    core = lax.rem(me + 1 + step, 2)
    return 8 * across + 2 * along + core


def greet(axes):
    barrier = pltpu.get_barrier_semaphore()
    for axis, size in axes:
        me = lax.axis_index(axis)

        @pl.loop(1, size)
        def _(step):
            peer = lax.rem(me + step, size)
            pl.semaphore_signal(barrier, inc=1, device_id={axis: peer}, device_id_type=MESH)

    return barrier


def main_kernel(
    groups, parts, places, batch, challenge_ref, x_hbm, multiplicity_hbm, index_hbm, high_hbm, low_hbm,
    coset_hbm, own_hbm, carry_hbm,
    x_ref, multiplicity_ref, index_ref, high_ref, low_ref, coset_ref, moments_ref, local_ref, own_ref, table_ref,
    partial_ref, gathered_ref, edge_send, edge_recv, pieces_ref, note_ref, notes_ref, entry_ref,
    x_sem, load_sem, table_sem, store_sem, own_sem, send_sem, recv_sem, edge_send_sem, edge_recv_sem,
    piece_send, piece_recv, note_send, note_recv, entry_send, entry_recv,
):
    me = lax.axis_index("rows")
    part = lax.axis_index("cols")
    rows = x_hbm.shape[1]
    leaves = rows // LEAF
    parents = leaves // RADIX
    tops = parents // RADIX
    span = LEAF * RADIX
    quarter_rows = rows // parts
    inner = pl.ds(LEAF, rows)

    def weights(name, first=0, last=None):
        start, stop = places[name]
        at = slice(start + first, stop if last is None else start + last)
        return high_ref[at, :], low_ref[at, :]

    early = places["up"][1]
    late = high_ref.shape[0] - early
    load_x = pltpu.make_async_copy(x_hbm, x_ref.at[:, inner], x_sem)
    loads = []
    for k, at in enumerate((pl.ds(0, early), pl.ds(early, late))):
        loads.append(
            [
                pltpu.make_async_copy(high_hbm.at[at], high_ref.at[at], load_sem.at[2 * k]),
                pltpu.make_async_copy(low_hbm.at[at], low_ref.at[at], load_sem.at[2 * k + 1]),
            ]
        )

    def table_loads(k):
        at = aligned(k * 2 * quarter_rows, 2 * quarter_rows)
        return (
            pltpu.make_async_copy(multiplicity_hbm.at[:, at], multiplicity_ref.at[:, at], table_sem.at[0, k]),
            pltpu.make_async_copy(index_hbm.at[:, at], index_ref.at[:, at], table_sem.at[1, k]),
        )

    for load in loads[0]:
        load.start()
    load_x.start()
    barrier = greet((("rows", groups), ("cols", parts)))
    for load in loads[0]:
        load.wait()
    load_x.wait()
    for k in range(parts):
        for load in table_loads(k):
            load.start()
    for load in loads[1]:
        load.start()

    own_group = lax.broadcasted_iota(jnp.int32, (LEAF, WIDE), 1) // NODES
    p2m = weights("p2m")
    total = jnp.zeros((8 * parents, WIDE), F32)
    for pair in range(RADIX // 2):
        start = LEAF + 2 * LEAF * pair
        left = jnp.concatenate(
            [x_ref[:, span * p + start : span * p + start + 2 * LEAF] for p in range(parents)], axis=0
        )
        right = [
            jnp.concatenate(
                [jnp.where(own_group == 2 * pair + k, piece, jnp.zeros_like(piece)) for k in range(2)], axis=0
            )
            for piece in p2m
        ]
        total = total + dot_pieces(two(left), right)
    moments_ref[...] = total
    up = weights("up")
    copies = dot_pieces(two(total), up)
    middle = [gather_children(copies[128 * g : 128 * g + 128]) for g in range(tops)]
    high = dot_pieces(two(jnp.concatenate(middle, axis=0)), [piece[:, :LANES] for piece in up])
    group = lax.broadcasted_iota(jnp.int32, (8, LANES), 1) // NODES
    packed = high[0:8]
    for g in range(1, tops):
        packed = jnp.where(group % tops == g, high[8 * g : 8 * g + 8], packed)
    gathered_ref[me] = packed
    edge_send[0, :, 0:LEAF] = x_ref[:, rows : rows + LEAF]
    edge_send[0, :, LEAF : LEAF + WIDE] = total[8 * (parents - 1) : 8 * parents]
    edge_send[0, :, LEAF + WIDE :] = middle[tops - 1]
    edge_send[1, :, 0:LEAF] = x_ref[:, LEAF : 2 * LEAF]
    edge_send[1, :, LEAF : LEAF + WIDE] = total[0:8]
    edge_send[1, :, LEAF + WIDE :] = middle[0]

    pl.semaphore_wait(barrier, groups + parts - 2)

    def edge(k):
        peer = lax.rem(me + (1 if k == 0 else groups - 1), groups)
        return pltpu.make_async_remote_copy(
            src_ref=edge_send.at[k], dst_ref=edge_recv.at[k], send_sem=edge_send_sem.at[k],
            recv_sem=edge_recv_sem.at[k], device_id={"rows": peer}, device_id_type=MESH,
        )

    def message(step):
        return pltpu.make_async_remote_copy(
            src_ref=gathered_ref.at[me], dst_ref=gathered_ref.at[me], send_sem=send_sem, recv_sem=recv_sem,
            device_id={"rows": row_peer(me, step)}, device_id_type=MESH,
        )

    def all_peers(slots_ref, semaphore):
        there = slots_ref.at[pl.ds(0, groups - 1)]
        return pltpu.make_async_copy(there, there, semaphore)

    edge(0).start()
    edge(1).start()

    @pl.loop(0, groups - 1)
    def _(step):
        message(step).start()

    weight = challenge_tile(challenge_ref)
    table_weight = weight * (TABLE_ROWS / 8.0) ** 2
    per_part = leaves // parts // 8

    @pl.loop(0, parts)
    def _(k):
        for load in table_loads(k):
            load.wait()

        @pl.loop(0, per_part)
        def _(j):
            block = k * per_part + j
            out = aligned(8 * block, 8)
            tiles = [[], []]
            for tile in range(16):
                at = aligned((16 * block + tile) * LANES, LANES)
                value = index_ref[:, at].astype(F32) - TABLE_ROWS / 2
                tiles[tile % 2].append(multiplicity_ref[:, at].astype(F32) * invert(table_weight + value * value))
            table_ref[out, 0:LANES] = column_sums(tiles[0]) * (TABLE_ROWS / 8.0) ** 2
            table_ref[out, LANES:] = column_sums(tiles[1]) * (TABLE_ROWS / 8.0) ** 2
            terms = []
            for tile in range(8):
                value = x_ref[:, aligned((8 * block + tile + 1) * LANES, LANES)]
                terms.append(invert(weight + value * value))
            partial_ref[out, 0:LANES] = column_sums(terms)

    for load in loads[1]:
        load.wait()
    shares = dot_exact(table_ref[...], weights("part")[0])
    partial_ref[:, 0:LANES] = partial_ref[:, 0:LANES] - shares[:, 0:LANES]
    table_ref[:, LANES:] = shares[:, LANES:]

    moments = moments_ref[...]
    blank = jnp.zeros((8, WIDE), F32)
    far0 = [weights("far0", k * WIDE, k * WIDE + WIDE) for k in range(3)]
    far1 = [weights("far1", k * WIDE, k * WIDE + WIDE) for k in range(3)]
    local = dot_pieces(two(moments), far0[1])
    local = local + dot_pieces(two(jnp.concatenate([blank, moments[:-8]], axis=0)), far0[0])
    local_ref[...] = local + dot_pieces(two(jnp.concatenate([moments[8:], blank], axis=0)), far0[2])
    line = [blank] + middle + [blank]
    left = jnp.concatenate([jnp.concatenate(line[g : g + 3], axis=1) for g in range(tops)], axis=0)
    inner_local = dot_pieces(two(left), weights("far1"))

    edge(0).wait()
    edge(1).wait()
    x_ref[:, 0:LEAF] = edge_recv[0, :, 0:LEAF]
    x_ref[:, rows + LEAF :] = edge_recv[1, :, 0:LEAF]
    for k, at in ((0, slice(0, 8)), (1, slice(8 * parents - 8, 8 * parents))):
        local_ref[at, :] = local_ref[at, :] + dot_pieces(two(edge_recv[k, :, LEAF : LEAF + WIDE]), far0[2 * k])
    edges = [dot_pieces(two(edge_recv[k, :, LEAF + WIDE :]), far1[2 * k]) for k in range(2)]

    all_peers(gathered_ref, recv_sem).wait()

    per_tile = LANES // (tops * NODES)
    pieces = []
    for k in range(groups // per_tile):
        tile = gathered_ref[lax.rem(me + per_tile * k, groups)]
        for place in range(1, per_tile):
            there = gathered_ref[lax.rem(me + per_tile * k + place, groups)]
            tile = jnp.where(group // tops == place, there, tile)
        pieces.append(tile)
    top_local = dot_pieces(
        two(jnp.concatenate(pieces, axis=1)), [piece[:, :LANES] for piece in weights("top")]
    )
    top_pair = two(top_local)
    expanded = []
    for g in range(tops):
        here = dot_pieces(top_pair, weights("top_down", LANES * g, LANES * g + LANES))
        here = here + inner_local[8 * g : 8 * g + 8]
        if g == 0:
            here = here + edges[0]
        if g == tops - 1:
            here = here + edges[1]
        expanded += spread(here, NODES)
    local_ref[...] = local_ref[...] + dot_pieces(two(jnp.concatenate(expanded, axis=0)), weights("down"))

    half_leaves = leaves // parts // 2
    half_rows = quarter_rows // 2
    before_me = lax.rem(part + parts - 1, parts)
    after_me = lax.rem(part + 1, parts)

    def half_at(quarter, half):
        return aligned((2 * quarter + half) * half_leaves, half_leaves)

    def ship(slot, source, peer):
        return pltpu.make_async_remote_copy(
            src_ref=partial_ref.at[source], dst_ref=pieces_ref.at[slot], send_sem=piece_send.at[slot],
            recv_sem=piece_recv.at[slot], device_id={"cols": peer}, device_id_type=MESH,
        )

    opposite = lax.rem(part + 2, parts)
    ships = (
        ship(0, half_at(opposite, 0), after_me),
        ship(1, half_at(opposite, 1), before_me),
        ship(2, half_at(after_me, 1), after_me),
        ship(3, half_at(before_me, 0), before_me),
        ship(4, half_at(after_me, 0), after_me),
        ship(5, half_at(before_me, 1), before_me),
    )

    def store(step, at):
        return pltpu.make_async_copy(coset_ref.at[:, at], coset_hbm.at[:, at], store_sem.at[step])

    @pl.loop(0, 2 * parts)
    def _(step):
        quarter = lax.rem(part + lax.rem(lax.shift_right_logical(QUARTERS, 2 * step), 4), parts)
        half = 2 * quarter + lax.rem(lax.shift_right_logical(HALVES, step), 2)

        @pl.loop(0, half_leaves // RADIX // batch)
        def _(chunk):
            first = half * (half_leaves // RADIX) + chunk * batch
            start = first * span
            count = batch * RADIX
            tiles = [x_ref[:, aligned(start + LEAF * j, LEAF)] for j in range(count + 2)]
            sources = [jnp.concatenate(tiles[k : k + count : 2], axis=0) for k in range(4)]
            expanded = []
            for p in range(batch):
                expanded += spread(local_ref[aligned(8 * (first + p), 8), :], 2 * NODES)
            sources.append(jnp.concatenate(expanded, axis=0))
            pairs = [two(source) for source in sources]
            left = [jnp.concatenate([pair[k] for pair in pairs], axis=1) for k in range(2)]
            result = dot_pieces(left, weights("out"))
            terms, total = [], jnp.zeros((8, LANES), F32)
            for j in range(count // 2):
                both = result[8 * j : 8 * j + 8]
                coset_ref[:, aligned(start + 2 * LEAF * j, 2 * LEAF)] = both
                for side in range(2):
                    value = both[:, LANES * side : LANES * side + LANES]
                    terms.append(invert(weight + value * value))
            for j in range(count // 8):
                at = aligned(first * RADIX + 8 * j, 8)
                odd = column_sums(terms[8 * j : 8 * j + 8]) - table_ref[at, LANES:]
                partial_ref[at, LANES:] = odd
                total = total + (odd + partial_ref[at, 0:LANES])
            note_ref[half] = total

        at = aligned(half * half_leaves, half_leaves)
        store(step, aligned(half * half_rows, half_rows)).start()
        for k in range(4):

            @pl.when(step == k)
            def _(k=k):
                ships[k].start()

    totals = [note_ref[2 * p] + note_ref[2 * p + 1] for p in range(parts)]
    notes_ref[me] = (totals[0] + totals[1]) + (totals[2] + totals[3])

    def note(step):
        return pltpu.make_async_remote_copy(
            src_ref=notes_ref.at[me], dst_ref=notes_ref.at[me], send_sem=note_send, recv_sem=note_recv,
            device_id={"rows": row_peer(me, step)}, device_id_type=MESH,
        )

    def entry(step):
        peer = lax.rem(part + parts - step, parts)
        return pltpu.make_async_remote_copy(
            src_ref=entry_ref.at[peer], dst_ref=carry_hbm.at[step], send_sem=entry_send.at[step],
            recv_sem=entry_recv.at[step], device_id={"cols": peer}, device_id_type=MESH,
        )

    @pl.loop(0, groups - 1)
    def _(step):
        note(step).start()

    for k in (4, 5):
        ships[k - 4].wait_recv()
        at = half_at((after_me, before_me)[k - 4], k - 4)
        partial_ref[at, :] = partial_ref[at, :] + pieces_ref[k - 4]
        ships[k].start()

    all_peers(notes_ref, note_recv).wait()
    entering = jnp.zeros((8, LANES), F32)
    for k in range(groups):
        entering = entering + jnp.where(k < me, notes_ref[k], 0.0)
    for p in range(parts):
        entry_ref[p] = entering
        entering = entering + totals[p]

    @pl.loop(1, parts)
    def _(step):
        entry(step).start()

    own_entry = pltpu.make_async_copy(entry_ref.at[part], carry_hbm.at[0], own_sem.at[1])
    own_entry.start()
    for k in range(2):
        ships[k].wait_send()
    for k in range(2, 6):
        ships[k].wait()
    for half, slots in ((0, (3, 4)), (1, (2, 5))):
        own = partial_ref[half_at(part, half), :]
        own_ref[half * half_leaves : (half + 1) * half_leaves, :] = own + pieces_ref[slots[0]] + pieces_ref[slots[1]]
    own_store = pltpu.make_async_copy(own_ref, own_hbm, own_sem.at[0])
    own_store.start()

    @pl.loop(0, 2 * parts)
    def _(step):
        store(step, aligned(step * half_rows, half_rows)).wait()

    own_store.wait()
    own_entry.wait()

    @pl.loop(1, parts)
    def _(step):
        entry(step).wait()

    all_peers(gathered_ref, send_sem).wait()
    all_peers(notes_ref, note_send).wait()


def output_kernel(
    scale, x_hbm, coset_hbm, own_hbm, carry_hbm, weave_hbm, order_hbm, lane_hbm, row_hbm, extended_hbm, fraction_hbm, running_hbm,
    x_ref, coset_ref, own_ref, carry_ref, weave_ref, order_ref, lane_ref, row_ref, extended_ref, fraction_ref, running_ref,
    load_sem, x_sem, coset_sem, out_sem, store_sem,
):
    rows = x_ref.shape[1]
    chunks = x_sem.shape[0]
    size = rows // chunks
    small = (
        (weave_hbm, weave_ref), (own_hbm, own_ref), (carry_hbm, carry_ref), (order_hbm, order_ref),
        (lane_hbm, lane_ref), (row_hbm, row_ref),
    )
    loads = [pltpu.make_async_copy(*pair, load_sem.at[k]) for k, pair in enumerate(small)]

    def rows_in(k):
        at = aligned(k * size, size)
        return (
            pltpu.make_async_copy(x_hbm.at[:, at], x_ref.at[:, at], x_sem.at[k]),
            pltpu.make_async_copy(coset_hbm.at[:, at], coset_ref.at[:, at], coset_sem.at[k]),
        )

    def rows_out(k):
        at = aligned(2 * k * size, 2 * size)
        return pltpu.make_async_copy(extended_ref.at[:, at], extended_hbm.at[:, at], out_sem.at[k])

    loads[0].start()
    for k in range(chunks):
        for load in rows_in(k):
            load.start()
    for load in loads[1:]:
        load.start()
    loads[0].wait()

    @pl.loop(0, chunks)
    def _(k):
        for load in rows_in(k):
            load.wait()
        count = size // LANES
        slices = [aligned(k * size + tile * LANES, LANES) for tile in range(count)]
        own = jnp.concatenate([x_ref[:, at] for at in slices], axis=0)
        between = jnp.concatenate([coset_ref[:, at] for at in slices], axis=0)
        high, low = two(own)
        rest = (own - high.astype(F32) - low.astype(F32)).astype(BF16)
        both = dot16(jnp.concatenate([rest, low, high, *two(between)], axis=1), weave_ref[...])
        for tile in range(count):
            extended_ref[:, aligned(2 * k * size + tile * WIDE, WIDE)] = both[8 * tile : 8 * tile + 8]
        rows_out(k).start()

    for load in loads[1:]:
        load.wait()
    own = own_ref[...]
    size_own = own.shape[0]
    fraction = dot_exact(own, order_ref[...])
    within = dot_exact(own, lane_ref[...])
    ends = jnp.broadcast_to(within[:, WIDE - 1 :], (size_own, LANES))
    high, low = two(ends)
    rest = (ends - high.astype(F32) - low.astype(F32)).astype(BF16)
    before = dot16(row_ref[...], rest) + dot16(row_ref[...], low) + dot16(row_ref[...], high)
    before = before + jnp.sum(carry_ref[...])
    for half in range(2):
        at = slice(half * LANES, (half + 1) * LANES)
        out = pl.ds(half, size_own, stride=2)
        fraction_ref[out, :] = fraction[:, at]
        running_ref[out, :] = (within[:, at] + before) * scale
    stores = [
        pltpu.make_async_copy(fraction_ref, fraction_hbm, store_sem.at[0]),
        pltpu.make_async_copy(running_ref, running_hbm, store_sem.at[1]),
    ]
    for store in stores:
        store.start()

    @pl.loop(0, chunks)
    def _(k):
        rows_out(k).wait()

    for store in stores:
        store.wait()


def local(groups, parts, trace_values, challenges, multiplicity, table_index):
    columns, rows = trace_values.shape
    total = groups * rows
    (high, low), places = matrices(total, groups)
    leaves = rows // LEAF
    parents = leaves // RADIX
    smem = pl.BlockSpec(memory_space=pltpu.SMEM)
    hbm = pl.BlockSpec(memory_space=pl.ANY)
    dma = pltpu.SemaphoreType.DMA
    size = leaves // parts
    tile = lambda *lead: pltpu.VMEM(lead + (columns, LANES), F32)
    coset, own, carry = pl.pallas_call(
        functools.partial(main_kernel, groups, parts, places, BATCH),
        out_shape=(
            jax.ShapeDtypeStruct((columns, rows), F32),
            jax.ShapeDtypeStruct((size, WIDE), F32),
            jax.ShapeDtypeStruct((parts, columns, LANES), F32),
        ),
        in_specs=[smem] + [hbm] * 5,
        out_specs=(hbm, hbm, hbm),
        scratch_shapes=[
            pltpu.VMEM((columns, rows + 2 * LEAF), F32),
            pltpu.VMEM((columns, 2 * rows), jnp.int32),
            pltpu.VMEM((columns, 2 * rows), jnp.int32),
            pltpu.VMEM(high.shape, BF16),
            pltpu.VMEM(high.shape, BF16),
            pltpu.VMEM((columns, rows), F32),
            pltpu.VMEM((columns * parents, WIDE), F32),
            pltpu.VMEM((columns * parents, WIDE), F32),
            pltpu.VMEM((size, WIDE), F32),
            pltpu.VMEM((leaves, WIDE), F32),
            pltpu.VMEM((leaves, WIDE), F32),
            tile(groups),
            pltpu.VMEM((2, columns, LEAF + 2 * WIDE), F32),
            pltpu.VMEM((2, columns, LEAF + 2 * WIDE), F32),
            pltpu.VMEM((6, size // 2, WIDE), F32),
            tile(2 * parts),
            tile(groups),
            tile(parts),
            dma, dma((4,)), dma((2, parts)), dma((2 * parts,)), dma((2,)),
            dma, dma, dma((2,)), dma((2,)),
            dma((6,)), dma((6,)), dma, dma, dma((parts,)), dma((parts,)),
        ],
        compiler_params=pltpu.CompilerParams(
            collective_id=0, has_side_effects=True, vmem_limit_bytes=56 * 2**20
        ),
        name="main",
    )(challenges, trace_values, multiplicity, table_index, high, low)
    order = high[slice(*places["weave"])]
    weave_rows = order.reshape(2, LEAF, WIDE)[np.array((0, 0, 0, 1, 1))].reshape(-1, WIDE)
    lane_sum = (order.astype(np.float32) @ np.triu(np.ones((WIDE, WIDE), np.float32))).astype(ml_dtypes.bfloat16)
    row_sum = np.tril(np.ones((size, size)), -1).astype(ml_dtypes.bfloat16)
    flat = jax.ShapeDtypeStruct((2 * size, LANES), F32)
    extended, fraction, running = pl.pallas_call(
        functools.partial(output_kernel, 1.0 / (2 * total)),
        out_shape=(jax.ShapeDtypeStruct((columns, 2 * rows), F32), flat, flat),
        in_specs=[hbm] * 8,
        out_specs=(hbm, hbm, hbm),
        scratch_shapes=[
            pltpu.VMEM((columns, rows), F32),
            pltpu.VMEM((columns, rows), F32),
            pltpu.VMEM((size, WIDE), F32),
            tile(parts),
            pltpu.VMEM((5 * LEAF, WIDE), BF16),
            pltpu.VMEM((WIDE, WIDE), BF16),
            pltpu.VMEM((WIDE, WIDE), BF16),
            pltpu.VMEM((size, size), BF16),
            pltpu.VMEM((columns, 2 * rows), F32),
            pltpu.VMEM((2 * size, LANES), F32),
            pltpu.VMEM((2 * size, LANES), F32),
            dma((6,)), dma((CHUNKS,)), dma((CHUNKS,)), dma((CHUNKS,)), dma((2,)),
        ],
        compiler_params=pltpu.CompilerParams(vmem_limit_bytes=60 * 2**20),
        name="weave",
    )(trace_values, coset, own, carry, weave_rows, order, lane_sum, row_sum)
    return extended, fraction.reshape(-1), running.reshape(-1)


def solution(mesh):
    return jax.shard_map(
        functools.partial(local, mesh.shape["rows"], mesh.shape["cols"]),
        mesh=mesh,
        in_specs=(P("cols", "rows"), P("cols"), P("cols", "rows"), P("cols", "rows")),
        out_specs=(P("cols", "rows"), P(("rows", "cols")), P(("rows", "cols"))),
        check_vma=False,
    )
```

```python
import functools
import math

import jax
import jax.numpy as jnp
import ml_dtypes
import numpy as np
from jax import lax
from jax.experimental import pallas as pl
from jax.experimental.pallas import tpu as pltpu
from jax.sharding import PartitionSpec as P

TABLE_ROWS = 8188
NODES = 16
LEAF = 128
RADIX = 16
LANES = 128
WIDE = RADIX * NODES
TABLE_BATCH = 2
TABLE_AFTER = 2
CHUNKS = 4
FAR_FIRST = 2 + 1 * 4 + 3 * 16 + 0 * 64
STEPS = ((2, 0), (2, 1), (1, 1), (3, 0), (1, 0), (3, 1), (0, 0), (0, 1))
QUARTERS = sum(quarter * 4**step for step, (quarter, _) in enumerate(STEPS))
HALVES = sum(half * 2**step for step, (_, half) in enumerate(STEPS))
MESH = pl.DeviceIdType.MESH
F32 = jnp.float32
BF16 = jnp.bfloat16


def chebyshev():
    return np.cos((2 * np.arange(NODES) + 1) * np.pi / (2 * NODES))


def lagrange(places):
    order = np.arange(1, NODES)
    waves = np.cos(order * np.arccos(np.clip(places, -1, 1))[..., None])
    at_nodes = np.cos(order * np.arccos(chebyshev())[:, None])
    return (1 + 2 * waves @ at_nodes.T) / NODES


def sign(index):
    return 1.0 - 2.0 * (index % 2)


def cotangent(offset, total):
    return 1.0 / np.tan(np.pi * offset / total) / total


def point_to_moment():
    rows = np.arange(LEAF)
    return sign(rows)[:, None] * lagrange((rows - LEAF / 2) / (LEAF / 2))


def local_to_point():
    rows = np.arange(LEAF)
    return (sign(rows)[:, None] * lagrange((rows + 0.5 - LEAF / 2) / (LEAF / 2))).T


def child_to_parent():
    child = np.arange(RADIX)[:, None]
    return lagrange((2 * child + 1 + chebyshev()[None]) / RADIX - 1).reshape(RADIX * NODES, NODES)


def far_weights(sources, targets, width, total, blocks):
    nodes = chebyshev()
    apart = (targets[None, :] - sources[:, None])[:, None, :, None]
    offset = width * apart + width / 2 * (nodes[None, None, None, :] - nodes[None, :, None, None])
    far = np.abs(apart) >= 2
    if blocks:
        far = far & (np.abs(apart) <= blocks - 2)
    far = np.broadcast_to(far, offset.shape)
    weights = np.where(far, cotangent(np.where(far, offset, 1.0), total), 0.0)
    return weights.reshape(sources.size * NODES, targets.size * NODES)


def split(matrix):
    high = matrix.astype(np.float32).astype(ml_dtypes.bfloat16)
    low = (matrix - high.astype(np.float64)).astype(np.float32).astype(ml_dtypes.bfloat16)
    return high, low


def matrices(total, groups):
    middle = LEAF * RADIX
    top = middle * RADIX
    blocks = total // top
    per_device = blocks // groups
    c2p = child_to_parent()
    three = np.arange(3 * RADIX) - RADIX
    one = np.arange(RADIX)
    top_far = np.zeros((blocks * NODES, WIDE))
    top_far[:, : per_device * NODES] = far_weights(
        np.arange(blocks), np.arange(per_device), top, total, blocks
    )
    top_down = np.zeros((per_device, LANES, WIDE))
    for block in range(per_device):
        top_down[block, block * NODES : (block + 1) * NODES] = c2p.T
    source = np.arange(4 * LEAF)[:, None] - LEAF
    target = np.arange(2 * LEAF)[None, :]
    near = sign(target - source) * cotangent(target - source + 0.5, total)
    near = np.where(np.abs(target // LEAF - source // LEAF) <= 1, near, 0.0)
    child_out = np.zeros((LANES // NODES, NODES, 2, LEAF))
    for child in range(LANES // NODES):
        child_out[child, :, child % 2] = local_to_point()
    weave = np.zeros((2, LEAF, 2 * LEAF))
    for side in range(2):
        weave[side, np.arange(LEAF), 2 * np.arange(LEAF) + side] = 1.0
    parts = dict(
        p2m=np.tile(point_to_moment(), (1, RADIX)),
        up=np.tile(c2p, (1, RADIX)),
        far0=far_weights(three, one, LEAF, total, 0),
        far1=far_weights(three, one, middle, total, 0),
        top=top_far,
        top_down=top_down.reshape(-1, WIDE),
        down=np.tile(c2p.T, (LANES // NODES, 1)),
        out=np.concatenate([near, child_out.reshape(LANES, WIDE)]),
        weave=weave.reshape(2 * LEAF, WIDE),
        part=weave.reshape(2 * LEAF, WIDE).T,
        lane=weave.reshape(2 * LEAF, WIDE) @ np.triu(np.ones((WIDE, WIDE))),
        row=np.tile(np.tril(np.ones((LANES, LANES)), -1), (1, 2)),
    )
    places, start = {}, 0
    for name, part in parts.items():
        places[name] = (start, start + part.shape[0])
        start += part.shape[0]
    high, low = split(np.concatenate(list(parts.values())))
    return (high, low[: places["weave"][0]]), places


def dot16(left, right):
    return jnp.dot(left, right, preferred_element_type=F32)


def two(value):
    high = value.astype(BF16)
    return high, (value - high.astype(F32)).astype(BF16)


def dot_pieces(left, right):
    rows = left[0].shape[0]
    both = dot16(jnp.concatenate(left, axis=0), right[0])
    return both[rows:] + dot16(left[0], right[1]) + both[:rows]


def dot_exact(left, right):
    rows = left.shape[0]
    high, low = two(left)
    rest = (left - high.astype(F32) - low.astype(F32)).astype(BF16)
    pieces = dot16(jnp.concatenate([rest, low, high], axis=0), right)
    return pieces[:rows] + pieces[rows : 2 * rows] + pieces[2 * rows :]


def spread(local, span):
    group = lax.broadcasted_iota(jnp.int32, (8, LANES), 1) // span
    half = LANES // span
    tiles = []
    for child in range(WIDE // span):
        tile = local[:, (child // half) * LANES : (child // half + 1) * LANES]
        tiles.append(jnp.where(group == child % half, tile, 0.0))
    return tiles


def gather_children(copies):
    group = lax.broadcasted_iota(jnp.int32, (8, WIDE), 1) // NODES
    total = jnp.zeros((8, WIDE), F32)
    for child in range(RADIX):
        total = jnp.where(group == child, copies[8 * child : 8 * child + 8], total)
    return total


def column_sums(tiles):
    row = lax.broadcasted_iota(jnp.int32, (8, LANES), 0)
    for shift in (1, 2, 4):
        first = (row // shift) % 2 == 0
        tiles = [
            jnp.where(first, a, b) + pltpu.roll(jnp.where(first, b, a), shift, 0)
            for a, b in zip(tiles[0::2], tiles[1::2])
        ]
    return tiles[0]


def invert(value):
    return pl.reciprocal(value, approx=True)


def challenge_tile(challenge_ref):
    row = lax.broadcasted_iota(jnp.int32, (8, LANES), 0)
    tile = jnp.zeros((8, LANES), F32)
    for column in range(8):
        tile = jnp.where(row == column, challenge_ref[column], tile)
    return tile


def aligned(start, size):
    return pl.ds(pl.multiple_of(start, size), size)


def row_peer(me, step):
    across = lax.rem(me // 8 + lax.rem(lax.shift_right_logical(FAR_FIRST, 2 * (step // 8)), 4), 4)
    along = lax.rem(me // 2 + lax.rem(lax.shift_right_logical(FAR_FIRST, 2 * lax.rem(step // 2, 4)), 4), 4)
    core = lax.rem(me + 1 + step, 2)
    return 8 * across + 2 * along + core


def greet(axes):
    barrier = pltpu.get_barrier_semaphore()
    for axis, size in axes:
        me = lax.axis_index(axis)

        @pl.loop(1, size)
        def _(step):
            peer = lax.rem(me + step, size)
            pl.semaphore_signal(barrier, inc=1, device_id={axis: peer}, device_id_type=MESH)

    return barrier


def main_kernel(
    groups, parts, scale, places, challenge_hbm, x_hbm, multiplicity_hbm, index_hbm, high_hbm, low_hbm,
    extended_out, fraction_out, running_out, carry_out,
    challenge_ref, x_ref, multiplicity_ref, index_ref, high_ref, low_ref, coset_ref, extended_ref, weave_ref, moments_ref, local_ref, fraction_ref, running_ref, table_ref,
    partial_ref, gathered_ref, edge_send, edge_recv, pieces_ref, note_ref, notes_ref, entry_ref,
    x_sem, load_sem, table_sem, store_sem, own_sem, send_sem, recv_sem, edge_send_sem, edge_recv_sem,
    piece_send, piece_recv, note_send, note_recv, entry_send, entry_recv,
):
    me = lax.axis_index("rows")
    part = lax.axis_index("cols")
    rows = x_hbm.shape[1]
    leaves = rows // LEAF
    parents = leaves // RADIX
    tops = parents // RADIX
    span = LEAF * RADIX
    quarter_rows = rows // parts

    def weights(name, first=0, last=None):
        start, stop = places[name]
        at = slice(start + first, stop if last is None else start + last)
        return high_ref[at, :], low_ref[at, :]

    def ones(name):
        return high_ref[slice(*places[name]), :]

    early = places["up"][1]
    load_x = [
        pltpu.make_async_copy(
            x_hbm.at[:, pl.ds(k * quarter_rows, quarter_rows)],
            x_ref.at[:, pl.ds(LEAF + k * quarter_rows, quarter_rows)],
            x_sem.at[k],
        )
        for k in range(parts)
    ]
    loads = []
    for k in range(2):
        pair = []
        for j, (source, target) in enumerate(((high_hbm, high_ref), (low_hbm, low_ref))):
            at = pl.ds(early, target.shape[0] - early) if k else pl.ds(0, early)
            pair.append(pltpu.make_async_copy(source.at[at], target.at[at], load_sem.at[2 * k + j]))
        loads.append(pair)
    load_challenges = pltpu.make_async_copy(challenge_hbm, challenge_ref, load_sem.at[4])

    def table_loads(k):
        at = aligned(k * 2 * quarter_rows, 2 * quarter_rows)
        return (
            pltpu.make_async_copy(multiplicity_hbm.at[:, at], multiplicity_ref.at[:, at], table_sem.at[0, k]),
            pltpu.make_async_copy(index_hbm.at[:, at], index_ref.at[:, at], table_sem.at[1, k]),
        )

    for load in loads[0]:
        load.start()
    load_challenges.start()
    for load in load_x:
        load.start()
    barrier = greet((("rows", groups), ("cols", parts)))
    for load in loads[0]:
        load.wait()
    for k in range(parts):
        load_x[k].wait()
        if k == TABLE_AFTER:
            for j in range(parts):
                for load in table_loads(j):
                    load.start()
            for load in loads[1]:
                load.start()

    own_group = lax.broadcasted_iota(jnp.int32, (LEAF, WIDE), 1) // NODES
    p2m = weights("p2m")
    total = jnp.zeros((8 * parents, WIDE), F32)
    for pair in range(RADIX // 2):
        start = LEAF + 2 * LEAF * pair
        left = jnp.concatenate(
            [x_ref[:, span * p + start : span * p + start + 2 * LEAF] for p in range(parents)], axis=0
        )
        right = [
            jnp.concatenate(
                [jnp.where(own_group == 2 * pair + k, piece, jnp.zeros_like(piece)) for k in range(2)], axis=0
            )
            for piece in p2m
        ]
        total = total + dot_pieces(two(left), right)
    moments_ref[...] = total
    up = weights("up")
    copies = dot_pieces(two(total), up)
    middle = [gather_children(copies[128 * g : 128 * g + 128]) for g in range(tops)]
    high = dot_pieces(two(jnp.concatenate(middle, axis=0)), [piece[:, :LANES] for piece in up])
    group = lax.broadcasted_iota(jnp.int32, (8, LANES), 1) // NODES
    packed = high[0:8]
    for g in range(1, tops):
        packed = jnp.where(group % tops == g, high[8 * g : 8 * g + 8], packed)
    gathered_ref[me] = packed
    edge_send[0, :, 0:LEAF] = x_ref[:, rows : rows + LEAF]
    edge_send[0, :, LEAF : LEAF + WIDE] = total[8 * (parents - 1) : 8 * parents]
    edge_send[0, :, LEAF + WIDE :] = middle[tops - 1]
    edge_send[1, :, 0:LEAF] = x_ref[:, LEAF : 2 * LEAF]
    edge_send[1, :, LEAF : LEAF + WIDE] = total[0:8]
    edge_send[1, :, LEAF + WIDE :] = middle[0]

    pl.semaphore_wait(barrier, groups + parts - 2)

    def edge(k):
        peer = lax.rem(me + (1 if k == 0 else groups - 1), groups)
        return pltpu.make_async_remote_copy(
            src_ref=edge_send.at[k], dst_ref=edge_recv.at[k], send_sem=edge_send_sem.at[k],
            recv_sem=edge_recv_sem.at[k], device_id={"rows": peer}, device_id_type=MESH,
        )

    def message(step):
        return pltpu.make_async_remote_copy(
            src_ref=gathered_ref.at[me], dst_ref=gathered_ref.at[me], send_sem=send_sem, recv_sem=recv_sem,
            device_id={"rows": row_peer(me, step)}, device_id_type=MESH,
        )

    def all_peers(slots_ref, semaphore):
        there = slots_ref.at[pl.ds(0, groups - 1)]
        return pltpu.make_async_copy(there, there, semaphore)

    edge(0).start()
    edge(1).start()

    @pl.loop(0, groups - 1)
    def _(step):
        message(step).start()

    load_challenges.wait()
    weight = challenge_tile(challenge_ref)
    table_weight = weight * (TABLE_ROWS / 8.0) ** 2
    per_part = leaves // parts // 8

    def table_block(block):
        out = aligned(8 * block, 8)
        tiles = [[], []]
        for tile in range(16):
            at = aligned((16 * block + tile) * LANES, LANES)
            value = index_ref[:, at].astype(F32) - TABLE_ROWS / 2
            tiles[tile % 2].append(multiplicity_ref[:, at].astype(F32) * invert(table_weight + value * value))
        table_ref[out, 0:LANES] = column_sums(tiles[0]) * (TABLE_ROWS / 8.0) ** 2
        table_ref[out, LANES:] = column_sums(tiles[1]) * (TABLE_ROWS / 8.0) ** 2
        terms = []
        for tile in range(8):
            value = x_ref[:, aligned((8 * block + tile + 1) * LANES, LANES)]
            terms.append(invert(weight + value * value))
        partial_ref[out, 0:LANES] = column_sums(terms)

    @pl.loop(0, parts)
    def _(k):
        for load in table_loads(k):
            load.wait()

        @pl.loop(0, per_part // TABLE_BATCH)
        def _(j):
            for more in range(TABLE_BATCH):
                table_block(k * per_part + j * TABLE_BATCH + more)

    for load in loads[1]:
        load.wait()
    shares = dot_exact(table_ref[...], ones("part"))
    partial_ref[:, 0:LANES] = partial_ref[:, 0:LANES] - shares[:, 0:LANES]
    table_ref[:, LANES:] = shares[:, LANES:]

    moments = moments_ref[...]
    edge(0).wait()
    edge(1).wait()
    x_ref[:, 0:LEAF] = edge_recv[0, :, 0:LEAF]
    x_ref[:, rows + LEAF :] = edge_recv[1, :, 0:LEAF]
    before = jnp.concatenate([edge_recv[0, :, LEAF : LEAF + WIDE], moments[:-8]], axis=0)
    after = jnp.concatenate([moments[8:], edge_recv[1, :, LEAF : LEAF + WIDE]], axis=0)
    left = jnp.concatenate([before, moments, after], axis=1)
    local_ref[...] = dot_pieces(two(left), weights("far0"))
    line = [edge_recv[0, :, LEAF + WIDE :]] + middle + [edge_recv[1, :, LEAF + WIDE :]]
    left = jnp.concatenate([jnp.concatenate(line[g : g + 3], axis=1) for g in range(tops)], axis=0)
    middle_local = dot_pieces(two(left), weights("far1"))
    all_peers(gathered_ref, recv_sem).wait()

    per_tile = LANES // (tops * NODES)
    pieces = []
    for k in range(groups // per_tile):
        tile = gathered_ref[lax.rem(me + per_tile * k, groups)]
        for place in range(1, per_tile):
            there = gathered_ref[lax.rem(me + per_tile * k + place, groups)]
            tile = jnp.where(group // tops == place, there, tile)
        pieces.append(tile)
    top_local = dot_pieces(
        two(jnp.concatenate(pieces, axis=1)), [piece[:, :LANES] for piece in weights("top")]
    )
    top_pair = two(top_local)
    expanded = []
    for g in range(tops):
        here = dot_pieces(top_pair, weights("top_down", LANES * g, LANES * g + LANES))
        here = here + middle_local[8 * g : 8 * g + 8]
        expanded += spread(here, NODES)
    local_ref[...] = local_ref[...] + dot_pieces(two(jnp.concatenate(expanded, axis=0)), weights("down"))

    half_leaves = leaves // parts // 2
    half_rows = quarter_rows // 2
    before_me = lax.rem(part + parts - 1, parts)
    after_me = lax.rem(part + 1, parts)

    def half_at(quarter, half):
        return aligned((2 * quarter + half) * half_leaves, half_leaves)

    def ship(slot, source, peer):
        return pltpu.make_async_remote_copy(
            src_ref=partial_ref.at[source], dst_ref=pieces_ref.at[slot], send_sem=piece_send.at[slot],
            recv_sem=piece_recv.at[slot], device_id={"cols": peer}, device_id_type=MESH,
        )

    opposite = lax.rem(part + 2, parts)
    ships = (
        ship(0, half_at(opposite, 0), after_me),
        ship(1, half_at(opposite, 1), before_me),
        ship(2, half_at(after_me, 1), after_me),
        ship(3, half_at(before_me, 0), before_me),
        ship(4, half_at(after_me, 0), after_me),
        ship(5, half_at(before_me, 1), before_me),
    )

    def half_of(step):
        quarter = lax.rem(part + lax.rem(lax.shift_right_logical(QUARTERS, 2 * step), 4), parts)
        return 2 * quarter + lax.rem(lax.shift_right_logical(HALVES, step), 2)

    def product(half):
        start = half * half_rows
        tiles = [x_ref[:, aligned(start + LEAF * j, LEAF)] for j in range(half_leaves + 2)]
        sources = [jnp.concatenate(tiles[k : k + half_leaves : 2], axis=0) for k in range(4)]
        expanded = []
        for p in range(half_leaves // RADIX):
            expanded += spread(local_ref[aligned(8 * (half * (half_leaves // RADIX) + p), 8), :], 2 * NODES)
        sources.append(jnp.concatenate(expanded, axis=0))
        pairs = [two(source) for source in sources]
        left = [jnp.concatenate([pair[k] for pair in pairs], axis=1) for k in range(2)]
        result = dot_pieces(left, weights("out"))
        for j in range(half_leaves // 2):
            coset_ref[:, aligned(start + 2 * LEAF * j, 2 * LEAF)] = result[8 * j : 8 * j + 8]

    def sums(half):
        total = jnp.zeros((8, LANES), F32)
        for j in range(half_leaves // 8):
            terms = []
            for k in range(8):
                value = coset_ref[:, aligned(half * half_rows + LEAF * (8 * j + k), LEAF)]
                terms.append(invert(weight + value * value))
            at = aligned(half * half_leaves + 8 * j, 8)
            odd = column_sums(terms) - table_ref[at, LANES:]
            partial_ref[at, LANES:] = odd
            total = total + (odd + partial_ref[at, 0:LANES])
        note_ref[half] = total

    product(half_of(0))

    @pl.loop(1, 2 * parts)
    def _(step):
        half = half_of(step - 1)
        sums(half)
        product(half_of(step))
        for k in range(4):

            @pl.when(step == k + 1)
            def _(k=k):
                ships[k].start()

    sums(half_of(2 * parts - 1))

    totals = [note_ref[2 * p] + note_ref[2 * p + 1] for p in range(parts)]
    notes_ref[me] = (totals[0] + totals[1]) + (totals[2] + totals[3])

    def note(step):
        return pltpu.make_async_remote_copy(
            src_ref=notes_ref.at[me], dst_ref=notes_ref.at[me], send_sem=note_send, recv_sem=note_recv,
            device_id={"rows": row_peer(me, step)}, device_id_type=MESH,
        )

    def entry(step):
        peer = lax.rem(part + parts - step, parts)
        return pltpu.make_async_remote_copy(
            src_ref=entry_ref.at[peer], dst_ref=carry_out.at[step], send_sem=entry_send.at[step],
            recv_sem=entry_recv.at[step], device_id={"cols": peer}, device_id_type=MESH,
        )

    @pl.loop(0, groups - 1)
    def _(step):
        note(step).start()

    for k in (4, 5):
        ships[k - 4].wait_recv()
        at = half_at((after_me, before_me)[k - 4], k - 4)
        partial_ref[at, :] = partial_ref[at, :] + pieces_ref[k - 4]
        ships[k].start()

    size = rows // CHUNKS
    weave = ones("weave")
    for k in range(5):
        weave_ref[LEAF * k : LEAF * k + LEAF, :] = weave[:LEAF] if k < 3 else weave[LEAF:]

    def hand_over(k):
        at = aligned(2 * k * size, 2 * size)
        return pltpu.make_async_copy(extended_ref.at[:, at], extended_out.at[:, at], store_sem.at[k])

    @pl.loop(0, CHUNKS)
    def _(k):
        count = size // LANES
        trace = [x_ref[:, aligned(LEAF + k * size + tile * LANES, LANES)] for tile in range(count)]
        trace = jnp.concatenate(trace, axis=0)
        between = [coset_ref[:, aligned(k * size + tile * LANES, LANES)] for tile in range(count)]
        between = jnp.concatenate(between, axis=0)
        high, low = two(trace)
        rest = (trace - high.astype(F32) - low.astype(F32)).astype(BF16)
        both = dot16(jnp.concatenate([rest, low, high, *two(between)], axis=1), weave_ref[...])
        for tile in range(count):
            extended_ref[:, aligned(2 * k * size + tile * WIDE, WIDE)] = both[8 * tile : 8 * tile + 8]
        hand_over(k).start()

    all_peers(notes_ref, note_recv).wait()
    entering = jnp.zeros((8, LANES), F32)
    for k in range(groups):
        entering = entering + jnp.where(k < me, notes_ref[k], 0.0)
    for p in range(parts):
        entry_ref[p] = entering
        entering = entering + totals[p]

    @pl.loop(1, parts)
    def _(step):
        entry(step).start()

    own_entry = pltpu.make_async_copy(entry_ref.at[part], carry_out.at[0], own_sem.at[1])
    own_entry.start()
    for k in range(2):
        ships[k].wait_send()
    for k in range(2, 6):
        ships[k].wait()
    own = []
    for half, slots in ((0, (3, 4)), (1, (2, 5))):
        own.append(partial_ref[half_at(part, half), :] + pieces_ref[slots[0]] + pieces_ref[slots[1]])
    own = jnp.concatenate(own, axis=0)
    own_rows = own.shape[0]
    fraction = dot_exact(own, ones("weave"))
    within = dot_exact(own, ones("lane"))
    ends = jnp.broadcast_to(within[:, WIDE - 1 :], (own_rows, LANES))
    high, low = two(ends)
    rest = (ends - high.astype(F32) - low.astype(F32)).astype(BF16)
    earlier = ones("row")[:, :LANES]
    before = dot16(earlier, rest) + dot16(earlier, low) + dot16(earlier, high)
    for half in range(2):
        at = slice(half * LANES, (half + 1) * LANES)
        out = pl.ds(half, own_rows, stride=2)
        fraction_ref[out, :] = fraction[:, at]
        running_ref[out, :] = (within[:, at] + before) * scale
    own_stores = [
        pltpu.make_async_copy(fraction_ref, fraction_out, own_sem.at[0]),
        pltpu.make_async_copy(running_ref, running_out, own_sem.at[2]),
    ]
    for store in own_stores:
        store.start()

    @pl.loop(0, CHUNKS)
    def _(k):
        hand_over(k).wait()

    for store in own_stores:
        store.wait()
    own_entry.wait()

    @pl.loop(1, parts)
    def _(step):
        entry(step).wait()

    all_peers(gathered_ref, send_sem).wait()
    all_peers(notes_ref, note_send).wait()


def output_kernel(
    scale, extended_in, fraction_in, running_in, carry_ref, extended_hbm, fraction_hbm, running_ref, store_sem
):
    size = extended_in.shape[1] // CHUNKS

    def store(k):
        at = pl.ds(k * size, size)
        return pltpu.make_async_copy(extended_in.at[:, at], extended_hbm.at[:, at], store_sem.at[k])

    for k in range(CHUNKS):
        store(k).start()
    store_fraction = pltpu.make_async_copy(fraction_in, fraction_hbm, store_sem.at[CHUNKS])
    store_fraction.start()
    running_ref[...] = running_in[...] + jnp.sum(carry_ref[...]) * scale
    for k in range(CHUNKS):
        store(k).wait()
    store_fraction.wait()


def local(groups, parts, trace_values, challenges, multiplicity, table_index):
    columns, rows = trace_values.shape
    total = groups * rows
    (high, low), places = matrices(total, groups)
    scale = 1.0 / (2 * total)
    leaves = rows // LEAF
    parents = leaves // RADIX
    vmem = pl.BlockSpec(memory_space=pltpu.VMEM)
    hbm = pl.BlockSpec(memory_space=pl.ANY)
    dma = pltpu.SemaphoreType.DMA
    size = leaves // parts
    tile = lambda *lead: pltpu.VMEM(lead + (columns, LANES), F32)
    sources = (challenges, trace_values, multiplicity, table_index, jnp.asarray(high), jnp.asarray(low))
    sources = [pltpu.with_memory_space_constraint(source, pltpu.HBM) for source in sources]
    extended, fraction, running, carry = pl.pallas_call(
        functools.partial(main_kernel, groups, parts, scale, places),
        out_shape=(
            pltpu.VMEM((columns, 2 * rows), F32),
            pltpu.VMEM((2 * size, LANES), F32),
            pltpu.VMEM((2 * size, LANES), F32),
            pltpu.VMEM((parts, columns, LANES), F32),
        ),
        in_specs=[hbm] * 6,
        out_specs=(hbm, hbm, hbm, hbm),
        scratch_shapes=[
            pltpu.SMEM((columns,), F32),
            pltpu.VMEM((columns, rows + 2 * LEAF), F32),
            pltpu.VMEM((columns, 2 * rows), jnp.int32),
            pltpu.VMEM((columns, 2 * rows), jnp.int32),
            pltpu.VMEM(high.shape, BF16),
            pltpu.VMEM(low.shape, BF16),
            pltpu.VMEM((columns, rows), F32),
            pltpu.VMEM((columns, 2 * rows), F32),
            pltpu.VMEM((5 * LEAF, WIDE), BF16),
            pltpu.VMEM((columns * parents, WIDE), F32),
            pltpu.VMEM((columns * parents, WIDE), F32),
            pltpu.VMEM((2 * size, LANES), F32),
            pltpu.VMEM((2 * size, LANES), F32),
            pltpu.VMEM((leaves, WIDE), F32),
            pltpu.VMEM((leaves, WIDE), F32),
            tile(groups),
            pltpu.VMEM((2, columns, LEAF + 2 * WIDE), F32),
            pltpu.VMEM((2, columns, LEAF + 2 * WIDE), F32),
            pltpu.VMEM((6, size // 2, WIDE), F32),
            tile(2 * parts),
            tile(groups),
            tile(parts),
            dma((parts,)), dma((5,)), dma((2, parts)), dma((CHUNKS,)), dma((3,)),
            dma, dma, dma((2,)), dma((2,)),
            dma((6,)), dma((6,)), dma, dma, dma((parts,)), dma((parts,)),
        ],
        compiler_params=pltpu.CompilerParams(
            collective_id=0, has_side_effects=True, vmem_limit_bytes=48 * 2**20
        ),
        name="main",
    )(*sources)
    flat = jax.ShapeDtypeStruct((2 * size, LANES), F32)
    extended, fraction, running = pl.pallas_call(
        functools.partial(output_kernel, scale),
        out_shape=(jax.ShapeDtypeStruct((columns, 2 * rows), F32), flat, flat),
        in_specs=[hbm, hbm, vmem, vmem],
        out_specs=(hbm, hbm, vmem),
        scratch_shapes=[dma((CHUNKS + 1,))],
        compiler_params=pltpu.CompilerParams(vmem_limit_bytes=16 * 2**20),
        name="finish",
    )(extended, fraction, running, carry)
    return extended, fraction.reshape(-1), running.reshape(-1)


def solution(mesh):
    return jax.shard_map(
        functools.partial(local, mesh.shape["rows"], mesh.shape["cols"]),
        mesh=mesh,
        in_specs=(P("cols", "rows"), P("cols"), P("cols", "rows"), P("cols", "rows")),
        out_specs=(P("cols", "rows"), P(("rows", "cols")), P(("rows", "cols"))),
        check_vma=False,
    )
```

```python
import functools
import math

import jax
import jax.numpy as jnp
import ml_dtypes
import numpy as np
from jax import lax
from jax.experimental import pallas as pl
from jax.experimental.pallas import tpu as pltpu
from jax.sharding import PartitionSpec as P

TABLE_ROWS = 8188
NODES = 16
LEAF = 128
RADIX = 16
LANES = 128
WIDE = RADIX * NODES
TABLE_BATCH = 2
TABLE_AFTER = 2
CHUNKS = 4

QUARTERS = 2 + 1 * 4 + 3 * 16 + 0 * 64
MESH = pl.DeviceIdType.MESH
F32 = jnp.float32
BF16 = jnp.bfloat16


def chebyshev():
    return np.cos((2 * np.arange(NODES) + 1) * np.pi / (2 * NODES))


def lagrange(places):
    order = np.arange(1, NODES)
    waves = np.cos(order * np.arccos(np.clip(places, -1, 1))[..., None])
    at_nodes = np.cos(order * np.arccos(chebyshev())[:, None])
    return (1 + 2 * waves @ at_nodes.T) / NODES


def sign(index):
    return 1.0 - 2.0 * (index % 2)


def cotangent(offset, total):
    return 1.0 / np.tan(np.pi * offset / total) / total


def point_to_moment():
    rows = np.arange(LEAF)
    return sign(rows)[:, None] * lagrange((rows - LEAF / 2) / (LEAF / 2))


def local_to_point():
    rows = np.arange(LEAF)
    return (sign(rows)[:, None] * lagrange((rows + 0.5 - LEAF / 2) / (LEAF / 2))).T


def child_to_parent():
    child = np.arange(RADIX)[:, None]
    return lagrange((2 * child + 1 + chebyshev()[None]) / RADIX - 1).reshape(RADIX * NODES, NODES)


def far_weights(sources, targets, width, total, blocks):
    nodes = chebyshev()
    apart = (targets[None, :] - sources[:, None])[:, None, :, None]
    offset = width * apart + width / 2 * (nodes[None, None, None, :] - nodes[None, :, None, None])
    far = np.abs(apart) >= 2
    if blocks:
        far = far & (np.abs(apart) <= blocks - 2)
    far = np.broadcast_to(far, offset.shape)
    weights = np.where(far, cotangent(np.where(far, offset, 1.0), total), 0.0)
    return weights.reshape(sources.size * NODES, targets.size * NODES)


def split(matrix):
    high = matrix.astype(np.float32).astype(ml_dtypes.bfloat16)
    low = (matrix - high.astype(np.float64)).astype(np.float32).astype(ml_dtypes.bfloat16)
    return high, low


def matrices(total, groups):
    middle = LEAF * RADIX
    top = middle * RADIX
    blocks = total // top
    per_device = blocks // groups
    c2p = child_to_parent()
    three = np.arange(3 * RADIX) - RADIX
    one = np.arange(RADIX)
    here = per_device * NODES
    top_far = far_weights(np.arange(blocks), np.arange(per_device), top, total, blocks)
    top_far = top_far.reshape(-1, LANES, here).transpose(1, 0, 2).reshape(LANES, -1)
    top_down = np.zeros((per_device, LANES, WIDE))
    for block in range(per_device):
        top_down[block, block * NODES : (block + 1) * NODES] = c2p.T
    source = np.arange(4 * LEAF)[:, None] - LEAF
    target = np.arange(2 * LEAF)[None, :]
    near = sign(target - source) * cotangent(target - source + 0.5, total)
    near = np.where(np.abs(target // LEAF - source // LEAF) <= 1, near, 0.0)
    child_out = np.zeros((LANES // NODES, NODES, 2, LEAF))
    for child in range(LANES // NODES):
        child_out[child, :, child % 2] = local_to_point()
    weave = np.zeros((2, LEAF, 2 * LEAF))
    for side in range(2):
        weave[side, np.arange(LEAF), 2 * np.arange(LEAF) + side] = 1.0
    parts = dict(
        p2m=np.tile(point_to_moment(), (1, RADIX)),
        up=np.tile(c2p, (1, RADIX)),
        far0=far_weights(three, one, LEAF, total, 0),
        far1=far_weights(three, one, middle, total, 0),
        top=top_far,
        top_down=top_down.reshape(-1, WIDE),
        down=np.tile(c2p.T, (LANES // NODES, 1)),
        out=np.concatenate([near, child_out.reshape(LANES, WIDE)]),
        weave=weave.reshape(2 * LEAF, WIDE),
        part=weave.reshape(2 * LEAF, WIDE).T,
        lane=weave.reshape(2 * LEAF, WIDE) @ np.triu(np.ones((WIDE, WIDE))),
        row=np.tile(np.tril(np.ones((LANES, LANES)), -1), (1, 2)),
    )
    places, start = {}, 0
    for name, part in parts.items():
        places[name] = (start, start + part.shape[0])
        start += part.shape[0]
    high, low = split(np.concatenate(list(parts.values())))
    return (high, low[: places["weave"][0]]), places


def dot16(left, right):
    return jnp.dot(left, right, preferred_element_type=F32)


def two(value):
    high = value.astype(BF16)
    return high, (value - high.astype(F32)).astype(BF16)


def dot_pieces(left, right):
    rows = left[0].shape[0]
    both = dot16(jnp.concatenate(left, axis=0), right[0])
    return both[rows:] + dot16(left[0], right[1]) + both[:rows]


def dot_exact(left, right):
    rows = left.shape[0]
    high, low = two(left)
    rest = (left - high.astype(F32) - low.astype(F32)).astype(BF16)
    pieces = dot16(jnp.concatenate([rest, low, high], axis=0), right)
    return pieces[:rows] + pieces[rows : 2 * rows] + pieces[2 * rows :]


def spread(local, span):
    group = lax.broadcasted_iota(jnp.int32, (8, LANES), 1) // span
    half = LANES // span
    tiles = []
    for child in range(WIDE // span):
        tile = local[:, (child // half) * LANES : (child // half + 1) * LANES]
        tiles.append(jnp.where(group == child % half, tile, 0.0))
    return tiles


def gather_children(copies):
    group = lax.broadcasted_iota(jnp.int32, (8, WIDE), 1) // NODES
    total = jnp.zeros((8, WIDE), F32)
    for child in range(RADIX):
        total = jnp.where(group == child, copies[8 * child : 8 * child + 8], total)
    return total


def column_sums(tiles):
    row = lax.broadcasted_iota(jnp.int32, (8, LANES), 0)
    for shift in (1, 2, 4):
        first = (row // shift) % 2 == 0
        tiles = [
            jnp.where(first, a, b) + pltpu.roll(jnp.where(first, b, a), shift, 0)
            for a, b in zip(tiles[0::2], tiles[1::2])
        ]
    return tiles[0]


def invert(value):
    return pl.reciprocal(value, approx=True)


def challenge_tile(challenge_ref):
    row = lax.broadcasted_iota(jnp.int32, (8, LANES), 0)
    tile = jnp.zeros((8, LANES), F32)
    for column in range(8):
        tile = jnp.where(row == column, challenge_ref[column], tile)
    return tile


def aligned(start, size):
    return pl.ds(pl.multiple_of(start, size), size)


def row_peer(me, step):
    far_first = (2, 1, 3, 0)
    across = lax.rem(me // 8 + far_first[step // 8], 4)
    along = lax.rem(me // 2 + far_first[step // 2 % 4], 4)
    core = lax.rem(me + 1 + step, 2)
    return 8 * across + 2 * along + core


def greet(axes):
    barrier = pltpu.get_barrier_semaphore()
    for axis, size in axes:
        me = lax.axis_index(axis)

        for step in range(1, size):
            peer = lax.rem(me + step, size)
            pl.semaphore_signal(barrier, inc=1, device_id={axis: peer}, device_id_type=MESH)

    return barrier


def main_kernel(
    groups, parts, scale, places, challenge_hbm, x_hbm, multiplicity_hbm, index_hbm, high_hbm, low_hbm,
    extended_out, fraction_out, running_out, carry_out,
    challenge_ref, x_ref, multiplicity_ref, index_ref, high_ref, low_ref, coset_ref, extended_ref, weave_ref, moments_ref, local_ref, fraction_ref, running_ref, table_ref,
    partial_ref, gathered_ref, edge_send, edge_recv, pieces_ref, note_ref, notes_ref, entry_ref,
    x_sem, load_sem, table_sem, store_sem, own_sem, send_sem, recv_sem, edge_send_sem, edge_recv_sem,
    piece_send, piece_recv, note_send, note_recv, entry_send, entry_recv,
):
    me = lax.axis_index("rows")
    part = lax.axis_index("cols")
    rows = x_hbm.shape[1]
    leaves = rows // LEAF
    parents = leaves // RADIX
    tops = parents // RADIX
    span = LEAF * RADIX
    quarter_rows = rows // parts

    def weights(name, first=0, last=None):
        start, stop = places[name]
        at = slice(start + first, stop if last is None else start + last)
        return high_ref[at, :], low_ref[at, :]

    def ones(name):
        return high_ref[slice(*places[name]), :]

    early = places["up"][1]
    load_x = [
        pltpu.make_async_copy(
            x_hbm.at[:, pl.ds(k * quarter_rows, quarter_rows)],
            x_ref.at[:, pl.ds(LEAF + k * quarter_rows, quarter_rows)],
            x_sem.at[k],
        )
        for k in range(parts)
    ]
    loads = []
    for k in range(2):
        pair = []
        for j, (source, target) in enumerate(((high_hbm, high_ref), (low_hbm, low_ref))):
            at = pl.ds(early, target.shape[0] - early) if k else pl.ds(0, early)
            pair.append(pltpu.make_async_copy(source.at[at], target.at[at], load_sem.at[2 * k + j]))
        loads.append(pair)
    load_challenges = pltpu.make_async_copy(challenge_hbm, challenge_ref, load_sem.at[4])

    def table_loads(k):
        at = aligned(k * 2 * quarter_rows, 2 * quarter_rows)
        return (
            pltpu.make_async_copy(multiplicity_hbm.at[:, at], multiplicity_ref.at[:, at], table_sem.at[0, k]),
            pltpu.make_async_copy(index_hbm.at[:, at], index_ref.at[:, at], table_sem.at[1, k]),
        )

    for load in loads[0]:
        load.start()
    load_challenges.start()
    for load in load_x:
        load.start()
    barrier = greet((("rows", groups), ("cols", parts)))
    for load in loads[0]:
        load.wait()
    for k in range(parts):
        load_x[k].wait()
        if k == TABLE_AFTER:
            for j in range(parts):
                for load in table_loads(j):
                    load.start()
            for load in loads[1]:
                load.start()

    own_group = lax.broadcasted_iota(jnp.int32, (LEAF, WIDE), 1) // NODES
    p2m = weights("p2m")
    total = jnp.zeros((8 * parents, WIDE), F32)
    for pair in range(RADIX // 2):
        start = LEAF + 2 * LEAF * pair
        left = jnp.concatenate(
            [x_ref[:, span * p + start : span * p + start + 2 * LEAF] for p in range(parents)], axis=0
        )
        right = [
            jnp.concatenate(
                [jnp.where(own_group == 2 * pair + k, piece, jnp.zeros_like(piece)) for k in range(2)], axis=0
            )
            for piece in p2m
        ]
        total = total + dot_pieces(two(left), right)
    moments_ref[...] = total
    up = weights("up")
    copies = dot_pieces(two(total), up)
    middle = [gather_children(copies[128 * g : 128 * g + 128]) for g in range(tops)]
    high = dot_pieces(two(jnp.concatenate(middle, axis=0)), [piece[:, :LANES] for piece in up])
    group = lax.broadcasted_iota(jnp.int32, (8, LANES), 1) // NODES
    packed = high[0:8]
    for g in range(1, tops):
        packed = jnp.where(group % tops == g, high[8 * g : 8 * g + 8], packed)
    gathered_ref[me] = packed
    edge_send[0, :, 0:LEAF] = x_ref[:, rows : rows + LEAF]
    edge_send[0, :, LEAF : LEAF + WIDE] = total[8 * (parents - 1) : 8 * parents]
    edge_send[0, :, LEAF + WIDE :] = middle[tops - 1]
    edge_send[1, :, 0:LEAF] = x_ref[:, LEAF : 2 * LEAF]
    edge_send[1, :, LEAF : LEAF + WIDE] = total[0:8]
    edge_send[1, :, LEAF + WIDE :] = middle[0]

    pl.semaphore_wait(barrier, groups + parts - 2)

    def edge(k):
        peer = lax.rem(me + (1 if k == 0 else groups - 1), groups)
        return pltpu.make_async_remote_copy(
            src_ref=edge_send.at[k], dst_ref=edge_recv.at[k], send_sem=edge_send_sem.at[k],
            recv_sem=edge_recv_sem.at[k], device_id={"rows": peer}, device_id_type=MESH,
        )

    def message(step):
        return pltpu.make_async_remote_copy(
            src_ref=gathered_ref.at[me], dst_ref=gathered_ref.at[me], send_sem=send_sem, recv_sem=recv_sem,
            device_id={"rows": row_peer(me, step)}, device_id_type=MESH,
        )

    def all_peers(slots_ref, semaphore):
        there = slots_ref.at[pl.ds(0, groups - 1)]
        return pltpu.make_async_copy(there, there, semaphore)

    edge(0).start()
    edge(1).start()

    for step in range(groups - 1):
        message(step).start()

    load_challenges.wait()
    weight = challenge_tile(challenge_ref)
    table_weight = weight * (TABLE_ROWS / 8.0) ** 2
    per_part = leaves // parts // 8

    def table_block(block):
        out = aligned(8 * block, 8)
        tiles = [[], []]
        for tile in range(16):
            at = aligned((16 * block + tile) * LANES, LANES)
            value = index_ref[:, at].astype(F32) - TABLE_ROWS / 2
            tiles[tile % 2].append(multiplicity_ref[:, at].astype(F32) * invert(table_weight + value * value))
        table_ref[out, 0:LANES] = column_sums(tiles[0]) * (TABLE_ROWS / 8.0) ** 2
        table_ref[out, LANES:] = column_sums(tiles[1]) * (TABLE_ROWS / 8.0) ** 2
        terms = []
        for tile in range(8):
            value = x_ref[:, aligned((8 * block + tile + 1) * LANES, LANES)]
            terms.append(invert(weight + value * value))
        partial_ref[out, 0:LANES] = column_sums(terms)

    @pl.loop(0, parts)
    def _(k):
        for load in table_loads(k):
            load.wait()

        @pl.loop(0, per_part // TABLE_BATCH)
        def _(j):
            for more in range(TABLE_BATCH):
                table_block(k * per_part + j * TABLE_BATCH + more)

    for load in loads[1]:
        load.wait()
    shares = dot_exact(table_ref[...], ones("part"))
    partial_ref[:, 0:LANES] = partial_ref[:, 0:LANES] - shares[:, 0:LANES]
    table_ref[:, LANES:] = shares[:, LANES:]

    moments = moments_ref[...]
    edge(0).wait()
    edge(1).wait()
    x_ref[:, 0:LEAF] = edge_recv[0, :, 0:LEAF]
    x_ref[:, rows + LEAF :] = edge_recv[1, :, 0:LEAF]
    before = jnp.concatenate([edge_recv[0, :, LEAF : LEAF + WIDE], moments[:-8]], axis=0)
    after = jnp.concatenate([moments[8:], edge_recv[1, :, LEAF : LEAF + WIDE]], axis=0)
    left = jnp.concatenate([before, moments, after], axis=1)
    local_ref[...] = dot_pieces(two(left), weights("far0"))
    line = [edge_recv[0, :, LEAF + WIDE :]] + middle + [edge_recv[1, :, LEAF + WIDE :]]
    left = jnp.concatenate([jnp.concatenate(line[g : g + 3], axis=1) for g in range(tops)], axis=0)
    middle_local = dot_pieces(two(left), weights("far1"))
    all_peers(gathered_ref, recv_sem).wait()

    per_tile = LANES // (tops * NODES)
    pieces = []
    for k in range(groups // per_tile):
        tile = gathered_ref[lax.rem(me + per_tile * k, groups)]
        for place in range(1, per_tile):
            there = gathered_ref[lax.rem(me + per_tile * k + place, groups)]
            tile = jnp.where(group // tops == place, there, tile)
        pieces.append(tile)
    top_local = dot_pieces(two(jnp.concatenate(pieces, axis=0)), weights("top"))
    tile_of = lax.broadcasted_iota(jnp.int32, (8, WIDE), 1) // (tops * NODES)
    picked = top_local[0:8]
    for k in range(1, len(pieces)):
        picked = jnp.where(tile_of == k, top_local[8 * k : 8 * k + 8], picked)
    picked = picked[:, :LANES] + picked[:, LANES:]
    for shift in (LANES // 2, LANES // 4):
        picked = picked + pltpu.roll(picked, shift, 1)
    top_pair = two(picked)
    expanded = []
    for g in range(tops):
        here = dot_pieces(top_pair, weights("top_down", LANES * g, LANES * g + LANES))
        here = here + middle_local[8 * g : 8 * g + 8]
        expanded += spread(here, NODES)
    local_ref[...] = local_ref[...] + dot_pieces(two(jnp.concatenate(expanded, axis=0)), weights("down"))

    half_leaves = leaves // parts // 2
    half_rows = quarter_rows // 2
    before_me = lax.rem(part + parts - 1, parts)
    after_me = lax.rem(part + 1, parts)

    def half_at(quarter, half):
        return aligned((2 * quarter + half) * half_leaves, half_leaves)

    def ship(slot, source, peer):
        return pltpu.make_async_remote_copy(
            src_ref=partial_ref.at[source], dst_ref=pieces_ref.at[slot], send_sem=piece_send.at[slot],
            recv_sem=piece_recv.at[slot], device_id={"cols": peer}, device_id_type=MESH,
        )

    opposite = lax.rem(part + 2, parts)
    ships = (
        ship(0, half_at(opposite, 0), after_me),
        ship(1, half_at(opposite, 1), before_me),
        ship(2, half_at(after_me, 1), after_me),
        ship(3, half_at(before_me, 0), before_me),
        ship(4, half_at(after_me, 0), after_me),
        ship(5, half_at(before_me, 1), before_me),
    )

    part_leaves = leaves // parts

    def quarter_of(step):
        return lax.rem(part + lax.rem(lax.shift_right_logical(QUARTERS, 2 * step), 4), parts)

    def product(quarter):
        start = quarter * quarter_rows
        tiles = [x_ref[:, aligned(start + LEAF * j, LEAF)] for j in range(part_leaves + 2)]
        sources = [jnp.concatenate(tiles[k : k + part_leaves : 2], axis=0) for k in range(4)]
        expanded = []
        for p in range(part_leaves // RADIX):
            expanded += spread(local_ref[aligned(8 * (quarter * (part_leaves // RADIX) + p), 8), :], 2 * NODES)
        sources.append(jnp.concatenate(expanded, axis=0))
        pairs = [two(source) for source in sources]
        left = [jnp.concatenate([pair[k] for pair in pairs], axis=1) for k in range(2)]
        result = dot_pieces(left, weights("out"))
        for j in range(part_leaves // 2):
            coset_ref[:, aligned(start + 2 * LEAF * j, 2 * LEAF)] = result[8 * j : 8 * j + 8]

    def sums(quarter):
        total = jnp.zeros((8, LANES), F32)
        for j in range(part_leaves // 8):
            terms = []
            for k in range(8):
                value = coset_ref[:, aligned(quarter * quarter_rows + LEAF * (8 * j + k), LEAF)]
                terms.append(invert(weight + value * value))
            at = aligned(quarter * part_leaves + 8 * j, 8)
            odd = column_sums(terms) - table_ref[at, LANES:]
            partial_ref[at, LANES:] = odd
            total = total + (odd + partial_ref[at, 0:LANES])
        note_ref[quarter] = total

    @pl.loop(0, parts)
    def _(step):
        quarter = quarter_of(step)
        product(quarter)
        sums(quarter)
        for k, ready in enumerate(((0, 1), (2,), (3,))):

            @pl.when(step == k)
            def _(ready=ready):
                for one in ready:
                    ships[one].start()

    totals = [note_ref[p] for p in range(parts)]
    notes_ref[me] = (totals[0] + totals[1]) + (totals[2] + totals[3])

    def note(step):
        return pltpu.make_async_remote_copy(
            src_ref=notes_ref.at[me], dst_ref=notes_ref.at[me], send_sem=note_send, recv_sem=note_recv,
            device_id={"rows": row_peer(me, step)}, device_id_type=MESH,
        )

    def entry(step):
        peer = lax.rem(part + parts - step, parts)
        return pltpu.make_async_remote_copy(
            src_ref=entry_ref.at[peer], dst_ref=carry_out.at[step], send_sem=entry_send.at[step],
            recv_sem=entry_recv.at[step], device_id={"cols": peer}, device_id_type=MESH,
        )

    for step in range(groups - 1):
        note(step).start()

    for k in (4, 5):
        ships[k - 4].wait_recv()
        at = half_at((after_me, before_me)[k - 4], k - 4)
        partial_ref[at, :] = partial_ref[at, :] + pieces_ref[k - 4]
        ships[k].start()

    size = rows // CHUNKS
    weave = ones("weave")
    for k in range(5):
        weave_ref[LEAF * k : LEAF * k + LEAF, :] = weave[:LEAF] if k < 3 else weave[LEAF:]

    def hand_over(k):
        at = aligned(2 * k * size, 2 * size)
        return pltpu.make_async_copy(extended_ref.at[:, at], extended_out.at[:, at], store_sem.at[k])

    @pl.loop(0, CHUNKS)
    def _(k):
        count = size // LANES
        trace = [x_ref[:, aligned(LEAF + k * size + tile * LANES, LANES)] for tile in range(count)]
        trace = jnp.concatenate(trace, axis=0)
        between = [coset_ref[:, aligned(k * size + tile * LANES, LANES)] for tile in range(count)]
        between = jnp.concatenate(between, axis=0)
        high, low = two(trace)
        rest = (trace - high.astype(F32) - low.astype(F32)).astype(BF16)
        both = dot16(jnp.concatenate([rest, low, high, *two(between)], axis=1), weave_ref[...])
        for tile in range(count):
            extended_ref[:, aligned(2 * k * size + tile * WIDE, WIDE)] = both[8 * tile : 8 * tile + 8]
        hand_over(k).start()

    all_peers(notes_ref, note_recv).wait()
    entering = jnp.zeros((8, LANES), F32)
    for k in range(groups):
        entering = entering + jnp.where(k < me, notes_ref[k], 0.0)
    for p in range(parts):
        entry_ref[p] = entering
        entering = entering + totals[p]

    for step in (2, 1, 3):
        entry(step).start()

    own_entry = pltpu.make_async_copy(entry_ref.at[part], carry_out.at[0], own_sem.at[1])
    own_entry.start()
    for k in range(2):
        ships[k].wait_send()
    for k in range(2, 6):
        ships[k].wait()
    own = []
    for half, slots in ((0, (3, 4)), (1, (2, 5))):
        own.append(partial_ref[half_at(part, half), :] + pieces_ref[slots[0]] + pieces_ref[slots[1]])
    own = jnp.concatenate(own, axis=0)
    own_rows = own.shape[0]
    fraction = dot_exact(own, ones("weave"))
    within = dot_exact(own, ones("lane"))
    ends = jnp.broadcast_to(within[:, WIDE - 1 :], (own_rows, LANES))
    high, low = two(ends)
    rest = (ends - high.astype(F32) - low.astype(F32)).astype(BF16)
    earlier = ones("row")[:, :LANES]
    before = dot16(earlier, rest) + dot16(earlier, low) + dot16(earlier, high)
    for half in range(2):
        at = slice(half * LANES, (half + 1) * LANES)
        out = pl.ds(half, own_rows, stride=2)
        fraction_ref[out, :] = fraction[:, at]
        running_ref[out, :] = (within[:, at] + before) * scale
    own_stores = [
        pltpu.make_async_copy(fraction_ref, fraction_out, own_sem.at[0]),
        pltpu.make_async_copy(running_ref, running_out, own_sem.at[2]),
    ]
    for store in own_stores:
        store.start()

    @pl.loop(0, CHUNKS)
    def _(k):
        hand_over(k).wait()

    for store in own_stores:
        store.wait()
    own_entry.wait()

    for step in range(1, parts):
        entry(step).wait()

    all_peers(gathered_ref, send_sem).wait()
    all_peers(notes_ref, note_send).wait()


def output_kernel(
    scale, extended_in, fraction_in, running_in, carry_ref, extended_hbm, fraction_hbm, running_ref, store_sem
):
    size = extended_in.shape[1] // CHUNKS

    def store(k):
        at = pl.ds(k * size, size)
        return pltpu.make_async_copy(extended_in.at[:, at], extended_hbm.at[:, at], store_sem.at[k])

    for k in range(CHUNKS):
        store(k).start()
    store_fraction = pltpu.make_async_copy(fraction_in, fraction_hbm, store_sem.at[CHUNKS])
    store_fraction.start()
    running_ref[...] = running_in[...] + jnp.sum(carry_ref[...]) * scale
    for k in range(CHUNKS):
        store(k).wait()
    store_fraction.wait()


def local(groups, parts, trace_values, challenges, multiplicity, table_index):
    columns, rows = trace_values.shape
    total = groups * rows
    (high, low), places = matrices(total, groups)
    scale = 1.0 / (2 * total)
    leaves = rows // LEAF
    parents = leaves // RADIX
    vmem = pl.BlockSpec(memory_space=pltpu.VMEM)
    hbm = pl.BlockSpec(memory_space=pl.ANY)
    dma = pltpu.SemaphoreType.DMA
    size = leaves // parts
    tile = lambda *lead: pltpu.VMEM(lead + (columns, LANES), F32)
    sources = (challenges, trace_values, multiplicity, table_index, jnp.asarray(high), jnp.asarray(low))
    sources = [pltpu.with_memory_space_constraint(source, pltpu.HBM) for source in sources]
    extended, fraction, running, carry = pl.pallas_call(
        functools.partial(main_kernel, groups, parts, scale, places),
        out_shape=(
            pltpu.VMEM((columns, 2 * rows), F32),
            pltpu.VMEM((2 * size, LANES), F32),
            pltpu.VMEM((2 * size, LANES), F32),
            pltpu.VMEM((parts, columns, LANES), F32),
        ),
        in_specs=[hbm] * 6,
        out_specs=(hbm, hbm, hbm, hbm),
        scratch_shapes=[
            pltpu.SMEM((columns,), F32),
            pltpu.VMEM((columns, rows + 2 * LEAF), F32),
            pltpu.VMEM((columns, 2 * rows), jnp.int32),
            pltpu.VMEM((columns, 2 * rows), jnp.int32),
            pltpu.VMEM(high.shape, BF16),
            pltpu.VMEM(low.shape, BF16),
            pltpu.VMEM((columns, rows), F32),
            pltpu.VMEM((columns, 2 * rows), F32),
            pltpu.VMEM((5 * LEAF, WIDE), BF16),
            pltpu.VMEM((columns * parents, WIDE), F32),
            pltpu.VMEM((columns * parents, WIDE), F32),
            pltpu.VMEM((2 * size, LANES), F32),
            pltpu.VMEM((2 * size, LANES), F32),
            pltpu.VMEM((leaves, WIDE), F32),
            pltpu.VMEM((leaves, WIDE), F32),
            tile(groups),
            pltpu.VMEM((2, columns, LEAF + 2 * WIDE), F32),
            pltpu.VMEM((2, columns, LEAF + 2 * WIDE), F32),
            pltpu.VMEM((6, size // 2, WIDE), F32),
            tile(2 * parts),
            tile(groups),
            tile(parts),
            dma((parts,)), dma((5,)), dma((2, parts)), dma((CHUNKS,)), dma((3,)),
            dma, dma, dma((2,)), dma((2,)),
            dma((6,)), dma((6,)), dma, dma, dma((parts,)), dma((parts,)),
        ],
        compiler_params=pltpu.CompilerParams(
            collective_id=0, has_side_effects=True, vmem_limit_bytes=48 * 2**20
        ),
        name="main",
    )(*sources)
    flat = jax.ShapeDtypeStruct((2 * size, LANES), F32)
    extended, fraction, running = pl.pallas_call(
        functools.partial(output_kernel, scale),
        out_shape=(jax.ShapeDtypeStruct((columns, 2 * rows), F32), flat, flat),
        in_specs=[hbm, hbm, vmem, vmem],
        out_specs=(hbm, hbm, vmem),
        scratch_shapes=[dma((CHUNKS + 1,))],
        compiler_params=pltpu.CompilerParams(vmem_limit_bytes=16 * 2**20),
        name="finish",
    )(extended, fraction, running, carry)
    return extended, fraction.reshape(-1), running.reshape(-1)


def solution(mesh):
    return jax.shard_map(
        functools.partial(local, mesh.shape["rows"], mesh.shape["cols"]),
        mesh=mesh,
        in_specs=(P("cols", "rows"), P("cols"), P("cols", "rows"), P("cols", "rows")),
        out_specs=(P("cols", "rows"), P(("rows", "cols")), P(("rows", "cols"))),
        check_vma=False,
    )
```

```python
import functools
import math

import jax
import jax.numpy as jnp
import ml_dtypes
import numpy as np
from jax import lax
from jax.experimental import pallas as pl
from jax.experimental.pallas import tpu as pltpu
from jax.sharding import PartitionSpec as P

TABLE_ROWS = 8188
NODES = 16
LEAF = 128
RADIX = 16
LANES = 128
WIDE = RADIX * NODES
TABLE_BATCH = 2
TABLE_AFTER = 2
CHUNKS = 4

QUARTERS = 2 + 1 * 4 + 3 * 16 + 0 * 64
MESH = pl.DeviceIdType.MESH
F32 = jnp.float32
BF16 = jnp.bfloat16


def chebyshev():
    return np.cos((2 * np.arange(NODES) + 1) * np.pi / (2 * NODES))


def lagrange(places):
    order = np.arange(1, NODES)
    waves = np.cos(order * np.arccos(np.clip(places, -1, 1))[..., None])
    at_nodes = np.cos(order * np.arccos(chebyshev())[:, None])
    return (1 + 2 * waves @ at_nodes.T) / NODES


def sign(index):
    return 1.0 - 2.0 * (index % 2)


def cotangent(offset, total):
    return 1.0 / np.tan(np.pi * offset / total) / total


def point_to_moment():
    rows = np.arange(LEAF)
    return sign(rows)[:, None] * lagrange((rows - LEAF / 2) / (LEAF / 2))


def local_to_point():
    rows = np.arange(LEAF)
    return (sign(rows)[:, None] * lagrange((rows + 0.5 - LEAF / 2) / (LEAF / 2))).T


def child_to_parent():
    child = np.arange(RADIX)[:, None]
    return lagrange((2 * child + 1 + chebyshev()[None]) / RADIX - 1).reshape(RADIX * NODES, NODES)


def far_weights(sources, targets, width, total, blocks):
    nodes = chebyshev()
    apart = (targets[None, :] - sources[:, None])[:, None, :, None]
    offset = width * apart + width / 2 * (nodes[None, None, None, :] - nodes[None, :, None, None])
    far = np.abs(apart) >= 2
    if blocks:
        far = far & (np.abs(apart) <= blocks - 2)
    far = np.broadcast_to(far, offset.shape)
    weights = np.where(far, cotangent(np.where(far, offset, 1.0), total), 0.0)
    return weights.reshape(sources.size * NODES, targets.size * NODES)


def split(matrix):
    high = matrix.astype(np.float32).astype(ml_dtypes.bfloat16)
    low = (matrix - high.astype(np.float64)).astype(np.float32).astype(ml_dtypes.bfloat16)
    return high, low


def matrices(total, groups):
    middle = LEAF * RADIX
    top = middle * RADIX
    blocks = total // top
    per_device = blocks // groups
    c2p = child_to_parent()
    three = np.arange(3 * RADIX) - RADIX
    one = np.arange(RADIX)
    here = per_device * NODES
    top_far = far_weights(np.arange(blocks), np.arange(per_device), top, total, blocks)
    top_far = top_far.reshape(-1, LANES, here).transpose(1, 0, 2).reshape(LANES, -1)
    top_down = np.zeros((per_device, LANES, WIDE))
    for block in range(per_device):
        top_down[block, block * NODES : (block + 1) * NODES] = c2p.T
    source = np.arange(4 * LEAF)[:, None] - LEAF
    target = np.arange(2 * LEAF)[None, :]
    near = sign(target - source) * cotangent(target - source + 0.5, total)
    near = np.where(np.abs(target // LEAF - source // LEAF) <= 1, near, 0.0)
    child_out = np.zeros((LANES // NODES, NODES, 2, LEAF))
    for child in range(LANES // NODES):
        child_out[child, :, child % 2] = local_to_point()
    weave = np.zeros((2, LEAF, 2 * LEAF))
    for side in range(2):
        weave[side, np.arange(LEAF), 2 * np.arange(LEAF) + side] = 1.0
    parts = dict(
        p2m=np.tile(point_to_moment(), (1, RADIX)),
        up=np.tile(c2p, (1, RADIX)),
        far0=far_weights(three, one, LEAF, total, 0),
        far1=far_weights(three, one, middle, total, 0),
        top=top_far,
        top_down=top_down.reshape(-1, WIDE),
        down=np.tile(c2p.T, (LANES // NODES, 1)),
        out=np.concatenate([near, child_out.reshape(LANES, WIDE)]),
        weave=weave.reshape(2 * LEAF, WIDE),
        part=weave.reshape(2 * LEAF, WIDE).T,
        lane=weave.reshape(2 * LEAF, WIDE) @ np.triu(np.ones((WIDE, WIDE))),
        row=np.tile(np.tril(np.ones((LANES, LANES)), -1), (1, 2)),
    )
    places, start = {}, 0
    for name, part in parts.items():
        places[name] = (start, start + part.shape[0])
        start += part.shape[0]
    high, low = split(np.concatenate(list(parts.values())))
    return (high, low[: places["weave"][0]]), places


def dot16(left, right):
    return jnp.dot(left, right, preferred_element_type=F32)


def two(value):
    high = value.astype(BF16)
    return high, (value - high.astype(F32)).astype(BF16)


def dot_pieces(left, right):
    rows = left[0].shape[0]
    both = dot16(jnp.concatenate(left, axis=0), right[0])
    return both[rows:] + dot16(left[0], right[1]) + both[:rows]


def dot_exact(left, right):
    rows = left.shape[0]
    high, low = two(left)
    rest = (left - high.astype(F32) - low.astype(F32)).astype(BF16)
    pieces = dot16(jnp.concatenate([rest, low, high], axis=0), right)
    return pieces[:rows] + pieces[rows : 2 * rows] + pieces[2 * rows :]


def spread(local, span):
    group = lax.broadcasted_iota(jnp.int32, (8, LANES), 1) // span
    half = LANES // span
    tiles = []
    for child in range(WIDE // span):
        tile = local[:, (child // half) * LANES : (child // half + 1) * LANES]
        tiles.append(jnp.where(group == child % half, tile, 0.0))
    return tiles


def gather_children(copies):
    group = lax.broadcasted_iota(jnp.int32, (8, WIDE), 1) // NODES
    total = jnp.zeros((8, WIDE), F32)
    for child in range(RADIX):
        total = jnp.where(group == child, copies[8 * child : 8 * child + 8], total)
    return total


def column_sums(tiles):
    row = lax.broadcasted_iota(jnp.int32, (8, LANES), 0)
    for shift in (1, 2, 4):
        first = (row // shift) % 2 == 0
        tiles = [
            jnp.where(first, a, b) + pltpu.roll(jnp.where(first, b, a), shift, 0)
            for a, b in zip(tiles[0::2], tiles[1::2])
        ]
    return tiles[0]


def invert(value):
    return pl.reciprocal(value, approx=True)


def challenge_tile(challenge_ref):
    row = lax.broadcasted_iota(jnp.int32, (8, LANES), 0)
    tile = jnp.zeros((8, LANES), F32)
    for column in range(8):
        tile = jnp.where(row == column, challenge_ref[column], tile)
    return tile


def aligned(start, size):
    return pl.ds(pl.multiple_of(start, size), size)


def row_peer(me, step):
    far_first = (2, 1, 3, 0)
    across = lax.rem(me // 8 + far_first[step // 8], 4)
    along = lax.rem(me // 2 + far_first[step // 2 % 4], 4)
    core = lax.rem(me + 1 + step, 2)
    return 8 * across + 2 * along + core


def greet(axes):
    barrier = pltpu.get_barrier_semaphore()
    for axis, size in axes:
        me = lax.axis_index(axis)

        for step in range(1, size):
            peer = lax.rem(me + step, size)
            pl.semaphore_signal(barrier, inc=1, device_id={axis: peer}, device_id_type=MESH)

    return barrier


def main_kernel(
    groups, parts, scale, places, challenge_hbm, x_hbm, multiplicity_hbm, index_hbm, high_hbm, low_hbm,
    extended_out, fraction_out, running_out, carry_out,
    challenge_ref, x_ref, multiplicity_ref, index_ref, high_ref, low_ref, coset_ref, extended_ref, weave_ref, moments_ref, local_ref, fraction_ref, running_ref, table_ref,
    partial_ref, gathered_ref, edge_send, edge_recv, pieces_ref, note_ref, notes_ref, entry_ref,
    x_sem, load_sem, table_sem, store_sem, own_sem, send_sem, recv_sem, edge_send_sem, edge_recv_sem,
    piece_send, piece_recv, note_send, note_recv, entry_send, entry_recv,
):
    me = lax.axis_index("rows")
    part = lax.axis_index("cols")
    rows = x_hbm.shape[1]
    leaves = rows // LEAF
    parents = leaves // RADIX
    tops = parents // RADIX
    span = LEAF * RADIX
    quarter_rows = rows // parts

    def weights(name, first=0, last=None):
        start, stop = places[name]
        at = slice(start + first, stop if last is None else start + last)
        return high_ref[at, :], low_ref[at, :]

    def ones(name):
        return high_ref[slice(*places[name]), :]

    early = places["up"][1]
    load_x = [
        pltpu.make_async_copy(
            x_hbm.at[:, pl.ds(k * quarter_rows, quarter_rows)],
            x_ref.at[:, pl.ds(LEAF + k * quarter_rows, quarter_rows)],
            x_sem.at[k],
        )
        for k in range(parts)
    ]
    loads = []
    for k in range(2):
        pair = []
        for j, (source, target) in enumerate(((high_hbm, high_ref), (low_hbm, low_ref))):
            at = pl.ds(early, target.shape[0] - early) if k else pl.ds(0, early)
            pair.append(pltpu.make_async_copy(source.at[at], target.at[at], load_sem.at[2 * k + j]))
        loads.append(pair)
    load_challenges = pltpu.make_async_copy(challenge_hbm, challenge_ref, load_sem.at[4])

    def table_loads(k):
        at = aligned(k * 2 * quarter_rows, 2 * quarter_rows)
        return (
            pltpu.make_async_copy(multiplicity_hbm.at[:, at], multiplicity_ref.at[:, at], table_sem.at[0, k]),
            pltpu.make_async_copy(index_hbm.at[:, at], index_ref.at[:, at], table_sem.at[1, k]),
        )

    for load in loads[0]:
        load.start()
    load_challenges.start()
    for load in load_x:
        load.start()
    barrier = greet((("rows", groups), ("cols", parts)))
    for load in loads[0]:
        load.wait()
    for k in range(parts):
        load_x[k].wait()
        if k == TABLE_AFTER:
            for j in range(parts):
                for load in table_loads(j):
                    load.start()
            for load in loads[1]:
                load.start()

    own_group = lax.broadcasted_iota(jnp.int32, (LEAF, WIDE), 1) // NODES
    p2m = weights("p2m")
    total = jnp.zeros((8 * parents, WIDE), F32)
    for pair in range(RADIX // 2):
        start = LEAF + 2 * LEAF * pair
        left = jnp.concatenate(
            [x_ref[:, span * p + start : span * p + start + 2 * LEAF] for p in range(parents)], axis=0
        )
        right = [
            jnp.concatenate(
                [jnp.where(own_group == 2 * pair + k, piece, jnp.zeros_like(piece)) for k in range(2)], axis=0
            )
            for piece in p2m
        ]
        total = total + dot_pieces(two(left), right)
    moments_ref[...] = total
    up = weights("up")
    copies = dot_pieces(two(total), up)
    middle = [gather_children(copies[128 * g : 128 * g + 128]) for g in range(tops)]
    high = dot_pieces(two(jnp.concatenate(middle, axis=0)), [piece[:, :LANES] for piece in up])
    group = lax.broadcasted_iota(jnp.int32, (8, LANES), 1) // NODES
    packed = high[0:8]
    for g in range(1, tops):
        packed = jnp.where(group % tops == g, high[8 * g : 8 * g + 8], packed)
    gathered_ref[me] = packed
    edge_send[0, :, 0:LEAF] = x_ref[:, rows : rows + LEAF]
    edge_send[0, :, LEAF : LEAF + WIDE] = total[8 * (parents - 1) : 8 * parents]
    edge_send[0, :, LEAF + WIDE :] = middle[tops - 1]
    edge_send[1, :, 0:LEAF] = x_ref[:, LEAF : 2 * LEAF]
    edge_send[1, :, LEAF : LEAF + WIDE] = total[0:8]
    edge_send[1, :, LEAF + WIDE :] = middle[0]

    pl.semaphore_wait(barrier, groups + parts - 2)

    def edge(k):
        peer = lax.rem(me + (1 if k == 0 else groups - 1), groups)
        return pltpu.make_async_remote_copy(
            src_ref=edge_send.at[k], dst_ref=edge_recv.at[k], send_sem=edge_send_sem.at[k],
            recv_sem=edge_recv_sem.at[k], device_id={"rows": peer}, device_id_type=MESH,
        )

    def message(step):
        return pltpu.make_async_remote_copy(
            src_ref=gathered_ref.at[me], dst_ref=gathered_ref.at[me], send_sem=send_sem, recv_sem=recv_sem,
            device_id={"rows": row_peer(me, step)}, device_id_type=MESH,
        )

    def all_peers(slots_ref, semaphore):
        there = slots_ref.at[pl.ds(0, groups - 1)]
        return pltpu.make_async_copy(there, there, semaphore)

    edge(0).start()
    edge(1).start()

    for step in range(groups - 1):
        message(step).start()

    load_challenges.wait()
    weight = challenge_tile(challenge_ref)
    table_weight = weight * (TABLE_ROWS / 8.0) ** 2
    per_part = leaves // parts // 8

    def table_block(block):
        out = aligned(8 * block, 8)
        tiles = [[], []]
        for tile in range(16):
            at = aligned((16 * block + tile) * LANES, LANES)
            value = index_ref[:, at].astype(F32) - TABLE_ROWS / 2
            tiles[tile % 2].append(multiplicity_ref[:, at].astype(F32) * invert(table_weight + value * value))
        table_ref[out, 0:LANES] = column_sums(tiles[0]) * (TABLE_ROWS / 8.0) ** 2
        table_ref[out, LANES:] = column_sums(tiles[1]) * (TABLE_ROWS / 8.0) ** 2
        terms = []
        for tile in range(8):
            value = x_ref[:, aligned((8 * block + tile + 1) * LANES, LANES)]
            terms.append(invert(weight + value * value))
        partial_ref[out, 0:LANES] = column_sums(terms)

    @pl.loop(0, parts)
    def _(k):
        for load in table_loads(k):
            load.wait()

        @pl.loop(0, per_part // TABLE_BATCH)
        def _(j):
            for more in range(TABLE_BATCH):
                table_block(k * per_part + j * TABLE_BATCH + more)

    for load in loads[1]:
        load.wait()
    shares = dot_exact(table_ref[...], ones("part"))
    partial_ref[:, 0:LANES] = partial_ref[:, 0:LANES] - shares[:, 0:LANES]
    table_ref[:, LANES:] = shares[:, LANES:]

    moments = moments_ref[...]
    edge(0).wait()
    edge(1).wait()
    x_ref[:, 0:LEAF] = edge_recv[0, :, 0:LEAF]
    x_ref[:, rows + LEAF :] = edge_recv[1, :, 0:LEAF]
    before = jnp.concatenate([edge_recv[0, :, LEAF : LEAF + WIDE], moments[:-8]], axis=0)
    after = jnp.concatenate([moments[8:], edge_recv[1, :, LEAF : LEAF + WIDE]], axis=0)
    left = jnp.concatenate([before, moments, after], axis=1)
    local_ref[...] = dot_pieces(two(left), weights("far0"))
    line = [edge_recv[0, :, LEAF + WIDE :]] + middle + [edge_recv[1, :, LEAF + WIDE :]]
    left = jnp.concatenate([jnp.concatenate(line[g : g + 3], axis=1) for g in range(tops)], axis=0)
    middle_local = dot_pieces(two(left), weights("far1"))
    all_peers(gathered_ref, recv_sem).wait()

    per_tile = LANES // (tops * NODES)
    pieces = []
    for k in range(groups // per_tile):
        tile = gathered_ref[lax.rem(me + per_tile * k, groups)]
        for place in range(1, per_tile):
            there = gathered_ref[lax.rem(me + per_tile * k + place, groups)]
            tile = jnp.where(group // tops == place, there, tile)
        pieces.append(tile)
    top_local = dot_pieces(two(jnp.concatenate(pieces, axis=0)), weights("top"))
    tile_of = lax.broadcasted_iota(jnp.int32, (8, WIDE), 1) // (tops * NODES)
    picked = top_local[0:8]
    for k in range(1, len(pieces)):
        picked = jnp.where(tile_of == k, top_local[8 * k : 8 * k + 8], picked)
    picked = picked[:, :LANES] + picked[:, LANES:]
    for shift in (LANES // 2, LANES // 4):
        picked = picked + pltpu.roll(picked, shift, 1)
    top_pair = two(picked)
    expanded = []
    for g in range(tops):
        here = dot_pieces(top_pair, weights("top_down", LANES * g, LANES * g + LANES))
        here = here + middle_local[8 * g : 8 * g + 8]
        expanded += spread(here, NODES)
    local_ref[...] = local_ref[...] + dot_pieces(two(jnp.concatenate(expanded, axis=0)), weights("down"))

    half_leaves = leaves // parts // 2
    half_rows = quarter_rows // 2
    before_me = lax.rem(part + parts - 1, parts)
    after_me = lax.rem(part + 1, parts)

    def half_at(quarter, half):
        return aligned((2 * quarter + half) * half_leaves, half_leaves)

    def ship(slot, source, peer):
        return pltpu.make_async_remote_copy(
            src_ref=partial_ref.at[source], dst_ref=pieces_ref.at[slot], send_sem=piece_send.at[slot],
            recv_sem=piece_recv.at[slot], device_id={"cols": peer}, device_id_type=MESH,
        )

    opposite = lax.rem(part + 2, parts)
    ships = (
        ship(0, half_at(opposite, 0), after_me),
        ship(1, half_at(opposite, 1), before_me),
        ship(2, half_at(after_me, 1), after_me),
        ship(3, half_at(before_me, 0), before_me),
        ship(4, half_at(after_me, 0), after_me),
        ship(5, half_at(before_me, 1), before_me),
    )

    part_leaves = leaves // parts

    def quarter_of(step):
        return lax.rem(part + lax.rem(lax.shift_right_logical(QUARTERS, 2 * step), 4), parts)

    def product(quarter):
        start = quarter * quarter_rows
        tiles = [x_ref[:, aligned(start + LEAF * j, LEAF)] for j in range(part_leaves + 2)]
        sources = [jnp.concatenate(tiles[k : k + part_leaves : 2], axis=0) for k in range(4)]
        expanded = []
        for p in range(part_leaves // RADIX):
            expanded += spread(local_ref[aligned(8 * (quarter * (part_leaves // RADIX) + p), 8), :], 2 * NODES)
        sources.append(jnp.concatenate(expanded, axis=0))
        pairs = [two(source) for source in sources]
        left = [jnp.concatenate([pair[k] for pair in pairs], axis=1) for k in range(2)]
        result = dot_pieces(left, weights("out"))
        for j in range(part_leaves // 2):
            coset_ref[:, aligned(start + 2 * LEAF * j, 2 * LEAF)] = result[8 * j : 8 * j + 8]

    def sums(quarter):
        total = jnp.zeros((8, LANES), F32)
        for j in range(part_leaves // 8):
            terms = []
            for k in range(8):
                value = coset_ref[:, aligned(quarter * quarter_rows + LEAF * (8 * j + k), LEAF)]
                terms.append(invert(weight + value * value))
            at = aligned(quarter * part_leaves + 8 * j, 8)
            odd = column_sums(terms) - table_ref[at, LANES:]
            partial_ref[at, LANES:] = odd
            total = total + (odd + partial_ref[at, 0:LANES])
        note_ref[quarter] = total

    @pl.loop(0, parts)
    def _(step):
        quarter = quarter_of(step)
        product(quarter)
        sums(quarter)
        for k, ready in enumerate(((0, 1), (2,), (3,))):

            @pl.when(step == k)
            def _(ready=ready):
                for one in ready:
                    ships[one].start()

    totals = [note_ref[p] for p in range(parts)]
    notes_ref[me] = (totals[0] + totals[1]) + (totals[2] + totals[3])

    def note(step):
        return pltpu.make_async_remote_copy(
            src_ref=notes_ref.at[me], dst_ref=notes_ref.at[me], send_sem=note_send.at[step],
            recv_sem=note_recv.at[me], device_id={"rows": row_peer(me, step)}, device_id_type=MESH,
        )

    def entry(step):
        peer = lax.rem(part + parts - step, parts)
        return pltpu.make_async_remote_copy(
            src_ref=entry_ref.at[peer], dst_ref=carry_out.at[step], send_sem=entry_send.at[step],
            recv_sem=entry_recv.at[step], device_id={"cols": peer}, device_id_type=MESH,
        )

    for step in range(groups - 1):

        @pl.when(row_peer(me, step) > me)
        def _(step=step):
            note(step).start()

    for k in (4, 5):
        ships[k - 4].wait_recv()
        at = half_at((after_me, before_me)[k - 4], k - 4)
        partial_ref[at, :] = partial_ref[at, :] + pieces_ref[k - 4]
        ships[k].start()

    size = rows // CHUNKS
    weave = ones("weave")
    for k in range(5):
        weave_ref[LEAF * k : LEAF * k + LEAF, :] = weave[:LEAF] if k < 3 else weave[LEAF:]

    def hand_over(k):
        at = aligned(2 * k * size, 2 * size)
        return pltpu.make_async_copy(extended_ref.at[:, at], extended_out.at[:, at], store_sem.at[k])

    @pl.loop(0, CHUNKS)
    def _(k):
        count = size // LANES
        trace = [x_ref[:, aligned(LEAF + k * size + tile * LANES, LANES)] for tile in range(count)]
        trace = jnp.concatenate(trace, axis=0)
        between = [coset_ref[:, aligned(k * size + tile * LANES, LANES)] for tile in range(count)]
        between = jnp.concatenate(between, axis=0)
        high, low = two(trace)
        rest = (trace - high.astype(F32) - low.astype(F32)).astype(BF16)
        both = dot16(jnp.concatenate([rest, low, high, *two(between)], axis=1), weave_ref[...])
        for tile in range(count):
            extended_ref[:, aligned(2 * k * size + tile * WIDE, WIDE)] = both[8 * tile : 8 * tile + 8]
        hand_over(k).start()

    @pl.loop(0, me)
    def _(k):
        pltpu.make_async_copy(notes_ref.at[k], notes_ref.at[k], note_recv.at[k]).wait()

    entering = jnp.zeros((8, LANES), F32)
    for k in range(groups):
        entering = entering + jnp.where(k < me, notes_ref[k], 0.0)
    for p in range(parts):
        entry_ref[p] = entering
        entering = entering + totals[p]

    for step in (2, 1, 3):
        entry(step).start()

    own_entry = pltpu.make_async_copy(entry_ref.at[part], carry_out.at[0], own_sem.at[1])
    own_entry.start()
    for k in range(2):
        ships[k].wait_send()
    for k in range(2, 6):
        ships[k].wait()
    own = []
    for half, slots in ((0, (3, 4)), (1, (2, 5))):
        own.append(partial_ref[half_at(part, half), :] + pieces_ref[slots[0]] + pieces_ref[slots[1]])
    own = jnp.concatenate(own, axis=0)
    own_rows = own.shape[0]
    fraction = dot_exact(own, ones("weave"))
    within = dot_exact(own, ones("lane"))
    ends = jnp.broadcast_to(within[:, WIDE - 1 :], (own_rows, LANES))
    high, low = two(ends)
    rest = (ends - high.astype(F32) - low.astype(F32)).astype(BF16)
    earlier = ones("row")[:, :LANES]
    before = dot16(earlier, rest) + dot16(earlier, low) + dot16(earlier, high)
    for half in range(2):
        at = slice(half * LANES, (half + 1) * LANES)
        out = pl.ds(half, own_rows, stride=2)
        fraction_ref[out, :] = fraction[:, at]
        running_ref[out, :] = (within[:, at] + before) * scale
    own_stores = [
        pltpu.make_async_copy(fraction_ref, fraction_out, own_sem.at[0]),
        pltpu.make_async_copy(running_ref, running_out, own_sem.at[2]),
    ]
    for store in own_stores:
        store.start()

    @pl.loop(0, CHUNKS)
    def _(k):
        hand_over(k).wait()

    for store in own_stores:
        store.wait()
    own_entry.wait()

    for step in range(1, parts):
        entry(step).wait()

    all_peers(gathered_ref, send_sem).wait()
    for step in range(groups - 1):

        @pl.when(row_peer(me, step) > me)
        def _(step=step):
            note(step).wait_send()


def output_kernel(
    scale, extended_in, fraction_in, running_in, carry_ref, extended_hbm, fraction_hbm, running_ref, store_sem
):
    size = extended_in.shape[1] // CHUNKS

    def store(k):
        at = pl.ds(k * size, size)
        return pltpu.make_async_copy(extended_in.at[:, at], extended_hbm.at[:, at], store_sem.at[k])

    for k in range(CHUNKS):
        store(k).start()
    store_fraction = pltpu.make_async_copy(fraction_in, fraction_hbm, store_sem.at[CHUNKS])
    store_fraction.start()
    running_ref[...] = running_in[...] + jnp.sum(carry_ref[...]) * scale
    for k in range(CHUNKS):
        store(k).wait()
    store_fraction.wait()


def local(groups, parts, trace_values, challenges, multiplicity, table_index):
    columns, rows = trace_values.shape
    total = groups * rows
    (high, low), places = matrices(total, groups)
    scale = 1.0 / (2 * total)
    leaves = rows // LEAF
    parents = leaves // RADIX
    vmem = pl.BlockSpec(memory_space=pltpu.VMEM)
    hbm = pl.BlockSpec(memory_space=pl.ANY)
    dma = pltpu.SemaphoreType.DMA
    size = leaves // parts
    tile = lambda *lead: pltpu.VMEM(lead + (columns, LANES), F32)
    sources = (challenges, trace_values, multiplicity, table_index, jnp.asarray(high), jnp.asarray(low))
    sources = [pltpu.with_memory_space_constraint(source, pltpu.HBM) for source in sources]
    extended, fraction, running, carry = pl.pallas_call(
        functools.partial(main_kernel, groups, parts, scale, places),
        out_shape=(
            pltpu.VMEM((columns, 2 * rows), F32),
            pltpu.VMEM((2 * size, LANES), F32),
            pltpu.VMEM((2 * size, LANES), F32),
            pltpu.VMEM((parts, columns, LANES), F32),
        ),
        in_specs=[hbm] * 6,
        out_specs=(hbm, hbm, hbm, hbm),
        scratch_shapes=[
            pltpu.SMEM((columns,), F32),
            pltpu.VMEM((columns, rows + 2 * LEAF), F32),
            pltpu.VMEM((columns, 2 * rows), jnp.int32),
            pltpu.VMEM((columns, 2 * rows), jnp.int32),
            pltpu.VMEM(high.shape, BF16),
            pltpu.VMEM(low.shape, BF16),
            pltpu.VMEM((columns, rows), F32),
            pltpu.VMEM((columns, 2 * rows), F32),
            pltpu.VMEM((5 * LEAF, WIDE), BF16),
            pltpu.VMEM((columns * parents, WIDE), F32),
            pltpu.VMEM((columns * parents, WIDE), F32),
            pltpu.VMEM((2 * size, LANES), F32),
            pltpu.VMEM((2 * size, LANES), F32),
            pltpu.VMEM((leaves, WIDE), F32),
            pltpu.VMEM((leaves, WIDE), F32),
            tile(groups),
            pltpu.VMEM((2, columns, LEAF + 2 * WIDE), F32),
            pltpu.VMEM((2, columns, LEAF + 2 * WIDE), F32),
            pltpu.VMEM((6, size // 2, WIDE), F32),
            tile(2 * parts),
            tile(groups),
            tile(parts),
            dma((parts,)), dma((5,)), dma((2, parts)), dma((CHUNKS,)), dma((3,)),
            dma, dma, dma((2,)), dma((2,)),
            dma((6,)), dma((6,)), dma((groups,)), dma((groups,)), dma((parts,)), dma((parts,)),
        ],
        compiler_params=pltpu.CompilerParams(
            collective_id=0, has_side_effects=True, vmem_limit_bytes=48 * 2**20
        ),
        name="main",
    )(*sources)
    flat = jax.ShapeDtypeStruct((2 * size, LANES), F32)
    extended, fraction, running = pl.pallas_call(
        functools.partial(output_kernel, scale),
        out_shape=(jax.ShapeDtypeStruct((columns, 2 * rows), F32), flat, flat),
        in_specs=[hbm, hbm, vmem, vmem],
        out_specs=(hbm, hbm, vmem),
        scratch_shapes=[dma((CHUNKS + 1,))],
        compiler_params=pltpu.CompilerParams(vmem_limit_bytes=16 * 2**20),
        name="finish",
    )(extended, fraction, running, carry)
    return extended, fraction.reshape(-1), running.reshape(-1)


def solution(mesh):
    return jax.shard_map(
        functools.partial(local, mesh.shape["rows"], mesh.shape["cols"]),
        mesh=mesh,
        in_specs=(P("cols", "rows"), P("cols"), P("cols", "rows"), P("cols", "rows")),
        out_specs=(P("cols", "rows"), P(("rows", "cols")), P(("rows", "cols"))),
        check_vma=False,
    )
```

```python
import functools
import math

import jax
import jax.numpy as jnp
import ml_dtypes
import numpy as np
from jax import lax
from jax.experimental import pallas as pl
from jax.experimental.pallas import tpu as pltpu
from jax.sharding import PartitionSpec as P

TABLE_ROWS = 8188
NODES = 16
LEAF = 128
RADIX = 16
LANES = 128
WIDE = RADIX * NODES
TABLE_BATCH = 2
TABLE_AFTER = 2
CHUNKS = 4

QUARTERS = 2 + 1 * 4 + 3 * 16 + 0 * 64
MESH = pl.DeviceIdType.MESH
F32 = jnp.float32
BF16 = jnp.bfloat16


def chebyshev():
    return np.cos((2 * np.arange(NODES) + 1) * np.pi / (2 * NODES))


def lagrange(places):
    order = np.arange(1, NODES)
    waves = np.cos(order * np.arccos(np.clip(places, -1, 1))[..., None])
    at_nodes = np.cos(order * np.arccos(chebyshev())[:, None])
    return (1 + 2 * waves @ at_nodes.T) / NODES


def sign(index):
    return 1.0 - 2.0 * (index % 2)


def cotangent(offset, total):
    return 1.0 / np.tan(np.pi * offset / total) / total


def point_to_moment():
    rows = np.arange(LEAF)
    return sign(rows)[:, None] * lagrange((rows - LEAF / 2) / (LEAF / 2))


def local_to_point():
    rows = np.arange(LEAF)
    return (sign(rows)[:, None] * lagrange((rows + 0.5 - LEAF / 2) / (LEAF / 2))).T


def child_to_parent():
    child = np.arange(RADIX)[:, None]
    return lagrange((2 * child + 1 + chebyshev()[None]) / RADIX - 1).reshape(RADIX * NODES, NODES)


def far_weights(sources, targets, width, total, blocks):
    nodes = chebyshev()
    apart = (targets[None, :] - sources[:, None])[:, None, :, None]
    offset = width * apart + width / 2 * (nodes[None, None, None, :] - nodes[None, :, None, None])
    far = np.abs(apart) >= 2
    if blocks:
        far = far & (np.abs(apart) <= blocks - 2)
    far = np.broadcast_to(far, offset.shape)
    weights = np.where(far, cotangent(np.where(far, offset, 1.0), total), 0.0)
    return weights.reshape(sources.size * NODES, targets.size * NODES)


def split(matrix):
    high = matrix.astype(np.float32).astype(ml_dtypes.bfloat16)
    low = (matrix - high.astype(np.float64)).astype(np.float32).astype(ml_dtypes.bfloat16)
    return high, low


def matrices(total, groups):
    middle = LEAF * RADIX
    top = middle * RADIX
    blocks = total // top
    per_device = blocks // groups
    c2p = child_to_parent()
    three = np.arange(3 * RADIX) - RADIX
    one = np.arange(RADIX)
    here = per_device * NODES
    top_far = far_weights(np.arange(blocks), np.arange(per_device), top, total, blocks)
    top_far = top_far.reshape(-1, LANES, here).transpose(1, 0, 2).reshape(LANES, -1)
    top_down = np.zeros((per_device, LANES, WIDE))
    for block in range(per_device):
        top_down[block, block * NODES : (block + 1) * NODES] = c2p.T
    source = np.arange(4 * LEAF)[:, None] - LEAF
    target = np.arange(2 * LEAF)[None, :]
    near = sign(target - source) * cotangent(target - source + 0.5, total)
    near = np.where(np.abs(target // LEAF - source // LEAF) <= 1, near, 0.0)
    child_out = np.zeros((LANES // NODES, NODES, 2, LEAF))
    for child in range(LANES // NODES):
        child_out[child, :, child % 2] = local_to_point()
    weave = np.zeros((2, LEAF, 2 * LEAF))
    for side in range(2):
        weave[side, np.arange(LEAF), 2 * np.arange(LEAF) + side] = 1.0
    parts = dict(
        p2m=np.tile(point_to_moment(), (1, RADIX)),
        up=np.tile(c2p, (1, RADIX)),
        far0=far_weights(three, one, LEAF, total, 0),
        far1=far_weights(three, one, middle, total, 0),
        top=top_far,
        top_down=top_down.reshape(-1, WIDE),
        down=np.tile(c2p.T, (LANES // NODES, 1)),
        out=np.concatenate([near, child_out.reshape(LANES, WIDE)]),
        weave=weave.reshape(2 * LEAF, WIDE),
        part=weave.reshape(2 * LEAF, WIDE).T,
        lane=weave.reshape(2 * LEAF, WIDE) @ np.triu(np.ones((WIDE, WIDE))),
        row=np.tile(np.tril(np.ones((LANES, LANES)), -1), (1, 2)),
    )
    places, start = {}, 0
    for name, part in parts.items():
        places[name] = (start, start + part.shape[0])
        start += part.shape[0]
    high, low = split(np.concatenate(list(parts.values())))
    return (high, low[: places["weave"][0]]), places


def dot16(left, right):
    return jnp.dot(left, right, preferred_element_type=F32)


def two(value):
    high = value.astype(BF16)
    return high, (value - high.astype(F32)).astype(BF16)


def dot_pieces(left, right):
    rows = left[0].shape[0]
    both = dot16(jnp.concatenate(left, axis=0), right[0])
    return both[rows:] + dot16(left[0], right[1]) + both[:rows]


def dot_exact(left, right):
    rows = left.shape[0]
    high, low = two(left)
    rest = (left - high.astype(F32) - low.astype(F32)).astype(BF16)
    pieces = dot16(jnp.concatenate([rest, low, high], axis=0), right)
    return pieces[:rows] + pieces[rows : 2 * rows] + pieces[2 * rows :]


def spread(local, span):
    group = lax.broadcasted_iota(jnp.int32, (8, LANES), 1) // span
    half = LANES // span
    tiles = []
    for child in range(WIDE // span):
        tile = local[:, (child // half) * LANES : (child // half + 1) * LANES]
        tiles.append(jnp.where(group == child % half, tile, 0.0))
    return tiles


def gather_children(copies):
    group = lax.broadcasted_iota(jnp.int32, (8, WIDE), 1) // NODES
    total = jnp.zeros((8, WIDE), F32)
    for child in range(RADIX):
        total = jnp.where(group == child, copies[8 * child : 8 * child + 8], total)
    return total


def column_sums(tiles):
    row = lax.broadcasted_iota(jnp.int32, (8, LANES), 0)
    for shift in (1, 2, 4):
        first = (row // shift) % 2 == 0
        tiles = [
            jnp.where(first, a, b) + pltpu.roll(jnp.where(first, b, a), shift, 0)
            for a, b in zip(tiles[0::2], tiles[1::2])
        ]
    return tiles[0]


def invert(value):
    return pl.reciprocal(value, approx=True)


def challenge_tile(challenge_ref):
    row = lax.broadcasted_iota(jnp.int32, (8, LANES), 0)
    tile = jnp.zeros((8, LANES), F32)
    for column in range(8):
        tile = jnp.where(row == column, challenge_ref[column], tile)
    return tile


def aligned(start, size):
    return pl.ds(pl.multiple_of(start, size), size)


def row_peer(me, step):
    far_first = (2, 1, 3, 0)
    across = lax.rem(me // 8 + far_first[step // 8], 4)
    along = lax.rem(me // 2 + far_first[step // 2 % 4], 4)
    core = lax.rem(me + 1 + step, 2)
    return 8 * across + 2 * along + core


def greet(axes):
    barrier = pltpu.get_barrier_semaphore()
    for axis, size in axes:
        me = lax.axis_index(axis)

        for step in range(1, size):
            peer = lax.rem(me + step, size)
            pl.semaphore_signal(barrier, inc=1, device_id={axis: peer}, device_id_type=MESH)

    return barrier


def main_kernel(
    groups, parts, scale, places, challenge_hbm, x_hbm, multiplicity_hbm, index_hbm, high_hbm, low_hbm,
    extended_out, fraction_out, running_out, carry_out,
    challenge_ref, x_ref, multiplicity_ref, index_ref, high_ref, low_ref, coset_ref, extended_ref, weave_ref, moments_ref, local_ref, fraction_ref, running_ref, table_ref,
    partial_ref, gathered_ref, edge_send, edge_recv, pieces_ref, note_ref, notes_ref, entry_ref,
    x_sem, load_sem, table_sem, store_sem, own_sem, send_sem, recv_sem, edge_send_sem, edge_recv_sem,
    piece_send, piece_recv, note_send, note_recv, entry_send, entry_recv,
):
    me = lax.axis_index("rows")
    part = lax.axis_index("cols")
    rows = x_hbm.shape[1]
    leaves = rows // LEAF
    parents = leaves // RADIX
    tops = parents // RADIX
    span = LEAF * RADIX
    quarter_rows = rows // parts

    def weights(name, first=0, last=None):
        start, stop = places[name]
        at = slice(start + first, stop if last is None else start + last)
        return high_ref[at, :], low_ref[at, :]

    def ones(name):
        return high_ref[slice(*places[name]), :]

    early = places["up"][1]
    load_x = [
        pltpu.make_async_copy(
            x_hbm.at[:, pl.ds(k * quarter_rows, quarter_rows)],
            x_ref.at[:, pl.ds(LEAF + k * quarter_rows, quarter_rows)],
            x_sem.at[k],
        )
        for k in range(parts)
    ]
    loads = []
    for k in range(2):
        pair = []
        for j, (source, target) in enumerate(((high_hbm, high_ref), (low_hbm, low_ref))):
            at = pl.ds(early, target.shape[0] - early) if k else pl.ds(0, early)
            pair.append(pltpu.make_async_copy(source.at[at], target.at[at], load_sem.at[2 * k + j]))
        loads.append(pair)
    load_challenges = pltpu.make_async_copy(challenge_hbm, challenge_ref, load_sem.at[4])

    def table_loads(k):
        at = aligned(k * 2 * quarter_rows, 2 * quarter_rows)
        return (
            pltpu.make_async_copy(multiplicity_hbm.at[:, at], multiplicity_ref.at[:, at], table_sem.at[0, k]),
            pltpu.make_async_copy(index_hbm.at[:, at], index_ref.at[:, at], table_sem.at[1, k]),
        )

    for load in loads[0]:
        load.start()
    load_challenges.start()
    for load in load_x:
        load.start()
    barrier = greet((("rows", groups), ("cols", parts)))
    for load in loads[0]:
        load.wait()
    for k in range(parts):
        load_x[k].wait()
        if k == TABLE_AFTER:
            for j in range(parts):
                for load in table_loads(j):
                    load.start()
            for load in loads[1]:
                load.start()

    own_group = lax.broadcasted_iota(jnp.int32, (LEAF, WIDE), 1) // NODES
    p2m = weights("p2m")
    total = jnp.zeros((8 * parents, WIDE), F32)
    for pair in range(RADIX // 2):
        start = LEAF + 2 * LEAF * pair
        left = jnp.concatenate(
            [x_ref[:, span * p + start : span * p + start + 2 * LEAF] for p in range(parents)], axis=0
        )
        right = [
            jnp.concatenate(
                [jnp.where(own_group == 2 * pair + k, piece, jnp.zeros_like(piece)) for k in range(2)], axis=0
            )
            for piece in p2m
        ]
        total = total + dot_pieces(two(left), right)
    moments_ref[...] = total
    up = weights("up")
    copies = dot_pieces(two(total), up)
    middle = [gather_children(copies[128 * g : 128 * g + 128]) for g in range(tops)]
    high = dot_pieces(two(jnp.concatenate(middle, axis=0)), [piece[:, :LANES] for piece in up])
    group = lax.broadcasted_iota(jnp.int32, (8, LANES), 1) // NODES
    packed = high[0:8]
    for g in range(1, tops):
        packed = jnp.where(group % tops == g, high[8 * g : 8 * g + 8], packed)
    gathered_ref[me] = packed
    edge_send[0, :, 0:LEAF] = x_ref[:, rows : rows + LEAF]
    edge_send[0, :, LEAF : LEAF + WIDE] = total[8 * (parents - 1) : 8 * parents]
    edge_send[0, :, LEAF + WIDE :] = middle[tops - 1]
    edge_send[1, :, 0:LEAF] = x_ref[:, LEAF : 2 * LEAF]
    edge_send[1, :, LEAF : LEAF + WIDE] = total[0:8]
    edge_send[1, :, LEAF + WIDE :] = middle[0]

    pl.semaphore_wait(barrier, groups + parts - 2)

    def edge(k):
        peer = lax.rem(me + (1 if k == 0 else groups - 1), groups)
        return pltpu.make_async_remote_copy(
            src_ref=edge_send.at[k], dst_ref=edge_recv.at[k], send_sem=edge_send_sem.at[k],
            recv_sem=edge_recv_sem.at[k], device_id={"rows": peer}, device_id_type=MESH,
        )

    def message(step):
        return pltpu.make_async_remote_copy(
            src_ref=gathered_ref.at[me], dst_ref=gathered_ref.at[me], send_sem=send_sem, recv_sem=recv_sem,
            device_id={"rows": row_peer(me, step)}, device_id_type=MESH,
        )

    def all_peers(slots_ref, semaphore):
        there = slots_ref.at[pl.ds(0, groups - 1)]
        return pltpu.make_async_copy(there, there, semaphore)

    edge(0).start()
    edge(1).start()

    for step in range(groups - 1):
        message(step).start()

    load_challenges.wait()
    weight = challenge_tile(challenge_ref)
    table_weight = weight * (TABLE_ROWS / 8.0) ** 2
    per_part = leaves // parts // 8

    def table_block(block):
        out = aligned(8 * block, 8)
        tiles = [[], []]
        for tile in range(16):
            at = aligned((16 * block + tile) * LANES, LANES)
            value = index_ref[:, at].astype(F32) - TABLE_ROWS / 2
            tiles[tile % 2].append(multiplicity_ref[:, at].astype(F32) * invert(table_weight + value * value))
        table_ref[out, 0:LANES] = column_sums(tiles[0]) * (TABLE_ROWS / 8.0) ** 2
        table_ref[out, LANES:] = column_sums(tiles[1]) * (TABLE_ROWS / 8.0) ** 2
        terms = []
        for tile in range(8):
            value = x_ref[:, aligned((8 * block + tile + 1) * LANES, LANES)]
            terms.append(invert(weight + value * value))
        partial_ref[out, 0:LANES] = column_sums(terms)

    @pl.loop(0, parts)
    def _(k):
        for load in table_loads(k):
            load.wait()

        @pl.loop(0, per_part // TABLE_BATCH)
        def _(j):
            for more in range(TABLE_BATCH):
                table_block(k * per_part + j * TABLE_BATCH + more)

    for load in loads[1]:
        load.wait()
    shares = dot_exact(table_ref[...], ones("part"))
    partial_ref[:, 0:LANES] = partial_ref[:, 0:LANES] - shares[:, 0:LANES]
    table_ref[:, LANES:] = shares[:, LANES:]

    moments = moments_ref[...]
    edge(0).wait()
    edge(1).wait()
    x_ref[:, 0:LEAF] = edge_recv[0, :, 0:LEAF]
    x_ref[:, rows + LEAF :] = edge_recv[1, :, 0:LEAF]
    before = jnp.concatenate([edge_recv[0, :, LEAF : LEAF + WIDE], moments[:-8]], axis=0)
    after = jnp.concatenate([moments[8:], edge_recv[1, :, LEAF : LEAF + WIDE]], axis=0)
    left = jnp.concatenate([before, moments, after], axis=1)
    local_ref[...] = dot_pieces(two(left), weights("far0"))
    line = [edge_recv[0, :, LEAF + WIDE :]] + middle + [edge_recv[1, :, LEAF + WIDE :]]
    left = jnp.concatenate([jnp.concatenate(line[g : g + 3], axis=1) for g in range(tops)], axis=0)
    middle_local = dot_pieces(two(left), weights("far1"))
    all_peers(gathered_ref, recv_sem).wait()

    per_tile = LANES // (tops * NODES)
    pieces = []
    for k in range(groups // per_tile):
        tile = gathered_ref[lax.rem(me + per_tile * k, groups)]
        for place in range(1, per_tile):
            there = gathered_ref[lax.rem(me + per_tile * k + place, groups)]
            tile = jnp.where(group // tops == place, there, tile)
        pieces.append(tile)
    top_local = dot_pieces(two(jnp.concatenate(pieces, axis=0)), weights("top"))
    tile_of = lax.broadcasted_iota(jnp.int32, (8, WIDE), 1) // (tops * NODES)
    picked = top_local[0:8]
    for k in range(1, len(pieces)):
        picked = jnp.where(tile_of == k, top_local[8 * k : 8 * k + 8], picked)
    picked = picked[:, :LANES] + picked[:, LANES:]
    for shift in (LANES // 2, LANES // 4):
        picked = picked + pltpu.roll(picked, shift, 1)
    top_pair = two(picked)
    expanded = []
    for g in range(tops):
        here = dot_pieces(top_pair, weights("top_down", LANES * g, LANES * g + LANES))
        here = here + middle_local[8 * g : 8 * g + 8]
        expanded += spread(here, NODES)
    local_ref[...] = local_ref[...] + dot_pieces(two(jnp.concatenate(expanded, axis=0)), weights("down"))

    half_leaves = leaves // parts // 2
    half_rows = quarter_rows // 2
    before_me = lax.rem(part + parts - 1, parts)
    after_me = lax.rem(part + 1, parts)

    def half_at(quarter, half):
        return aligned((2 * quarter + half) * half_leaves, half_leaves)

    def ship(slot, source, peer):
        return pltpu.make_async_remote_copy(
            src_ref=partial_ref.at[source], dst_ref=pieces_ref.at[slot], send_sem=piece_send.at[slot],
            recv_sem=piece_recv.at[slot], device_id={"cols": peer}, device_id_type=MESH,
        )

    opposite = lax.rem(part + 2, parts)
    ships = (
        ship(0, half_at(opposite, 0), after_me),
        ship(1, half_at(opposite, 1), before_me),
        ship(2, half_at(after_me, 1), after_me),
        ship(3, half_at(before_me, 0), before_me),
        ship(4, half_at(after_me, 0), after_me),
        ship(5, half_at(before_me, 1), before_me),
    )

    part_leaves = leaves // parts

    def quarter_of(step):
        return lax.rem(part + lax.rem(lax.shift_right_logical(QUARTERS, 2 * step), 4), parts)

    def product(quarter):
        start = quarter * quarter_rows
        tiles = [x_ref[:, aligned(start + LEAF * j, LEAF)] for j in range(part_leaves + 2)]
        sources = [jnp.concatenate(tiles[k : k + part_leaves : 2], axis=0) for k in range(4)]
        expanded = []
        for p in range(part_leaves // RADIX):
            expanded += spread(local_ref[aligned(8 * (quarter * (part_leaves // RADIX) + p), 8), :], 2 * NODES)
        sources.append(jnp.concatenate(expanded, axis=0))
        pairs = [two(source) for source in sources]
        left = [jnp.concatenate([pair[k] for pair in pairs], axis=1) for k in range(2)]
        result = dot_pieces(left, weights("out"))
        for j in range(part_leaves // 2):
            coset_ref[:, aligned(start + 2 * LEAF * j, 2 * LEAF)] = result[8 * j : 8 * j + 8]

    def sums(quarter):
        total = jnp.zeros((8, LANES), F32)
        for j in range(part_leaves // 8):
            terms = []
            for k in range(8):
                value = coset_ref[:, aligned(quarter * quarter_rows + LEAF * (8 * j + k), LEAF)]
                terms.append(invert(weight + value * value))
            at = aligned(quarter * part_leaves + 8 * j, 8)
            odd = column_sums(terms) - table_ref[at, LANES:]
            partial_ref[at, LANES:] = odd
            total = total + (odd + partial_ref[at, 0:LANES])
        note_ref[quarter] = total

    @pl.loop(0, parts)
    def _(step):
        quarter = quarter_of(step)
        product(quarter)
        sums(quarter)
        for k, ready in enumerate(((0, 1), (2,), (3,))):

            @pl.when(step == k)
            def _(ready=ready):
                for one in ready:
                    ships[one].start()

    totals = [note_ref[p] for p in range(parts)]
    notes_ref[me] = (totals[0] + totals[1]) + (totals[2] + totals[3])

    def note(step):
        return pltpu.make_async_remote_copy(
            src_ref=notes_ref.at[me], dst_ref=notes_ref.at[me], send_sem=note_send.at[step],
            recv_sem=note_recv.at[me], device_id={"rows": row_peer(me, step)}, device_id_type=MESH,
        )

    def entry(step):
        peer = lax.rem(part + parts - step, parts)
        return pltpu.make_async_remote_copy(
            src_ref=entry_ref.at[peer], dst_ref=carry_out.at[step], send_sem=entry_send.at[step],
            recv_sem=entry_recv.at[step], device_id={"cols": peer}, device_id_type=MESH,
        )

    for step in range(groups - 1):

        @pl.when(row_peer(me, step) > me)
        def _(step=step):
            note(step).start()

    for k in (4, 5):
        ships[k - 4].wait_recv()
        at = half_at((after_me, before_me)[k - 4], k - 4)
        partial_ref[at, :] = partial_ref[at, :] + pieces_ref[k - 4]
        ships[k].start()

    size = rows // CHUNKS
    weave = ones("weave")
    for k in range(5):
        weave_ref[LEAF * k : LEAF * k + LEAF, :] = weave[:LEAF] if k < 3 else weave[LEAF:]

    def hand_over(k):
        at = aligned(2 * k * size, 2 * size)
        return pltpu.make_async_copy(extended_ref.at[:, at], extended_out.at[:, at], store_sem.at[k])

    def interleave(k):
        count = size // LANES
        trace = [x_ref[:, aligned(LEAF + k * size + tile * LANES, LANES)] for tile in range(count)]
        trace = jnp.concatenate(trace, axis=0)
        between = [coset_ref[:, aligned(k * size + tile * LANES, LANES)] for tile in range(count)]
        between = jnp.concatenate(between, axis=0)
        high, low = two(trace)
        rest = (trace - high.astype(F32) - low.astype(F32)).astype(BF16)
        both = dot16(jnp.concatenate([rest, low, high, *two(between)], axis=1), weave_ref[...])
        for tile in range(count):
            extended_ref[:, aligned(2 * k * size + tile * WIDE, WIDE)] = both[8 * tile : 8 * tile + 8]
        hand_over(k).start()

    pl.loop(0, CHUNKS // 2)(interleave)

    @pl.loop(0, me)
    def _(k):
        pltpu.make_async_copy(notes_ref.at[k], notes_ref.at[k], note_recv.at[k]).wait()

    entering = jnp.zeros((8, LANES), F32)
    for k in range(groups):
        entering = entering + jnp.where(k < me, notes_ref[k], 0.0)
    for p in range(parts):
        entry_ref[p] = entering
        entering = entering + totals[p]

    for step in (2, 1, 3):
        entry(step).start()

    own_entry = pltpu.make_async_copy(entry_ref.at[part], carry_out.at[0], own_sem.at[1])
    own_entry.start()
    pl.loop(CHUNKS // 2, CHUNKS)(interleave)
    for k in range(2):
        ships[k].wait_send()
    for k in range(2, 6):
        ships[k].wait()
    own = []
    for half, slots in ((0, (3, 4)), (1, (2, 5))):
        own.append(partial_ref[half_at(part, half), :] + pieces_ref[slots[0]] + pieces_ref[slots[1]])
    own = jnp.concatenate(own, axis=0)
    own_rows = own.shape[0]
    fraction = dot_exact(own, ones("weave"))
    within = dot_exact(own, ones("lane"))
    ends = jnp.broadcast_to(within[:, WIDE - 1 :], (own_rows, LANES))
    high, low = two(ends)
    rest = (ends - high.astype(F32) - low.astype(F32)).astype(BF16)
    earlier = ones("row")[:, :LANES]
    before = dot16(earlier, rest) + dot16(earlier, low) + dot16(earlier, high)
    for half in range(2):
        at = slice(half * LANES, (half + 1) * LANES)
        out = pl.ds(half, own_rows, stride=2)
        fraction_ref[out, :] = fraction[:, at]
        running_ref[out, :] = (within[:, at] + before) * scale
    own_stores = [
        pltpu.make_async_copy(fraction_ref, fraction_out, own_sem.at[0]),
        pltpu.make_async_copy(running_ref, running_out, own_sem.at[2]),
    ]
    for store in own_stores:
        store.start()

    @pl.loop(0, CHUNKS)
    def _(k):
        hand_over(k).wait()

    for store in own_stores:
        store.wait()
    own_entry.wait()

    for step in range(1, parts):
        entry(step).wait()

    all_peers(gathered_ref, send_sem).wait()
    for step in range(groups - 1):

        @pl.when(row_peer(me, step) > me)
        def _(step=step):
            note(step).wait_send()


def output_kernel(
    scale, extended_in, fraction_in, running_in, carry_ref, extended_hbm, fraction_hbm, running_ref, store_sem
):
    size = extended_in.shape[1] // CHUNKS

    def store(k):
        at = pl.ds(k * size, size)
        return pltpu.make_async_copy(extended_in.at[:, at], extended_hbm.at[:, at], store_sem.at[k])

    for k in range(CHUNKS):
        store(k).start()
    store_fraction = pltpu.make_async_copy(fraction_in, fraction_hbm, store_sem.at[CHUNKS])
    store_fraction.start()
    running_ref[...] = running_in[...] + jnp.sum(carry_ref[...]) * scale
    for k in range(CHUNKS):
        store(k).wait()
    store_fraction.wait()


def local(groups, parts, trace_values, challenges, multiplicity, table_index):
    columns, rows = trace_values.shape
    total = groups * rows
    (high, low), places = matrices(total, groups)
    scale = 1.0 / (2 * total)
    leaves = rows // LEAF
    parents = leaves // RADIX
    vmem = pl.BlockSpec(memory_space=pltpu.VMEM)
    hbm = pl.BlockSpec(memory_space=pl.ANY)
    dma = pltpu.SemaphoreType.DMA
    size = leaves // parts
    tile = lambda *lead: pltpu.VMEM(lead + (columns, LANES), F32)
    sources = (challenges, trace_values, multiplicity, table_index, jnp.asarray(high), jnp.asarray(low))
    sources = [pltpu.with_memory_space_constraint(source, pltpu.HBM) for source in sources]
    extended, fraction, running, carry = pl.pallas_call(
        functools.partial(main_kernel, groups, parts, scale, places),
        out_shape=(
            pltpu.VMEM((columns, 2 * rows), F32),
            pltpu.VMEM((2 * size, LANES), F32),
            pltpu.VMEM((2 * size, LANES), F32),
            pltpu.VMEM((parts, columns, LANES), F32),
        ),
        in_specs=[hbm] * 6,
        out_specs=(hbm, hbm, hbm, hbm),
        scratch_shapes=[
            pltpu.SMEM((columns,), F32),
            pltpu.VMEM((columns, rows + 2 * LEAF), F32),
            pltpu.VMEM((columns, 2 * rows), jnp.int32),
            pltpu.VMEM((columns, 2 * rows), jnp.int32),
            pltpu.VMEM(high.shape, BF16),
            pltpu.VMEM(low.shape, BF16),
            pltpu.VMEM((columns, rows), F32),
            pltpu.VMEM((columns, 2 * rows), F32),
            pltpu.VMEM((5 * LEAF, WIDE), BF16),
            pltpu.VMEM((columns * parents, WIDE), F32),
            pltpu.VMEM((columns * parents, WIDE), F32),
            pltpu.VMEM((2 * size, LANES), F32),
            pltpu.VMEM((2 * size, LANES), F32),
            pltpu.VMEM((leaves, WIDE), F32),
            pltpu.VMEM((leaves, WIDE), F32),
            tile(groups),
            pltpu.VMEM((2, columns, LEAF + 2 * WIDE), F32),
            pltpu.VMEM((2, columns, LEAF + 2 * WIDE), F32),
            pltpu.VMEM((6, size // 2, WIDE), F32),
            tile(2 * parts),
            tile(groups),
            tile(parts),
            dma((parts,)), dma((5,)), dma((2, parts)), dma((CHUNKS,)), dma((3,)),
            dma, dma, dma((2,)), dma((2,)),
            dma((6,)), dma((6,)), dma((groups,)), dma((groups,)), dma((parts,)), dma((parts,)),
        ],
        compiler_params=pltpu.CompilerParams(
            collective_id=0, has_side_effects=True, vmem_limit_bytes=48 * 2**20
        ),
        name="main",
    )(*sources)
    flat = jax.ShapeDtypeStruct((2 * size, LANES), F32)
    extended, fraction, running = pl.pallas_call(
        functools.partial(output_kernel, scale),
        out_shape=(jax.ShapeDtypeStruct((columns, 2 * rows), F32), flat, flat),
        in_specs=[hbm, hbm, vmem, vmem],
        out_specs=(hbm, hbm, vmem),
        scratch_shapes=[dma((CHUNKS + 1,))],
        compiler_params=pltpu.CompilerParams(vmem_limit_bytes=16 * 2**20),
        name="finish",
    )(extended, fraction, running, carry)
    return extended, fraction.reshape(-1), running.reshape(-1)


def solution(mesh):
    return jax.shard_map(
        functools.partial(local, mesh.shape["rows"], mesh.shape["cols"]),
        mesh=mesh,
        in_specs=(P("cols", "rows"), P("cols"), P("cols", "rows"), P("cols", "rows")),
        out_specs=(P("cols", "rows"), P(("rows", "cols")), P(("rows", "cols"))),
        check_vma=False,
    )
```
